32 devices in a mesh: dp: 4 (over y, core), ctx: 2 (over x), fsdp: 4 (over z).
Axes of the slice: x: 2, y: 2, z: 4, core: 2. Of those that a mesh axis runs over, the one named last changes fastest.
Arguments:
- tokens: bfloat16 [16, 1024, 1152], P(('dp', 'fsdp'), 'ctx'), may hold values from -6 to 6
- segments: int32 [16, 1024], P(('dp', 'fsdp'), 'ctx'), may hold values from 0 to 1023, as said below
- cotangent: bfloat16 [16, 1024, 1152], P(('dp', 'fsdp'), 'ctx'), may hold values from -6 to 6
- attn_gain: float32 [1152], P('fsdp'), may hold values from 0.1 to 1.9
- w_query: float32 [1152, 1152], P('fsdp'), may hold values from -0.1875 to 0.1875
- key_matrix: float32 [1152, 384], P('fsdp'), may hold values from -0.1875 to 0.1875
- value_matrix: float32 [1152, 384], P('fsdp'), may hold values from -0.1875 to 0.1875
- w_out: float32 [1152, 1152], P('fsdp'), may hold values from -0.75 to 0.75
- ffn_gain: float32 [1152], P('fsdp'), may hold values from 0.1 to 1.9
- w_gate: float32 [1152, 3072], P('fsdp'), may hold values from -0.1875 to 0.1875
- w_up: float32 [1152, 3072], P('fsdp'), may hold values from -0.1875 to 0.1875
- w_down: float32 [3072, 1152], P('fsdp'), may hold values from -0.109375 to 0.109375
Outputs:
- output: bfloat16 [16, 1024, 1152], P(('dp', 'fsdp'), 'ctx')
- grad_tokens: bfloat16 [16, 1024, 1152], P(('dp', 'fsdp'), 'ctx')
- grad_attn_gain: float32 [1152], P('fsdp')
- grad_w_query: float32 [1152, 1152], P('fsdp')
- grad_w_key: float32 [1152, 384], P('fsdp')
- grad_w_value: float32 [1152, 384], P('fsdp')
- grad_w_out: float32 [1152, 1152], P('fsdp')
- grad_ffn_gain: float32 [1152], P('fsdp')
- grad_w_gate: float32 [1152, 3072], P('fsdp')
- grad_w_up: float32 [1152, 3072], P('fsdp')
- grad_w_down: float32 [3072, 1152], P('fsdp')
The draws below stay inside these ranges and needn't reach their ends.
Inputs may be any that keep to these rules, and one draw needn't show every extreme that they name: `segments`: in each sequence the document numbers start at 0 at the first token and rise by 0 or 1 from one token to the next; in one sequence, chosen by the seed, all tokens belong to document 0; in another, also chosen by the seed, every token is a document of its own.
All inputs are finite; a program needn't handle non-finite values.
Results may differ from the reference program's by a relative error of at most 0.02.
Values may be sent and summed in bfloat16 or wider, within the bound.
No kernel may reach another device: no remote copies, remote signals or barrier semaphores. Data moves between devices by JAX's collectives and lax.ppermute only.
A program may use at most 256 MiB of HBM per device.

```python
import math
import jax
import jax.numpy as jnp
from jax import lax

MODEL_WIDTH = 1152
QUERY_HEADS = 18
KEY_VALUE_HEADS = 6
HEAD_WIDTH = 64
FF = 3072
LENGTH = 1024
SEQS = 16


def draw_segments(key, part):
    key = jax.random.fold_in(key, 7)
    level_key, break_key, pick_key, other_key = jax.random.split(key, 4)
    levels = jax.random.randint(level_key, (SEQS, 1), 0, 4)
    rates = 8 * 4 ** levels
    draws = jax.random.randint(break_key, (SEQS, LENGTH), 0, 1 << 20)
    chosen = jax.random.randint(pick_key, (), 0, SEQS)
    single = (chosen + 1 + jax.random.randint(other_key, (), 0, SEQS - 1)) % SEQS
    sequence = jnp.arange(SEQS, dtype=jnp.int32)[:, None]
    column = jnp.arange(LENGTH, dtype=jnp.int32)[None, :]
    breaks = ((draws % rates == 0) | (sequence == single)) & (column > 0) & (sequence != chosen)
    return jnp.cumsum(breaks.astype(jnp.int32), axis=1).astype(jnp.int32)


def shard_levels(stream_key, extent, cuts, least, high):
    def one(axis_at, blocks):
        steps = jax.random.uniform(jax.random.fold_in(jax.random.fold_in(stream_key, 6), axis_at), (blocks,), jnp.float32, least / len(cuts), high / len(cuts))
        return jnp.repeat(jnp.exp(steps), extent[axis_at] // blocks).reshape((-1,) + (1,) * (len(extent) - axis_at - 1))

    gain = one(*cuts[0])
    for cut in cuts[1:]:
        gain = gain * one(*cut)
    return gain


def normal_values(key, dims, scale, limit, pieces=(), kind=jnp.bfloat16):
    entries = jax.random.normal(key, dims, jnp.float32) * scale
    if len(pieces) > 0:
        entries = shard_levels(key, dims, pieces, -0.22, 0.18) * entries
    return jnp.clip(entries, min=-limit, max=limit).astype(kind)


def setup_inputs(seed: int = 0) -> dict:
    key_of = jax.random.split(jax.random.key(seed), 13)
    tokens = normal_values(key_of[0], (SEQS, LENGTH, MODEL_WIDTH), 1.0, 6.0, ((0, 16), (1, 2)))
    segments = draw_segments(jax.random.fold_in(key_of[12], 71), 0)
    cotangent = normal_values(key_of[2], (SEQS, LENGTH, MODEL_WIDTH), 1.0, 6.0, ((0, 16), (1, 2)))
    attn_gain = jnp.clip(1.0 + 0.18 * jax.random.normal(key_of[3], (MODEL_WIDTH,), jnp.float32), 0.1, 1.9)
    w_query = normal_values(key_of[4], (MODEL_WIDTH, QUERY_HEADS * HEAD_WIDTH), MODEL_WIDTH ** -0.5, 0.1875, ((0, 4),), jnp.float32)
    key_matrix = normal_values(key_of[5], (MODEL_WIDTH, KEY_VALUE_HEADS * HEAD_WIDTH), MODEL_WIDTH ** -0.5, 0.1875, ((0, 4),), jnp.float32)
    value_matrix = normal_values(key_of[6], (MODEL_WIDTH, KEY_VALUE_HEADS * HEAD_WIDTH), MODEL_WIDTH ** -0.5, 0.1875, ((0, 4),), jnp.float32)
    w_out = normal_values(key_of[7], (QUERY_HEADS * HEAD_WIDTH, MODEL_WIDTH), (QUERY_HEADS * HEAD_WIDTH // 16) ** -0.5, 0.75, ((0, 4),), jnp.float32)
    ffn_gain = jnp.clip(1.0 + 0.18 * jax.random.normal(key_of[8], (MODEL_WIDTH,), jnp.float32), 0.1, 1.9)
    w_gate = normal_values(key_of[9], (MODEL_WIDTH, FF), MODEL_WIDTH ** -0.5, 0.1875, ((0, 4),), jnp.float32)
    w_up = normal_values(key_of[10], (MODEL_WIDTH, FF), MODEL_WIDTH ** -0.5, 0.1875, ((0, 4),), jnp.float32)
    w_down = normal_values(key_of[11], (FF, MODEL_WIDTH), FF ** -0.5, 0.109375, ((0, 4),), jnp.float32)
    return {"tokens": tokens, "segments": segments, "cotangent": cotangent, "attn_gain": attn_gain, "w_query": w_query, "key_matrix": key_matrix, "value_matrix": value_matrix, "w_out": w_out, "ffn_gain": ffn_gain, "w_gate": w_gate, "w_up": w_up, "w_down": w_down}


@jax.custom_vjp
def low(v):
    return lax.optimization_barrier(v.astype(jnp.bfloat16)).astype(jnp.float32)

@jax.custom_vjp
def low_back(v):
    return v

def low_keep(v):
    return (low(v), None)

def low_pass(kept, grad):
    return (grad,)

def back_keep(v):
    return (v, None)

def back_low(kept, grad):
    return (low(grad),)
low.defvjp(low_keep, low_pass)
low_back.defvjp(back_keep, back_low)
negative_large = -1e+30
eps_norm = 1e-05
highest = lax.Precision.HIGHEST

def matmul(left, right):
    return jnp.dot(left, right, precision=highest, preferred_element_type=jnp.float32)

def inverse_freq():
    return 10000.0 ** (-(jnp.arange(HEAD_WIDTH // 2, dtype=jnp.float32) * 2.0) / HEAD_WIDTH)

def rotate(field, angles):
    block_length = field.shape[0]
    heads = field.reshape(block_length, -1, HEAD_WIDTH)
    cosine = jnp.cos(angles)[:, None, :]
    sine = jnp.sin(angles)[:, None, :]
    former = heads[..., :HEAD_WIDTH // 2]
    latter = heads[..., HEAD_WIDTH // 2:]
    turned = jnp.concatenate([former * cosine - latter * sine, latter * cosine + former * sine], axis=-1)
    return turned.reshape(block_length, -1)

def positions_of(ids):
    index = jnp.arange(ids.shape[0], dtype=jnp.int32)
    change = jnp.concatenate([jnp.ones((1,), dtype=bool), ids[1:] != ids[:-1]])
    starts = lax.cummax(jnp.where(change, index, 0), axis=0)
    return index - starts

def norm_scale(value):
    return lax.rsqrt(lax.optimization_barrier(jnp.mean(value * value, axis=-1, keepdims=True)) + eps_norm)

def layer(inputs, attn_gain, w_query, key_matrix, value_matrix, w_out, ffn_gain, w_gate, w_up, w_down, ids, angles):
    block_length = inputs.shape[0]
    group_width = QUERY_HEADS // KEY_VALUE_HEADS
    scale = HEAD_WIDTH ** (-0.5)
    normed = low(inputs * norm_scale(inputs) * low(attn_gain))
    query_rows = low(rotate(low_back(matmul(normed, low(w_query))), angles))
    key_rows = low(rotate(low_back(matmul(normed, low(key_matrix))), angles))
    value_rows = low(low_back(matmul(normed, low(value_matrix))))
    key_heads = key_rows.reshape(block_length, KEY_VALUE_HEADS, HEAD_WIDTH)
    value_heads = value_rows.reshape(block_length, KEY_VALUE_HEADS, HEAD_WIDTH)
    block_index = math.gcd(block_length, 512)
    index = jnp.arange(block_length, dtype=jnp.int32)

    def attend(items):
        query_block_rows, first = items
        row_total = first + jnp.arange(block_index, dtype=jnp.int32)
        row_ids = lax.dynamic_slice_in_dim(ids, first, block_index)
        grouped_queries = query_block_rows.reshape(block_index, KEY_VALUE_HEADS, group_width, HEAD_WIDTH)
        raw = low_back(jnp.einsum('tgrd,ngd->grtn', grouped_queries, key_heads, precision=highest))
        allowed = (index[None, :] <= row_total[:, None]) & (ids[None, :] == row_ids[:, None])
        scores = jnp.where(allowed, raw * scale, negative_large)
        peak = lax.optimization_barrier(jnp.max(scores, axis=-1, keepdims=True))
        log_total = peak + jnp.log(lax.optimization_barrier(jnp.sum(jnp.exp(scores - peak), axis=-1, keepdims=True)))
        weights = jnp.where(allowed, jnp.exp(scores - log_total), 0.0)
        mixed = jnp.einsum('grtn,ngd->tgrd', low(weights), value_heads, precision=highest)
        return mixed.reshape(block_index, QUERY_HEADS * HEAD_WIDTH)
    blocks = query_rows.reshape(block_length // block_index, block_index, QUERY_HEADS * HEAD_WIDTH)
    firsts = jnp.arange(block_length // block_index, dtype=jnp.int32) * block_index
    attention_output = lax.map(jax.checkpoint(attend), (blocks, firsts)).reshape(block_length, QUERY_HEADS * HEAD_WIDTH)
    attended_low = low(low_back(attention_output))
    middle = inputs + low_back(matmul(attended_low, low(w_out)))
    normed_two = low(middle * norm_scale(middle) * low(ffn_gain))
    gate = low_back(matmul(normed_two, low(w_gate)))
    upward = low_back(matmul(normed_two, low(w_up)))
    hidden = low(jax.nn.silu(gate) * upward)
    return middle + matmul(hidden, low(w_down))

def reference(tokens, segments, cotangent, attn_gain, w_query, key_matrix, value_matrix, w_out, ffn_gain, w_gate, w_up, w_down):
    params = (attn_gain, w_query, key_matrix, value_matrix, w_out, ffn_gain, w_gate, w_up, w_down)

    def one(carry, items):
        inputs, ids, incoming = items
        angles = positions_of(ids).astype(jnp.float32)[:, None] * inverse_freq()[None, :]

        def wrapped(inputs, attn_gain, w_query, key_matrix, value_matrix, w_out, ffn_gain, w_gate, w_up, w_down):
            return layer(inputs, attn_gain, w_query, key_matrix, value_matrix, w_out, ffn_gain, w_gate, w_up, w_down, ids, angles)
        result, pullback = jax.vjp(wrapped, inputs.astype(jnp.float32), attn_gain, w_query, key_matrix, value_matrix, w_out, ffn_gain, w_gate, w_up, w_down)
        grads = pullback(incoming.astype(jnp.float32))
        summed = tuple((held + fresh for held, fresh in zip(carry, grads[1:])))
        return (summed, (result.astype(jnp.bfloat16), grads[0].astype(jnp.bfloat16)))
    zero_filled = tuple((jnp.zeros(member.shape, jnp.float32) for member in params))
    totals, stacked = lax.scan(one, zero_filled, (tokens, segments, cotangent))
    return (stacked[0], stacked[1], totals[0], totals[1], totals[2], totals[3], totals[4], totals[5], totals[6], totals[7], totals[8])
```

```python
import math

import jax
import jax.numpy as jnp
from jax import lax
from jax.experimental import pallas as pl
from jax.experimental.pallas import tpu as pltpu
from jax.sharding import Mesh
from jax.sharding import PartitionSpec as P

QUERY_HEADS = 18
KEY_VALUE_HEADS = 6
HEAD_WIDTH = 64
TURN = HEAD_WIDTH // 2
GROUP = QUERY_HEADS // KEY_VALUE_HEADS
GROUPS = KEY_VALUE_HEADS // 2
HALF_QUERY = QUERY_HEADS // 2 * HEAD_WIDTH
HALF_KEY = GROUPS * HEAD_WIDTH
CHUNKS = 3
BLOCKS = 4

low_type = jnp.bfloat16
eps_norm = 1e-05
masked_score = -1e30
lowest_peak = -1e20
LOG2E = math.log2(math.e)
SCORE_SCALE = HEAD_WIDTH ** (-0.5)
VMEM_LIMIT = 58 * 1024 * 1024

PAIR = [(0, 1), (1, 0)]
ANY = pl.BlockSpec(memory_space=pl.ANY)
SCALARS = pl.BlockSpec(memory_space=pltpu.SMEM)


def inverse_freq():
    return 10000.0 ** (-(jnp.arange(TURN, dtype=jnp.float32) * 2.0) / HEAD_WIDTH)


def norm_scale(value):
    return lax.rsqrt(jnp.mean(value * value, axis=-1, keepdims=True) + eps_norm)


def norm_back(scaled, value, scale):
    return scale * scaled - value * scale**3 * jnp.mean(scaled * value, axis=-1, keepdims=True)


def dot(left, right, over=(1, 0)):
    return lax.dot_general(
        left, right, (((over[0],), (over[1],)), ((), ())), preferred_element_type=jnp.float32
    )


def swap_core(value):
    return lax.ppermute(value, "core", PAIR)


def params():
    return pltpu.CompilerParams(vmem_limit_bytes=VMEM_LIMIT)


def cost(flops, moved, special=0):
    return pl.CostEstimate(flops=int(flops), bytes_accessed=int(moved), transcendentals=int(special))


def shape(dims, kind=low_type):
    return jax.ShapeDtypeStruct(tuple(dims), kind)


def pack_attn_kernel(info, q_ref, k_ref, v_ref, o_ref, own_ref, *piece_ref):
    def half(ref):
        size = ref.shape[1] // 2
        value = ref[...].astype(low_type)
        return jnp.where(info[0] == 0, value[:, :size], value[:, size:])

    own_ref[...] = jnp.concatenate([half(r) for r in (q_ref, k_ref, v_ref, o_ref)], axis=1)
    for ref in piece_ref:
        part = ref.shape[1]
        ref[...] = own_ref[:, pl.ds(pl.multiple_of(info[1] * part, part), part)]


def pack_attn(info, arrays, tuned):
    rows = arrays[0].shape[0]
    width = sum(a.shape[1] for a in arrays) // 2
    outs = [shape((rows, width))] + [shape((rows, width // BLOCKS))] * tuned
    return pl.pallas_call(
        pack_attn_kernel,
        in_specs=[SCALARS] + [pl.BlockSpec()] * 4,
        out_specs=[pl.BlockSpec()] * len(outs),
        out_shape=outs,
        compiler_params=params(),
        cost_estimate=cost(0, rows * width * 10),
    )(info, *arrays)


def pack_ffn_kernel(info, gate_ref, up_ref, down_ref, own_ref, *piece_ref):
    step, steps = pl.program_id(0), pl.num_programs(0)
    part = gate_ref.shape[1] // CHUNKS
    rows = gate_ref.shape[0]
    blocks = own_ref.shape[2] // part // 3
    for c in range(CHUNKS):
        at = slice(c * part, (c + 1) * part)
        here = pl.ds(pl.multiple_of(step * part, part), part)
        own_ref[c, :, here] = gate_ref[:, at].astype(low_type)
        there = pl.ds(pl.multiple_of((blocks + step) * part, part), part)
        own_ref[c, :, there] = up_ref[:, at].astype(low_type)

    @pl.when(step == 0)
    def _():
        turned = down_ref[...].astype(low_type).T
        for c in range(CHUNKS):
            for q in range(blocks):
                own_ref[c, :, (2 * blocks + q) * part : (2 * blocks + q + 1) * part] = turned[
                    q * rows : (q + 1) * rows, c * part : (c + 1) * part
                ]

    @pl.when(step == steps - 1)
    def _():
        for c, ref in enumerate(piece_ref):
            size = ref.shape[1]
            ref[...] = own_ref[c, :, pl.ds(pl.multiple_of(info[1] * size, size), size)]


def pack_ffn(info, gate, up, down, tuned):
    rows, hidden = gate.shape
    hidden_rows, width = down.shape
    steps = hidden // hidden_rows
    half = hidden_rows // 2
    packed = 3 * steps * (half // CHUNKS)
    outs = [shape((CHUNKS, rows, packed))] + [shape((rows, packed // BLOCKS))] * (CHUNKS * tuned)
    columns = pl.BlockSpec((rows, half), lambda z, info: (0, 2 * z + info[0]))
    return pl.pallas_call(
        pack_ffn_kernel,
        grid_spec=pltpu.PrefetchScalarGridSpec(
            num_scalar_prefetch=1,
            grid=(steps,),
            in_specs=[columns, columns, pl.BlockSpec((half, width), lambda z, info: (info[0], 0))],
            out_specs=[pl.BlockSpec((CHUNKS, rows, packed), lambda z, info: (0, 0, 0))]
            + [pl.BlockSpec((rows, packed // BLOCKS), lambda z, info: (0, 0))] * (CHUNKS * tuned),
        ),
        out_shape=outs,
        compiler_params=params(),
        cost_estimate=cost(0, rows * packed * CHUNKS * 6),
    )(info, gate, up, down)


def ring(count, step):
    return [(i, (i + step) % count) for i in range(count)]


def assemble_kernel(count, info, own_ref, *refs):
    pieces, out_ref, sems = refs[:-2], refs[-2], refs[-1]
    rows = own_ref.shape[0]
    part = out_ref.shape[2]
    copies = []

    def begin(source, block, row):
        target = out_ref.at[block, pl.ds(pl.multiple_of(row * rows, rows), rows), :]
        copies.append(pltpu.make_async_copy(source, target, sems.at[len(copies)]))
        copies[-1].start()

    for b in range(BLOCKS):
        begin(own_ref.at[:, b * part : (b + 1) * part], b, info[2])
    for flip in range(BLOCKS):
        for k in range(1, count):
            begin(
                pieces[flip * (count - 1) + k - 1],
                jnp.bitwise_xor(info[1], flip),
                lax.rem(info[2] + count - k, count),
            )
    for copy in copies:
        copy.wait()


def assemble(info, own, pieces, count):
    rows, width = own.shape
    out = shape((BLOCKS, rows * count, width // BLOCKS))

    def kernel(*refs):
        assemble_kernel(count, *refs)

    return pl.pallas_call(
        kernel,
        in_specs=[SCALARS] + [ANY] * (1 + len(pieces)),
        out_specs=pl.BlockSpec(),
        out_shape=out,
        scratch_shapes=[pltpu.SemaphoreType.DMA((BLOCKS * count,))],
        compiler_params=params(),
        cost_estimate=cost(0, rows * width * count * 4),
    )(info, own, *pieces)


def gather_weights(info, own, piece, sizes, turn):
    nz = sizes[2]
    if piece is None:
        full = lax.all_gather(own, "z", axis=0, tiled=True)
        return full.reshape(full.shape[0], BLOCKS, -1).transpose(1, 0, 2)
    slots = [lax.ppermute(piece, "z", ring(nz, k)) for k in range(1, nz)]
    by_x = [lax.ppermute(s, "x", PAIR) for s in slots]
    by_y = [lax.ppermute(s, "y", PAIR) for s in slots]
    far = [
        lax.ppermute(by_x[k], "y", PAIR) if (k + turn) % 2 else lax.ppermute(by_y[k], "x", PAIR)
        for k in range(nz - 1)
    ]
    return assemble(info, own, slots + by_x + by_y + far, nz)


def send_out(info, packed, outs, sems):
    copies = []

    def begin(source, target):
        copies.append(pltpu.make_async_copy(source, target, sems.at[len(copies)]))
        copies[-1].start()

    if len(outs) == 1:
        begin(packed, outs[0])
    else:
        keep_one, send_one, keep_two, send_two = outs
        cut = packed.shape[1] // 2
        y, x = lax.div(info[1], 2), lax.rem(info[1], 2)
        for i in range(2):
            at_y, at_x = jnp.bitwise_xor(y, i), jnp.bitwise_xor(x, i)
            begin(packed.at[at_y * 2 + x, :cut], keep_one.at[i])
            begin(packed.at[at_y * 2 + 1 - x, :cut], send_one.at[i])
            begin(packed.at[y * 2 + at_x, cut:], keep_two.at[i])
            begin(packed.at[(1 - y) * 2 + at_x, cut:], send_two.at[i])
    for copy in copies:
        copy.wait()


def sent_shapes(rows, part, tuned):
    if tuned:
        return [shape((2, rows // 2, part))] * 4
    return [shape((BLOCKS, rows, part))]


def sum_over(value, axis, count):
    if count & (count - 1):
        return lax.psum(value, axis)
    step = 1
    while step < count:
        value = value + lax.ppermute(value, axis, [(i, i ^ step) for i in range(count)])
        step *= 2
    return value


def add_low(kept, came):
    return (kept.astype(jnp.float32) + came.astype(jnp.float32)).astype(low_type)


def scatter_gradients(outs, sizes):
    ny, nx, nz = sizes
    if len(outs) == 1:
        packed = outs[0]
        total = packed.shape[1]
        split = packed.transpose(1, 0, 2).reshape(total, ny * nx, -1).transpose(1, 0, 2)
        mine = lax.psum_scatter(split, ("y", "x"), scatter_dimension=0, tiled=True)[0]
    else:
        keep_one, send_one, keep_two, send_two = outs
        came_one = lax.ppermute(send_one, "x", PAIR)
        came_two = lax.ppermute(send_two, "y", PAIR)
        one = lax.ppermute(add_low(keep_one[1], came_one[1]), "y", PAIR)
        two = lax.ppermute(add_low(keep_two[1], came_two[1]), "x", PAIR)
        one = add_low(add_low(keep_one[0], came_one[0]), one)
        two = add_low(add_low(keep_two[0], came_two[0]), two)
        mine = jnp.concatenate([one, two])
    return lax.psum_scatter(mine, "z", scatter_dimension=0, tiled=True)


def spread(mine, sizes):
    everyone = lax.all_gather(mine, ("core", "y", "x"), axis=0)
    both = everyone.reshape((2, sizes[0] * sizes[1]) + mine.shape)
    if sizes[0] * sizes[1] == BLOCKS:
        return both
    both = jnp.moveaxis(both, 1, -2).reshape((2,) + mine.shape[:2] + (BLOCKS, -1))
    return jnp.moveaxis(both, -2, 1)


def turn_heads(ref, value, cosine, sine, start):
    for h in range(value.shape[0] // HEAD_WIDTH):
        former = value[h * HEAD_WIDTH : h * HEAD_WIDTH + TURN]
        latter = value[h * HEAD_WIDTH + TURN : (h + 1) * HEAD_WIDTH]
        at = start + h * HEAD_WIDTH
        ref[at : at + TURN, :] = (former * cosine - latter * sine).astype(ref.dtype)
        ref[at + TURN : at + HEAD_WIDTH, :] = (latter * cosine + former * sine).astype(ref.dtype)


def project_kernel(mine_ref, other_ref, gain_ref, w_ref, cos_ref, sin_ref, normed_ref, q_ref, kv_ref):
    rows = mine_ref.shape[0]
    hk, part = HALF_KEY, w_ref.shape[2]
    for i, ref in enumerate((mine_ref, other_ref)):
        value = ref[...].astype(jnp.float32)
        normed = (value * norm_scale(value) * gain_ref[...]).astype(low_type)
        at = slice(i * rows, (i + 1) * rows)
        normed_ref[:, at] = normed.T
    weights = [w_ref[0].T, w_ref[1].T, w_ref[2].T[:hk]]
    for i in range(2):
        at = slice(i * rows, (i + 1) * rows)
        normed = normed_ref[:, at]
        cosine, sine = cos_ref[:, at], sin_ref[:, at]
        first = dot(weights[0], normed)
        turn_heads(q_ref.at[:, at], first, cosine, sine, 0)
        second = dot(weights[1], normed)
        turn_heads(q_ref.at[:, at], second[: part - hk], cosine, sine, part)
        turn_heads(kv_ref.at[0, :, at], second[part - hk :], cosine, sine, 0)
        kv_ref[1, :, at] = dot(weights[2], normed).astype(low_type)


def project(mine, other, gain, weights, cosine, sine):
    rows, width = mine.shape
    return pl.pallas_call(
        project_kernel,
        in_specs=[pl.BlockSpec()] * 6,
        out_specs=[pl.BlockSpec()] * 3,
        out_shape=[
            shape((width, 2 * rows)), shape((HALF_QUERY, 2 * rows)), shape((2, HALF_KEY, 2 * rows))
        ],
        compiler_params=params(),
        cost_estimate=cost(4 * rows * width * 960, 14 << 20),
    )(mine, other, gain, weights, cosine, sine)


def tile_mask(first, place0, key0, size, causal):
    key_place = key0 + lax.broadcasted_iota(jnp.int32, (size, size), 0)
    allowed = key_place >= first
    if causal:
        place = place0 + lax.broadcasted_iota(jnp.int32, (size, size), 1)
        allowed = allowed & (key_place <= place)
    return jnp.concatenate([allowed] * GROUP, axis=1)


def heads_of(ref):
    return jnp.concatenate(
        [ref[r * HEAD_WIDTH : (r + 1) * HEAD_WIDTH, :] for r in range(GROUP)], axis=1
    )


def over_tiles(info, size, rows, turn):
    per = rows // size
    half = pl.program_id(2)
    own = info[3] * per
    hi = own + half
    lo = info[4 + pl.program_id(0) * per + half]

    def columns(b):
        return pl.ds(pl.multiple_of(lax.rem(b, per) * size, size), size)

    def earlier(b, _):
        turn(hi, b, lax.div(b, per), columns(b))
        return 0

    def here(b, _):
        turn(hi, b, None, columns(b))
        return 0

    lax.fori_loop(lo, own, earlier, 0)
    lax.fori_loop(jnp.maximum(lo, own), hi + 1, here, 0)


def attend_kernel(info, q_ref, kv_ref, past_ref, first_ref, o_ref, total_ref, peak_s, sum_s, acc_s):
    size, rows = q_ref.shape[1], kv_ref.shape[2]
    q = heads_of(q_ref)
    peak_s[...] = jnp.full(peak_s.shape, lowest_peak, jnp.float32)
    sum_s[...] = jnp.zeros(sum_s.shape, jnp.float32)
    acc_s[...] = jnp.zeros(acc_s.shape, jnp.float32)

    def turn(hi, b, past, at):
        k = kv_ref[0, :, at] if past is None else past_ref[past, 0, :, at]
        v = kv_ref[1, :, at] if past is None else past_ref[past, 1, :, at]
        allowed = tile_mask(first_ref[0], hi * size, b * size, size, past is None)
        scores = dot(k, q, (0, 0)) * (SCORE_SCALE * LOG2E)
        scores = jnp.where(allowed, scores, masked_score)
        peak = peak_s[...]
        fresh = jnp.maximum(peak, jnp.max(scores, axis=0, keepdims=True))
        shrink = jnp.exp2(peak - fresh)
        terms = jnp.exp2(scores - fresh)
        peak_s[...] = fresh
        sum_s[...] = sum_s[...] * shrink + jnp.sum(terms, axis=0, keepdims=True)
        acc_s[...] = acc_s[...] * shrink + dot(v, terms.astype(low_type))

    over_tiles(info, size, rows, turn)
    total = sum_s[...]
    mixed = acc_s[...] / total
    log_total = peak_s[...] + jnp.log2(total)
    for r in range(GROUP):
        o_ref[r * HEAD_WIDTH : (r + 1) * HEAD_WIDTH, :] = mixed[:, r * size : (r + 1) * size]
        total_ref[0, r : r + 1, :] = log_total[:, r * size : (r + 1) * size]


def attend_back_kernel(
    info, q_ref, kv_ref, past_ref, g_ref, first_ref, total_ref, delta_ref, dq_ref, dkv_ref, dpast_ref,
    acc_s, past_s,
):
    size, rows = q_ref.shape[1], kv_ref.shape[2]
    q = heads_of(q_ref)
    g = heads_of(g_ref)
    total = jnp.concatenate([total_ref[0, r : r + 1, :] for r in range(GROUP)], axis=1)
    delta = jnp.concatenate([delta_ref[0, r : r + 1, :] for r in range(GROUP)], axis=1)
    acc_s[...] = jnp.zeros(acc_s.shape, jnp.float32)

    @pl.when(pl.program_id(2) == 0)
    def _():
        dkv_ref[...] = jnp.zeros(dkv_ref.shape, jnp.float32)
        past_s[...] = jnp.zeros(past_s.shape, jnp.float32)

    def turn(hi, b, past, at):
        k = kv_ref[0, :, at] if past is None else past_ref[past, 0, :, at]
        v = kv_ref[1, :, at] if past is None else past_ref[past, 1, :, at]
        allowed = tile_mask(first_ref[0], hi * size, b * size, size, past is None)
        scores = dot(k, q, (0, 0)) * (SCORE_SCALE * LOG2E)
        weights = jnp.exp2(jnp.where(allowed, scores - total, masked_score))
        grad_weights = dot(v, g, (0, 0))
        grad_scores = (weights * (grad_weights - delta) * SCORE_SCALE).astype(low_type)
        dk = dot(q, grad_scores, (1, 1))
        dv = dot(g, weights.astype(low_type), (1, 1))
        if past is None:
            dkv_ref[0, :, at] += dk
            dkv_ref[1, :, at] += dv
        else:
            past_s[past, 0, :, at] += dk
            past_s[past, 1, :, at] += dv
        acc_s[...] += dot(k, grad_scores)

    over_tiles(info, size, rows, turn)
    acc = acc_s[...]
    for r in range(GROUP):
        dq_ref[r * HEAD_WIDTH : (r + 1) * HEAD_WIDTH, :] = acc[:, r * size : (r + 1) * size]

    @pl.when(pl.program_id(2) == pl.num_programs(2) - 1)
    def _():
        dpast_ref[...] = past_s[...].astype(low_type)


def attention_specs(parts, rows, size):
    per = rows // size
    wide = pl.BlockSpec((GROUP * HEAD_WIDTH, size), lambda s, g, h: (g, s * per + h))
    own = pl.BlockSpec((2, HEAD_WIDTH, rows), lambda s, g, h: (0, g, s))
    past = pl.BlockSpec((parts, 2, HEAD_WIDTH, rows), lambda s, g, h: (0, 0, g, s))
    first = pl.BlockSpec((1, 1, size), lambda s, g, h: (s, 0, h))
    stat = pl.BlockSpec((1, 8, size), lambda s, g, h: (g, 0, s * per + h))
    return (2, GROUPS, per), wide, own, past, first, stat


def attend(info, query, keyvalue, past, first, size):
    both = keyvalue.shape[2]
    rows = both // 2
    grid, wide, own, past_spec, first_spec, stat = attention_specs(past.shape[0], rows, size)
    pairs = 2 * rows * rows * 3 // 2
    return pl.pallas_call(
        attend_kernel,
        grid=grid,
        in_specs=[SCALARS, wide, own, past_spec, first_spec],
        out_specs=[wide, stat],
        out_shape=[shape(query.shape, jnp.float32), shape((GROUPS, 8, both), jnp.float32)],
        scratch_shapes=[
            pltpu.VMEM((1, GROUP * size), jnp.float32),
            pltpu.VMEM((1, GROUP * size), jnp.float32),
            pltpu.VMEM((HEAD_WIDTH, GROUP * size), jnp.float32),
        ],
        compiler_params=params(),
        cost_estimate=cost(pairs * 9 * 64 * 4 * 5, 8 << 20, pairs * 9),
    )(info, query, keyvalue, past, first)


def attend_back(info, query, keyvalue, past, grad, first, log_total, delta, size):
    both = keyvalue.shape[2]
    rows = both // 2
    grid, wide, own, past_spec, first_spec, stat = attention_specs(past.shape[0], rows, size)
    pairs = 2 * rows * rows * 3 // 2
    return pl.pallas_call(
        attend_back_kernel,
        grid=grid,
        in_specs=[SCALARS, wide, own, past_spec, wide, first_spec, stat, stat],
        out_specs=[wide, own, past_spec],
        out_shape=[
            shape(query.shape, jnp.float32), shape(keyvalue.shape, jnp.float32), shape(past.shape)
        ],
        scratch_shapes=[
            pltpu.VMEM((HEAD_WIDTH, GROUP * size), jnp.float32),
            pltpu.VMEM((past.shape[0], 2, HEAD_WIDTH, rows), jnp.float32),
        ],
        compiler_params=params(),
        cost_estimate=cost(pairs * 9 * 64 * 10 * 3, 12 << 20, pairs * 9),
    )(info, query, keyvalue, past, grad, first, log_total, delta)


def place_out(core, mine_ref, other_ref, out_ref):
    cut, part = HALF_KEY, mine_ref.shape[2]
    mine = jnp.concatenate([mine_ref[0][:, cut:], mine_ref[1]], axis=1)
    other = jnp.concatenate([other_ref[0][:, cut:], other_ref[1]], axis=1)
    out_ref[...] = jnp.where(
        core == 0,
        jnp.concatenate([mine, other], axis=1),
        jnp.concatenate([other, mine], axis=1),
    )


def out_kernel(
    info, mine_ref, came_ref, w_ref, w_other_ref, tokens_ref, gain_ref, middle_ref, normed_ref,
    turned_ref, rows_ref, w_s,
):
    place_out(info[0], w_ref, w_other_ref, w_s)
    hq = HALF_QUERY
    mine = w_s[pl.ds(pl.multiple_of(info[0] * hq, hq), hq), :]
    other = w_s[pl.ds(pl.multiple_of((1 - info[0]) * hq, hq), hq), :]
    rows_ref[...] = mine
    middle = (
        tokens_ref[...].astype(jnp.float32)
        + dot(mine_ref[...].astype(low_type).T, mine)
        + dot(came_ref[...].T, other)
    )
    middle_ref[...] = middle
    normed = (middle * norm_scale(middle) * gain_ref[...]).astype(low_type)
    normed_ref[...] = normed
    turned_ref[...] = normed.T


def project_out(info, attended, came, weights, weights_other, tokens, gain):
    rows, width = tokens.shape
    hq = HALF_QUERY
    part = weights.shape[2]
    return pl.pallas_call(
        out_kernel,
        grid=(1,),
        in_specs=[
            SCALARS,
            pl.BlockSpec((hq, rows), lambda i: (0, 0)),
            pl.BlockSpec((hq, rows), lambda i: (0, 0)),
            pl.BlockSpec((2, width, part), lambda i: (1, 0, 0)),
            pl.BlockSpec((2, width, part), lambda i: (0, 0, 0)),
            pl.BlockSpec((rows, width), lambda i: (0, 0)),
            pl.BlockSpec((1, width), lambda i: (0, 0)),
        ],
        out_specs=[
            pl.BlockSpec((rows, width), lambda i: (0, 0)),
            pl.BlockSpec((rows, width), lambda i: (0, 0)),
            pl.BlockSpec((width, rows), lambda i: (0, 0)),
            pl.BlockSpec((hq, width), lambda i: (0, 0)),
        ],
        out_shape=[
            shape((rows, width), jnp.float32), shape((rows, width)), shape((width, rows)),
            shape((hq, width)),
        ],
        scratch_shapes=[pltpu.VMEM((width, width), low_type)],
        compiler_params=params(),
        cost_estimate=cost(2 * rows * width * width, 16 << 20),
    )(info, attended, came, weights, weights_other, tokens, gain)


def ffn_kernel(held, info, *refs):
    x_refs, c_refs, xt_refs, ct_refs, w_ref = refs[0:2], refs[2:4], refs[4:6], refs[6:8], refs[8]
    sums = refs[9 : 9 + 2 * held]
    refs = refs[9 + 2 * held :]
    result_ref, grad_ref, outs = refs[0], refs[1], refs[2:-9]
    gate_s, up_s, down_s, hidden_s, dgate_s, dup_s, packed_s, _, sems = refs[-9:]
    step = pl.program_id(0)
    size = result_ref.shape[0]
    half = 2
    block = gate_s.shape[1]
    part = w_ref.shape[2]
    width = gate_s.shape[0]
    lane = block // BLOCKS
    rows = width // BLOCKS

    @pl.when(step == 0)
    def _():
        gate_s[:, :part] = w_ref[0]
        gate_s[:, part:] = w_ref[1, :, : block - part]
        up_s[:, : 2 * part - block] = w_ref[1, :, block - part :]
        up_s[:, 2 * part - block :] = w_ref[2, :, : 2 * block - 2 * part]
        for q in range(BLOCKS):
            for z in range(BLOCKS):
                column = 2 * block + q * lane
                b, at = column // part, column % part
                down_s[q * rows : (q + 1) * rows, z * lane : (z + 1) * lane] = w_ref[
                    b, z * rows : (z + 1) * rows, at : at + lane
                ]

    @pl.when(step < 2 * half)
    def _():
        mine = step < half
        x = jnp.where(mine, x_refs[0][...], x_refs[1][...])
        c = jnp.where(mine, c_refs[0][...], c_refs[1][...])
        gate = dot(x, gate_s[...])
        upward = dot(x, up_s[...])
        grad_hidden = dot(c, down_s[...])
        sigmoid = 1.0 / (1.0 + jnp.exp(-gate))
        silu = gate * sigmoid
        hidden = (silu * upward).astype(low_type)
        grad_gate = (grad_hidden * upward * sigmoid * (1.0 + gate * (1.0 - sigmoid))).astype(low_type)
        grad_up = (grad_hidden * silu).astype(low_type)
        at = pl.ds(pl.multiple_of(step * size, size), size)
        hidden_s[at, :] = hidden
        dgate_s[at, :] = grad_gate
        dup_s[at, :] = grad_up
        result = dot(hidden, down_s[...], (1, 1))
        grad = dot(grad_gate, gate_s[...], (1, 1)) + dot(grad_up, up_s[...], (1, 1))
        if held:
            result = result + sums[0][...]
            grad = grad + sums[1][...]
        result_ref[...] = result
        grad_ref[...] = grad

    @pl.when(step >= 2 * half)
    def _():
        q = step - 2 * half
        cut = half * size
        at = pl.ds(pl.multiple_of(q * rows, rows), rows)
        gate = dot(xt_refs[0][...], dgate_s[:cut]) + dot(xt_refs[1][...], dgate_s[cut:])
        up = dot(xt_refs[0][...], dup_s[:cut]) + dot(xt_refs[1][...], dup_s[cut:])
        down = dot(ct_refs[0][...], hidden_s[:cut]) + dot(ct_refs[1][...], hidden_s[cut:])
        gate, up, down = gate.astype(low_type), up.astype(low_type), down.astype(low_type)
        packed_s[0, at, :] = gate[:, :part]
        packed_s[1, at, : block - part] = gate[:, part:]
        packed_s[1, at, block - part :] = up[:, : 2 * part - block]
        packed_s[2, at, : 2 * block - 2 * part] = up[:, 2 * part - block :]
        column = 2 * block + q * lane
        b = lax.div(column, part)
        there = pl.ds(pl.multiple_of(lax.rem(column, part), lane), lane)
        for z in range(BLOCKS):
            packed_s[b, z * rows : (z + 1) * rows, there] = down[:, z * lane : (z + 1) * lane]

    @pl.when(step == pl.num_programs(0) - 1)
    def _():
        send_out(info, packed_s, outs, sems)


def ffn_chunk(info, xs, cs, xts, cts, weights, sums, tuned):
    rows, width = xs[0].shape
    size = rows // 2
    part = weights.shape[2]
    block = BLOCKS * part // 3
    turned = width // BLOCKS

    def first(i):
        return (jnp.minimum(i, 1), 0)

    def second(i):
        return (jnp.clip(i - 2, 0, 1), 0)

    def either(i):
        return (jnp.minimum(i, 3), 0)

    def later(i):
        return (jnp.maximum(i - 4, 0), 0)

    token = [pl.BlockSpec((size, width), first), pl.BlockSpec((size, width), second)]
    across = [pl.BlockSpec((turned, rows), later)] * 2
    total = [pl.BlockSpec((size, width), either)] * 2
    held = len(sums) > 0
    sent = sent_shapes(width, part, tuned)

    def kernel(info, *refs):
        ffn_kernel(held, info, *refs)

    return pl.pallas_call(
        kernel,
        grid=(8,),
        in_specs=[SCALARS] + token + token + across + across
        + [pl.BlockSpec(weights.shape, lambda i: (0, 0, 0))] + (total if held else []),
        out_specs=total + [ANY] * len(sent),
        out_shape=[shape((2 * rows, width), jnp.float32)] * 2 + sent,
        scratch_shapes=[
            pltpu.VMEM((width, block), low_type),
            pltpu.VMEM((width, block), low_type),
            pltpu.VMEM((width, block), low_type),
            pltpu.VMEM((2 * rows, block), low_type),
            pltpu.VMEM((2 * rows, block), low_type),
            pltpu.VMEM((2 * rows, block), low_type),
            pltpu.VMEM((BLOCKS, width, part), low_type),
            pltpu.VMEM((8, 128), jnp.float32),
            pltpu.SemaphoreType.DMA((8,)),
        ],
        compiler_params=params(),
        cost_estimate=cost(18 * 2 * rows * width * block, 40 << 20, 2 * rows * block),
    )(info, *xs, *cs, *xts, *cts, weights, *sums)


def branch_kernel(g_ref, g_other_ref, w_ref, attended_ref, grad_ref, delta_ref, rows_ref):
    rows = g_ref.shape[0]
    delta_ref[...] = jnp.zeros(delta_ref.shape, jnp.float32)
    for i, ref in enumerate((g_ref, g_other_ref)):
        at = slice(i * rows, (i + 1) * rows)
        grad = dot(w_ref[...], ref[...], (1, 1)).astype(low_type)
        grad_ref[:, at] = grad
        product = grad.astype(jnp.float32) * attended_ref[:, at]
        for h in range(GROUP * GROUPS):
            delta_ref[h // GROUP, h % GROUP : h % GROUP + 1, at] = jnp.sum(
                product[h * HEAD_WIDTH : (h + 1) * HEAD_WIDTH], axis=0, keepdims=True
            )
    attended = attended_ref[...].astype(low_type)
    rows_ref[...] = (
        dot(attended[:, :rows], g_ref[...]) + dot(attended[:, rows:], g_other_ref[...])
    ).astype(low_type)


def branch(grad, grad_other, out_rows, attended):
    rows, width = grad.shape
    return pl.pallas_call(
        branch_kernel,
        in_specs=[pl.BlockSpec()] * 4,
        out_specs=[pl.BlockSpec()] * 3,
        out_shape=[
            shape(attended.shape), shape((GROUPS, 8, 2 * rows), jnp.float32),
            shape((HALF_QUERY, width)),
        ],
        compiler_params=params(),
        cost_estimate=cost(8 * rows * width * HALF_QUERY, 12 << 20),
    )(grad, grad_other, out_rows, attended)


def attn_grad_kernel(
    info, dq_ref, dkv_ref, came_ref, cos_ref, sin_ref, normed_ref, mine_ref, other_ref, d_ref, *refs
):
    outs, packed_s, sems = refs[:-2], refs[-2], refs[-1]
    hq, hk = HALF_QUERY, HALF_KEY
    part = packed_s.shape[2]
    cosine, sine = cos_ref[...], -sin_ref[...]
    turn_heads(d_ref, dq_ref[...], cosine, sine, 0)
    whole = dkv_ref[...] + came_ref[...].astype(jnp.float32)
    turn_heads(d_ref, whole[0], cosine, sine, hq)
    d_ref[hq + hk :, :] = whole[1].astype(low_type)
    normed = normed_ref[...]
    packed_s[0] = dot(normed, d_ref[:part, :], (1, 1)).astype(low_type)
    packed_s[1] = dot(normed, d_ref[part : 2 * part, :], (1, 1)).astype(low_type)
    last = dot(normed, d_ref[2 * part :, :], (1, 1)).astype(low_type)
    mine, other = mine_ref[...], other_ref[...]
    low = info[0] == 0
    out = jnp.concatenate(
        [jnp.where(low, mine, other), jnp.where(low, other, mine)], axis=0
    )
    packed_s[2] = jnp.concatenate([last, out[:, : part - hk]], axis=1)
    packed_s[3] = out[:, part - hk :]
    send_out(info, packed_s, outs, sems)


def attn_grads(info, grad_query, grad_kv, came, cosine, sine, normed, mine, other, tuned):
    width, both = normed.shape
    part = (2 * HALF_QUERY + 2 * HALF_KEY) // BLOCKS
    sent = sent_shapes(width, part, tuned)
    return pl.pallas_call(
        attn_grad_kernel,
        in_specs=[SCALARS] + [pl.BlockSpec()] * 8,
        out_specs=[pl.BlockSpec()] + [ANY] * len(sent),
        out_shape=[shape((HALF_QUERY + 2 * HALF_KEY, both))] + sent,
        scratch_shapes=[
            pltpu.VMEM((BLOCKS, width, part), low_type),
            pltpu.SemaphoreType.DMA((8,)),
        ],
        compiler_params=params(),
        cost_estimate=cost(2 * both * width * 960, 20 << 20),
    )(info, grad_query, grad_kv, came, cosine, sine, normed, mine, other)


def normed_grad_kernel(d_ref, w_ref, mine_ref, other_ref):
    rows = mine_ref.shape[0]
    hk, part = HALF_KEY, w_ref.shape[2]
    for i, ref in enumerate((other_ref, mine_ref)):
        at = slice((1 - i) * rows, (2 - i) * rows)
        d = d_ref[:, at].T
        value = dot(d[:, :part], w_ref[0], (1, 1)) + dot(d[:, part : 2 * part], w_ref[1], (1, 1))
        value = value + dot(d[:, 2 * part :], w_ref[2][:, :hk], (1, 1))
        ref[...] = value.astype(ref.dtype)


def normed_grad(d, weights):
    width = weights.shape[1]
    rows = d.shape[1] // 2
    return pl.pallas_call(
        normed_grad_kernel,
        in_specs=[pl.BlockSpec()] * 2,
        out_specs=[pl.BlockSpec()] * 2,
        out_shape=[shape((rows, width), jnp.float32), shape((rows, width))],
        compiler_params=params(),
        cost_estimate=cost(4 * rows * width * 960, 9 << 20),
    )(d, weights)


def unpack_attn_kernel(all_ref, q_ref, k_ref, v_ref, o_ref):
    hq, hk = HALF_QUERY, HALF_KEY
    both = [
        jnp.concatenate([all_ref[h, b, 0] for b in range(BLOCKS)], axis=1).astype(jnp.float32)
        for h in range(2)
    ]
    start = 0
    for ref, size in ((q_ref, hq), (k_ref, hk), (v_ref, hk), (o_ref, hq)):
        ref[...] = jnp.concatenate([v[:, start : start + size] for v in both], axis=1)
        start += size


def unpack_attn(everyone):
    rows = everyone.shape[3]
    return pl.pallas_call(
        unpack_attn_kernel,
        in_specs=[pl.BlockSpec()],
        out_specs=[pl.BlockSpec()] * 4,
        out_shape=[
            shape((rows, 2 * n), jnp.float32) for n in (HALF_QUERY, HALF_KEY, HALF_KEY, HALF_QUERY)
        ],
        compiler_params=params(),
        cost_estimate=cost(0, 6 << 20),
    )(everyone)


def unpack_ffn_kernel(all_ref, gate_ref, up_ref, down_ref):
    rows, part = all_ref.shape[3], all_ref.shape[4]
    block = BLOCKS * part // 3
    lane = block // BLOCKS
    half = CHUNKS * lane
    for h in range(2):
        for c in range(CHUNKS):
            value = jnp.concatenate([all_ref[h, b, c] for b in range(BLOCKS)], axis=1)
            value = value.astype(jnp.float32)
            for z in range(BLOCKS):
                at = z * 2 * half + h * half + c * lane
                gate_ref[:, at : at + lane] = value[:, z * lane : (z + 1) * lane]
                up_ref[:, at : at + lane] = value[:, block + z * lane : block + (z + 1) * lane]
            down = jnp.concatenate(
                [value[:, 2 * block + q * lane : 2 * block + (q + 1) * lane] for q in range(BLOCKS)],
                axis=0,
            )
            down_ref[h * half + c * lane : h * half + (c + 1) * lane, :] = down.T


def unpack_ffn(everyone):
    rows, part = everyone.shape[3:]
    lane = part // 3
    return pl.pallas_call(
        unpack_ffn_kernel,
        in_specs=[pl.BlockSpec()],
        out_specs=[pl.BlockSpec()] * 3,
        out_shape=[
            shape((rows, 2 * BLOCKS * CHUNKS * lane), jnp.float32),
            shape((rows, 2 * BLOCKS * CHUNKS * lane), jnp.float32),
            shape((2 * CHUNKS * lane, BLOCKS * rows), jnp.float32),
        ],
        compiler_params=params(),
        cost_estimate=cost(0, 16 << 20),
    )(everyone)


def shards(sizes, *arrays):
    (
        tokens, segments, cotangent, attn_gain, w_query, key_matrix, value_matrix, w_out, ffn_gain,
        w_gate, w_up, w_down,
    ) = arrays
    ny, nx, nz = sizes
    tuned = (ny, nx) == (2, 2)
    core, xi = lax.axis_index("core"), lax.axis_index("x")
    place = lax.axis_index("y") * nx + xi
    info = jnp.stack([core, place, lax.axis_index("z"), xi]).astype(jnp.int32)
    tokens, cotangent, ids = tokens[0], cotangent[0], segments[0]
    rows, width = tokens.shape
    own_rows = w_query.shape[0]

    attn_own, *attn_piece = pack_attn(info, (w_query, key_matrix, value_matrix, w_out), tuned)
    ffn_own, *ffn_piece = pack_ffn(info, w_gate, w_up, w_down, tuned)
    weights = gather_weights(info, attn_own, attn_piece[0] if tuned else None, sizes, 0)
    ffn_weights = [
        gather_weights(info, ffn_own[c], ffn_piece[c] if tuned else None, sizes, c + 1)
        for c in range(CHUNKS)
    ]
    weights_other = swap_core(weights[2:])

    all_ids = lax.all_gather(ids, "x", axis=0, tiled=True)
    first = jnp.sum((all_ids[:, None] < ids[None, :]).astype(jnp.int32), axis=0)
    firsts = jnp.concatenate([first[None], swap_core(first[None])])
    token_place = xi * rows + jnp.arange(rows, dtype=jnp.int32)
    positions = (token_place[None] - firsts).reshape(-1)
    angles = inverse_freq()[:, None] * positions.astype(jnp.float32)[None, :]
    cosine, sine = jnp.cos(angles), jnp.sin(angles)
    size = rows // 2
    starts = firsts.reshape(2, rows // size, size)[:, :, 0] // size
    info = jnp.concatenate([info, starts.reshape(-1)])
    firsts = firsts[:, None, :]

    gains = lax.all_gather(jnp.stack([attn_gain, ffn_gain]).astype(low_type), "z", axis=1, tiled=True)
    gain_one, gain_two = gains[:1].astype(jnp.float32), gains[1:].astype(jnp.float32)

    turned = cotangent.T
    cs, cts = (cotangent, swap_core(cotangent)), (turned, swap_core(turned))

    normed, query, keyvalue = project(
        tokens, swap_core(tokens), gain_one, weights, cosine, sine
    )
    if nx == 2:
        past = lax.ppermute(keyvalue, "x", [(0, 1)])[None]
    else:
        past = lax.all_gather(keyvalue, "x", axis=0)
    attended, log_total = attend(info, query, keyvalue, past, firsts, size)
    came = swap_core(attended[:, rows:].astype(low_type))
    middle, normed_two, normed_turned, out_rows = project_out(
        info, attended, came, weights, weights_other, tokens, gain_two
    )

    xs, xts = (normed_two, swap_core(normed_two)), (normed_turned, swap_core(normed_turned))
    sums, ffn_sent = (), []
    for c in range(CHUNKS):
        *sums, = ffn_chunk(info, xs, cs, xts, cts, ffn_weights[c], sums, tuned)
        sums, sent = sums[:2], sums[2:]
        ffn_sent.append(sent)
    result, grad_normed_two = sums

    def pair_sum(value):
        return value[:rows] + swap_core(value[rows:].astype(low_type)).astype(jnp.float32)

    grad_normed_two = pair_sum(grad_normed_two)
    scale_two = norm_scale(middle)
    grad_gain_two = jnp.sum(grad_normed_two * middle * scale_two, axis=0)
    grad_middle = cotangent.astype(jnp.float32) + norm_back(
        grad_normed_two * gain_two, middle, scale_two
    )
    grad_branch = grad_middle.astype(low_type)
    output = (middle + pair_sum(result)).astype(low_type)

    grad_other = swap_core(grad_branch)
    grad_attended, delta, grad_rows = branch(grad_branch, grad_other, out_rows, attended)
    hq = HALF_QUERY
    mine = lax.dynamic_slice_in_dim(grad_rows, core * hq, hq, 1)
    other = swap_core(lax.dynamic_slice_in_dim(grad_rows, (1 - core) * hq, hq, 1))
    grad_query, grad_kv, grad_past = attend_back(
        info, query, keyvalue, past, grad_attended, firsts, log_total, delta, size
    )
    if nx == 2:
        came = lax.ppermute(grad_past[0], "x", [(1, 0)])
    else:
        came = lax.psum_scatter(grad_past, "x", scatter_dimension=0, tiled=True)[0]
    grad_projected, *attn_sent = attn_grads(
        info, grad_query, grad_kv, came, cosine, sine, normed, mine, other, tuned
    )
    normed_mine, normed_other = normed_grad(grad_projected, weights)
    grad_normed = normed_mine + swap_core(normed_other).astype(jnp.float32)
    inputs = tokens.astype(jnp.float32)
    scale_one = norm_scale(inputs)
    grad_gain_one = jnp.sum(grad_normed * inputs * scale_one, axis=0)
    grad_inputs = (
        grad_middle + norm_back(grad_normed * gain_one, inputs, scale_one)
    ).astype(low_type)

    gain_grads = jnp.stack([grad_gain_one, grad_gain_two])
    for axis, count in (("core", 2), ("x", nx), ("y", ny), ("z", nz)):
        gain_grads = sum_over(gain_grads, axis, count)
    gain_grads = lax.dynamic_slice_in_dim(gain_grads, lax.axis_index("z") * own_rows, own_rows, 1)

    ffn_sums = jnp.stack([scatter_gradients(sent, sizes) for sent in ffn_sent])
    attn_sum = scatter_gradients(attn_sent, sizes)
    grad_w_gate, grad_w_up, grad_w_down = unpack_ffn(spread(ffn_sums, sizes))
    attn_out = unpack_attn(spread(attn_sum[None], sizes))
    return (
        output[None], grad_inputs[None], gain_grads[0], *attn_out, gain_grads[1], grad_w_gate,
        grad_w_up, grad_w_down,
    )


def solution(mesh):
    dp, ctx, fsdp = (mesh.shape[name] for name in ("dp", "ctx", "fsdp"))
    fine = Mesh(mesh.devices.reshape(dp // 2, 2, ctx, fsdp), ("y", "core", "x", "z"))
    sizes = (dp // 2, ctx, fsdp)
    wide = P(("y", "core", "z"), "x", None)
    matrix, vector = P("z", None), P("z")
    in_specs = (
        wide, P(("y", "core", "z"), "x"), wide, vector, matrix, matrix, matrix, matrix, vector,
        matrix, matrix, matrix,
    )
    out_specs = (
        wide, wide, vector, matrix, matrix, matrix, matrix, vector, matrix, matrix, matrix
    )

    def layer(*arrays):
        return shards(sizes, *arrays)

    return jax.shard_map(
        layer, mesh=fine, in_specs=in_specs, out_specs=out_specs, check_vma=False
    )
```

```python
import math

import jax
import jax.numpy as jnp
from jax import lax
from jax.experimental import pallas as pl
from jax.experimental.pallas import tpu as pltpu
from jax.sharding import Mesh
from jax.sharding import PartitionSpec as P

QUERY_HEADS = 18
KEY_VALUE_HEADS = 6
HEAD_WIDTH = 64
TURN = HEAD_WIDTH // 2
GROUP = QUERY_HEADS // KEY_VALUE_HEADS
GROUPS = KEY_VALUE_HEADS // 2
HALF_QUERY = QUERY_HEADS // 2 * HEAD_WIDTH
HALF_KEY = GROUPS * HEAD_WIDTH
CHUNKS = 3
BLOCKS = 4
GAIN_ROWS = 16

low_type = jnp.bfloat16
eps_norm = 1e-05
masked_score = -1e30
lowest_peak = -1e20
LOG2E = math.log2(math.e)
SCORE_SCALE = HEAD_WIDTH ** (-0.5)
VMEM_LIMIT = 58 * 1024 * 1024

PAIR = [(0, 1), (1, 0)]
ANY = pl.BlockSpec(memory_space=pl.ANY)
SCALARS = pl.BlockSpec(memory_space=pltpu.SMEM)


def inverse_freq():
    return 10000.0 ** (-(jnp.arange(TURN, dtype=jnp.float32) * 2.0) / HEAD_WIDTH)


def norm_scale(value):
    return lax.rsqrt(jnp.mean(value * value, axis=-1, keepdims=True) + eps_norm)


def norm_back(scaled, value, scale):
    return scale * scaled - value * scale**3 * jnp.mean(scaled * value, axis=-1, keepdims=True)


def dot(left, right, over=(1, 0)):
    return lax.dot_general(
        left, right, (((over[0],), (over[1],)), ((), ())), preferred_element_type=jnp.float32
    )


def swap_core(value):
    return lax.ppermute(value, "core", PAIR)


def behind(value, others):
    return lax.optimization_barrier((value, *others))[0]


def ignoring(kernel, given, after):
    def wrapped(*refs):
        kernel(*refs[:given], *refs[given + len(after) :])

    return wrapped


def params():
    return pltpu.CompilerParams(vmem_limit_bytes=VMEM_LIMIT)


def cost(flops, moved, special=0):
    return pl.CostEstimate(flops=int(flops), bytes_accessed=int(moved), transcendentals=int(special))


def shape(dims, kind=low_type):
    return jax.ShapeDtypeStruct(tuple(dims), kind)


def pack_attn_kernel(info, q_ref, k_ref, v_ref, o_ref, gain_ref, own_ref, *piece_ref):
    def half(ref):
        size = ref.shape[1] // 2
        value = ref[...].astype(low_type)
        return jnp.where(info[0] == 0, value[:, :size], value[:, size:])

    own_ref[...] = jnp.concatenate([half(r) for r in (q_ref, k_ref, v_ref, o_ref)], axis=1)
    rows = own_ref.shape[0]
    for ref in piece_ref:
        part = ref.shape[1]
        ref[:rows, :] = own_ref[:, pl.ds(pl.multiple_of(info[1] * part, part), part)]
        gains = jnp.concatenate([gain_ref[...], jnp.zeros((GAIN_ROWS - 2, rows), jnp.float32)], axis=0)
        gains = jnp.concatenate([gains, jnp.zeros((GAIN_ROWS, part - rows), jnp.float32)], axis=1)
        ref[rows:, :] = gains.astype(low_type)


def pack_attn(info, arrays, gains, tuned):
    rows = arrays[0].shape[0]
    width = sum(a.shape[1] for a in arrays) // 2
    outs = [shape((rows, width))] + [shape((rows + GAIN_ROWS, width // BLOCKS))] * tuned
    return pl.pallas_call(
        pack_attn_kernel,
        in_specs=[SCALARS] + [pl.BlockSpec()] * 5,
        out_specs=[pl.BlockSpec()] * len(outs),
        out_shape=outs,
        compiler_params=params(),
        cost_estimate=cost(0, rows * width * 10),
    )(info, *arrays, gains)


def pack_ffn_kernel(info, gate_ref, up_ref, down_ref, own_ref, *piece_ref):
    step, steps = pl.program_id(0), pl.num_programs(0)
    part = gate_ref.shape[1] // CHUNKS
    rows = gate_ref.shape[0]
    blocks = own_ref.shape[2] // part // 3
    for c in range(CHUNKS):
        at = slice(c * part, (c + 1) * part)
        here = pl.ds(pl.multiple_of(step * part, part), part)
        own_ref[c, :, here] = gate_ref[:, at].astype(low_type)
        there = pl.ds(pl.multiple_of((blocks + step) * part, part), part)
        own_ref[c, :, there] = up_ref[:, at].astype(low_type)

    @pl.when(step == 0)
    def _():
        turned = down_ref[...].astype(low_type).T
        for c in range(CHUNKS):
            for q in range(blocks):
                own_ref[c, :, (2 * blocks + q) * part : (2 * blocks + q + 1) * part] = turned[
                    q * rows : (q + 1) * rows, c * part : (c + 1) * part
                ]

    @pl.when(step == steps - 1)
    def _():
        if piece_ref:
            one, rest = piece_ref
            size = one.shape[1]
            at = pl.ds(pl.multiple_of(info[1] * size, size), size)
            one[...] = own_ref[0, :, at]
            rest[...] = own_ref[1:, :, at]


def pack_ffn(info, gate, up, down, tuned):
    rows, hidden = gate.shape
    hidden_rows, width = down.shape
    steps = hidden // hidden_rows
    half = hidden_rows // 2
    packed = 3 * steps * (half // CHUNKS)
    part = packed // BLOCKS
    outs = [shape((CHUNKS, rows, packed))]
    if tuned:
        outs += [shape((rows, part)), shape((CHUNKS - 1, rows, part))]
    columns = pl.BlockSpec((rows, half), lambda z, info: (0, 2 * z + info[0]))
    return pl.pallas_call(
        pack_ffn_kernel,
        grid_spec=pltpu.PrefetchScalarGridSpec(
            num_scalar_prefetch=1,
            grid=(steps,),
            in_specs=[columns, columns, pl.BlockSpec((half, width), lambda z, info: (info[0], 0))],
            out_specs=[
                pl.BlockSpec(o.shape, lambda z, info, n=len(o.shape): (0,) * n) for o in outs
            ],
        ),
        out_shape=outs,
        compiler_params=params(),
        cost_estimate=cost(0, rows * packed * CHUNKS * 6),
    )(info, gate, up, down)


def ring(count, step):
    return [(i, (i + step) % count) for i in range(count)]


def place_pieces(info, count, own, stacks, forward, out_ref, sems):
    rows, part = own.shape[0], out_ref.shape[2]
    copies = []

    def begin(source, block, row):
        target = out_ref.at[block, pl.ds(pl.multiple_of(row * rows, rows), rows), :]
        copies.append(pltpu.make_async_copy(source, target, sems.at[len(copies)]))
        copies[-1].start()

    for b in range(BLOCKS):
        begin(own.at[:, b * part : (b + 1) * part], b, info[2])
    for flip, stack in enumerate(stacks):
        for k in range(1, count):
            row = lax.rem(info[2] + (k if forward else count - k), count)
            begin(stack.at[k - 1], jnp.bitwise_xor(info[1], flip), row)
    return copies


def assemble(info, own, stacks, count):
    rows, width = own.shape
    out = shape((BLOCKS, rows * count, width // BLOCKS))

    def kernel(info, own_ref, *refs):
        for copy in place_pieces(info, count, own_ref, refs[:-2], False, refs[-2], refs[-1]):
            copy.wait()

    return pl.pallas_call(
        kernel,
        in_specs=[SCALARS] + [ANY] * (1 + len(stacks)),
        out_specs=pl.BlockSpec(),
        out_shape=out,
        scratch_shapes=[pltpu.SemaphoreType.DMA((BLOCKS * count,))],
        compiler_params=params(),
        cost_estimate=cost(0, rows * width * count * 4),
    )(info, own, *stacks)


def pick_kernel(info, all_ref, *refs):
    outs, sems = refs[:-1], refs[-1]
    count = all_ref.shape[0]
    copies = []
    for c, out in enumerate(outs):
        for k in range(1, count):
            source = all_ref.at[lax.rem(info[2] + k, count), c]
            copies.append(pltpu.make_async_copy(source, out.at[k - 1], sems.at[len(copies)]))
            copies[-1].start()
    for copy in copies:
        copy.wait()


def pick(info, everyone):
    count, chunks, rows, part = everyone.shape
    return pl.pallas_call(
        pick_kernel,
        in_specs=[SCALARS, ANY],
        out_specs=[pl.BlockSpec()] * chunks,
        out_shape=[shape((count - 1, rows, part))] * chunks,
        scratch_shapes=[pltpu.SemaphoreType.DMA((chunks * (count - 1),))],
        compiler_params=params(),
        cost_estimate=cost(0, count * chunks * rows * part * 4),
    )(info, everyone)


def travel_z(piece, sizes):
    return [lax.ppermute(piece, "z", ring(sizes[2], k)) for k in range(1, sizes[2])]


def gather_whole(own):
    full = lax.all_gather(own, "z", axis=0, tiled=True)
    return full.reshape(full.shape[0], BLOCKS, -1).transpose(1, 0, 2)


def send_out(info, packed, outs, sems):
    copies = []

    def begin(source, target):
        copies.append(pltpu.make_async_copy(source, target, sems.at[len(copies)]))
        copies[-1].start()

    if len(outs) == 1:
        begin(packed, outs[0])
    else:
        keep_one, send_one, keep_two, send_two = outs
        cut = packed.shape[1] // 2
        y, x = lax.div(info[1], 2), lax.rem(info[1], 2)
        for i in range(2):
            at_y, at_x = jnp.bitwise_xor(y, i), jnp.bitwise_xor(x, i)
            begin(packed.at[at_y * 2 + x, :cut], keep_one.at[i])
            begin(packed.at[at_y * 2 + 1 - x, :cut], send_one.at[i])
            begin(packed.at[y * 2 + at_x, cut:], keep_two.at[i])
            begin(packed.at[(1 - y) * 2 + at_x, cut:], send_two.at[i])
    for copy in copies:
        copy.wait()


def sent_shapes(rows, part, tuned):
    if tuned:
        return [shape((2, rows // 2, part))] * 4
    return [shape((BLOCKS, rows, part))]


def sum_over(value, axis, count):
    if count & (count - 1):
        return lax.psum(value, axis)
    step = 1
    while step < count:
        value = value + lax.ppermute(value, axis, [(i, i ^ step) for i in range(count)])
        step *= 2
    return value


def add_low(kept, came):
    return (kept.astype(jnp.float32) + came.astype(jnp.float32)).astype(low_type)


def scatter_first(outs):
    if len(outs) == 1:
        return ()
    return lax.ppermute(outs[1], "x", PAIR), lax.ppermute(outs[3], "y", PAIR)


def scatter_sums(outs, came, last):
    if len(outs) == 1:
        return ()
    came = lax.optimization_barrier((*came, *last))
    return add_low(outs[0][1], came[0][1]), add_low(outs[2][1], came[1][1])


def scatter_second(sums):
    if len(sums) == 0:
        return ()
    return lax.ppermute(sums[0], "y", PAIR), lax.ppermute(sums[1], "x", PAIR)


def scatter_mine(outs, first, second, last, sizes):
    ny, nx, nz = sizes
    if len(outs) == 1:
        packed = outs[0]
        total = packed.shape[1]
        split = packed.transpose(1, 0, 2).reshape(total, ny * nx, -1).transpose(1, 0, 2)
        return lax.psum_scatter(split, ("y", "x"), scatter_dimension=0, tiled=True)[0]
    second = lax.optimization_barrier((*second, *last))
    one = add_low(add_low(outs[0][0], first[0][0]), second[0])
    two = add_low(add_low(outs[2][0], first[1][0]), second[1])
    return jnp.concatenate([one, two])


def scatter_rows(mine):
    return lax.psum_scatter(mine, "z", scatter_dimension=0, tiled=True)


def spread(mine, sizes):
    everyone = lax.all_gather(mine, ("core", "y", "x"), axis=0)
    both = everyone.reshape((2, sizes[0] * sizes[1]) + mine.shape)
    if sizes[0] * sizes[1] == BLOCKS:
        return both
    both = jnp.moveaxis(both, 1, -2).reshape((2,) + mine.shape[:2] + (BLOCKS, -1))
    return jnp.moveaxis(both, -2, 1)


def turn_heads(ref, value, cosine, sine, start):
    for h in range(value.shape[0] // HEAD_WIDTH):
        former = value[h * HEAD_WIDTH : h * HEAD_WIDTH + TURN]
        latter = value[h * HEAD_WIDTH + TURN : (h + 1) * HEAD_WIDTH]
        at = start + h * HEAD_WIDTH
        ref[at : at + TURN, :] = (former * cosine - latter * sine).astype(ref.dtype)
        ref[at + TURN : at + HEAD_WIDTH, :] = (latter * cosine + former * sine).astype(ref.dtype)


def project_kernel(mine_ref, other_ref, gain_ref, w_ref, cos_ref, sin_ref, normed_ref, q_ref, kv_ref):
    rows = mine_ref.shape[0]
    hk, part = HALF_KEY, w_ref.shape[2]
    for i, ref in enumerate((mine_ref, other_ref)):
        value = ref[...].astype(jnp.float32)
        normed = (value * norm_scale(value) * gain_ref[...]).astype(low_type)
        at = slice(i * rows, (i + 1) * rows)
        normed_ref[:, at] = normed.T
    weights = [w_ref[0].T, w_ref[1].T, w_ref[2].T[:hk]]
    for i in range(2):
        at = slice(i * rows, (i + 1) * rows)
        normed = normed_ref[:, at]
        cosine, sine = cos_ref[:, at], sin_ref[:, at]
        first = dot(weights[0], normed)
        turn_heads(q_ref.at[:, at], first, cosine, sine, 0)
        second = dot(weights[1], normed)
        turn_heads(q_ref.at[:, at], second[: part - hk], cosine, sine, part)
        turn_heads(kv_ref.at[0, :, at], second[part - hk :], cosine, sine, 0)
        kv_ref[1, :, at] = dot(weights[2], normed).astype(low_type)


def project(mine, other, gain, weights, cosine, sine):
    rows, width = mine.shape
    return pl.pallas_call(
        project_kernel,
        in_specs=[pl.BlockSpec()] * 6,
        out_specs=[pl.BlockSpec()] * 3,
        out_shape=[
            shape((width, 2 * rows)), shape((HALF_QUERY, 2 * rows)), shape((2, HALF_KEY, 2 * rows))
        ],
        compiler_params=params(),
        cost_estimate=cost(4 * rows * width * 960, 14 << 20),
    )(mine, other, gain, weights, cosine, sine)


def tile_mask(first, place0, key0, size, causal):
    key_place = key0 + lax.broadcasted_iota(jnp.int32, (size, size), 0)
    allowed = key_place >= first
    if causal:
        place = place0 + lax.broadcasted_iota(jnp.int32, (size, size), 1)
        allowed = allowed & (key_place <= place)
    return jnp.concatenate([allowed] * GROUP, axis=1)


def heads_of(ref):
    return jnp.concatenate(
        [ref[r * HEAD_WIDTH : (r + 1) * HEAD_WIDTH, :] for r in range(GROUP)], axis=1
    )


def over_tiles(info, size, rows, turn):
    per = rows // size
    half = pl.program_id(2)
    own = info[3] * per
    hi = own + half
    lo = info[4 + pl.program_id(0) * per + half]

    def columns(b):
        return pl.ds(pl.multiple_of(lax.rem(b, per) * size, size), size)

    def earlier(b, _):
        turn(hi, b, lax.div(b, per), columns(b))
        return 0

    def here(b, _):
        turn(hi, b, None, columns(b))
        return 0

    lax.fori_loop(lo, own, earlier, 0)
    lax.fori_loop(jnp.maximum(lo, own), hi + 1, here, 0)


def attend_kernel(info, q_ref, kv_ref, past_ref, first_ref, o_ref, total_ref, peak_s, sum_s, acc_s):
    size, rows = q_ref.shape[1], kv_ref.shape[2]
    q = heads_of(q_ref)
    peak_s[...] = jnp.full(peak_s.shape, lowest_peak, jnp.float32)
    sum_s[...] = jnp.zeros(sum_s.shape, jnp.float32)
    acc_s[...] = jnp.zeros(acc_s.shape, jnp.float32)

    def turn(hi, b, past, at):
        k = kv_ref[0, :, at] if past is None else past_ref[past, 0, :, at]
        v = kv_ref[1, :, at] if past is None else past_ref[past, 1, :, at]
        allowed = tile_mask(first_ref[0], hi * size, b * size, size, past is None)
        scores = dot(k, q, (0, 0)) * (SCORE_SCALE * LOG2E)
        scores = jnp.where(allowed, scores, masked_score)
        peak = peak_s[...]
        fresh = jnp.maximum(peak, jnp.max(scores, axis=0, keepdims=True))
        shrink = jnp.exp2(peak - fresh)
        terms = jnp.exp2(scores - fresh)
        peak_s[...] = fresh
        sum_s[...] = sum_s[...] * shrink + jnp.sum(terms, axis=0, keepdims=True)
        acc_s[...] = acc_s[...] * shrink + dot(v, terms.astype(low_type))

    over_tiles(info, size, rows, turn)
    total = sum_s[...]
    mixed = acc_s[...] / total
    log_total = peak_s[...] + jnp.log2(total)
    for r in range(GROUP):
        o_ref[r * HEAD_WIDTH : (r + 1) * HEAD_WIDTH, :] = mixed[:, r * size : (r + 1) * size]
        total_ref[0, r : r + 1, :] = log_total[:, r * size : (r + 1) * size]


def attend_back_kernel(
    info, q_ref, kv_ref, past_ref, g_ref, first_ref, total_ref, delta_ref, dq_ref, dkv_ref, dpast_ref,
    acc_s, past_s,
):
    size, rows = q_ref.shape[1], kv_ref.shape[2]
    q = heads_of(q_ref)
    g = heads_of(g_ref)
    total = jnp.concatenate([total_ref[0, r : r + 1, :] for r in range(GROUP)], axis=1)
    delta = jnp.concatenate([delta_ref[0, r : r + 1, :] for r in range(GROUP)], axis=1)
    acc_s[...] = jnp.zeros(acc_s.shape, jnp.float32)

    @pl.when(pl.program_id(2) == 0)
    def _():
        dkv_ref[...] = jnp.zeros(dkv_ref.shape, jnp.float32)
        past_s[...] = jnp.zeros(past_s.shape, jnp.float32)

    def turn(hi, b, past, at):
        k = kv_ref[0, :, at] if past is None else past_ref[past, 0, :, at]
        v = kv_ref[1, :, at] if past is None else past_ref[past, 1, :, at]
        allowed = tile_mask(first_ref[0], hi * size, b * size, size, past is None)
        scores = dot(k, q, (0, 0)) * (SCORE_SCALE * LOG2E)
        weights = jnp.exp2(jnp.where(allowed, scores - total, masked_score))
        grad_weights = dot(v, g, (0, 0))
        grad_scores = (weights * (grad_weights - delta) * SCORE_SCALE).astype(low_type)
        dk = dot(q, grad_scores, (1, 1))
        dv = dot(g, weights.astype(low_type), (1, 1))
        if past is None:
            dkv_ref[0, :, at] += dk
            dkv_ref[1, :, at] += dv
        else:
            past_s[past, 0, :, at] += dk
            past_s[past, 1, :, at] += dv
        acc_s[...] += dot(k, grad_scores)

    over_tiles(info, size, rows, turn)
    acc = acc_s[...]
    for r in range(GROUP):
        dq_ref[r * HEAD_WIDTH : (r + 1) * HEAD_WIDTH, :] = acc[:, r * size : (r + 1) * size]

    @pl.when(pl.program_id(2) == pl.num_programs(2) - 1)
    def _():
        dpast_ref[...] = past_s[...].astype(low_type)


def attention_specs(parts, rows, size):
    per = rows // size
    wide = pl.BlockSpec((GROUP * HEAD_WIDTH, size), lambda s, g, h: (g, s * per + h))
    own = pl.BlockSpec((2, HEAD_WIDTH, rows), lambda s, g, h: (0, g, s))
    past = pl.BlockSpec((parts, 2, HEAD_WIDTH, rows), lambda s, g, h: (0, 0, g, s))
    first = pl.BlockSpec((1, 1, size), lambda s, g, h: (s, 0, h))
    stat = pl.BlockSpec((1, 8, size), lambda s, g, h: (g, 0, s * per + h))
    return (2, GROUPS, per), wide, own, past, first, stat


def attend(info, query, keyvalue, past, first, size, after):
    both = keyvalue.shape[2]
    rows = both // 2
    grid, wide, own, past_spec, first_spec, stat = attention_specs(past.shape[0], rows, size)
    pairs = 2 * rows * rows * 3 // 2
    return pl.pallas_call(
        ignoring(attend_kernel, 5, after),
        grid=grid,
        in_specs=[SCALARS, wide, own, past_spec, first_spec] + [ANY] * len(after),
        out_specs=[wide, stat],
        out_shape=[shape(query.shape, jnp.float32), shape((GROUPS, 8, both), jnp.float32)],
        scratch_shapes=[
            pltpu.VMEM((1, GROUP * size), jnp.float32),
            pltpu.VMEM((1, GROUP * size), jnp.float32),
            pltpu.VMEM((HEAD_WIDTH, GROUP * size), jnp.float32),
        ],
        compiler_params=params(),
        cost_estimate=cost(pairs * 9 * 64 * 4 * 5, 8 << 20, pairs * 9),
    )(info, query, keyvalue, past, first, *after)


def attend_back(info, query, keyvalue, past, grad, first, log_total, delta, size, after):
    both = keyvalue.shape[2]
    rows = both // 2
    grid, wide, own, past_spec, first_spec, stat = attention_specs(past.shape[0], rows, size)
    pairs = 2 * rows * rows * 3 // 2
    return pl.pallas_call(
        ignoring(attend_back_kernel, 8, after),
        grid=grid,
        in_specs=[SCALARS, wide, own, past_spec, wide, first_spec, stat, stat] + [ANY] * len(after),
        out_specs=[wide, own, past_spec],
        out_shape=[
            shape(query.shape, jnp.float32), shape(keyvalue.shape, jnp.float32), shape(past.shape)
        ],
        scratch_shapes=[
            pltpu.VMEM((HEAD_WIDTH, GROUP * size), jnp.float32),
            pltpu.VMEM((past.shape[0], 2, HEAD_WIDTH, rows), jnp.float32),
        ],
        compiler_params=params(),
        cost_estimate=cost(pairs * 9 * 64 * 10 * 3, 12 << 20, pairs * 9),
    )(info, query, keyvalue, past, grad, first, log_total, delta, *after)


def place_out(core, mine_ref, other_ref, out_ref):
    cut, part = HALF_KEY, mine_ref.shape[2]
    mine = jnp.concatenate([mine_ref[0][:, cut:], mine_ref[1]], axis=1)
    other = jnp.concatenate([other_ref[0][:, cut:], other_ref[1]], axis=1)
    out_ref[...] = jnp.where(
        core == 0,
        jnp.concatenate([mine, other], axis=1),
        jnp.concatenate([other, mine], axis=1),
    )


def out_kernel(
    info, mine_ref, came_ref, w_ref, w_other_ref, tokens_ref, gain_ref, middle_ref, normed_ref,
    turned_ref, rows_ref, w_s,
):
    place_out(info[0], w_ref, w_other_ref, w_s)
    hq = HALF_QUERY
    mine = w_s[pl.ds(pl.multiple_of(info[0] * hq, hq), hq), :]
    other = w_s[pl.ds(pl.multiple_of((1 - info[0]) * hq, hq), hq), :]
    rows_ref[...] = mine
    middle = (
        tokens_ref[...].astype(jnp.float32)
        + dot(mine_ref[...].astype(low_type).T, mine)
        + dot(came_ref[...].T, other)
    )
    middle_ref[...] = middle
    normed = (middle * norm_scale(middle) * gain_ref[...]).astype(low_type)
    normed_ref[...] = normed
    turned_ref[...] = normed.T


def project_out(info, attended, came, weights, weights_other, tokens, gain, after):
    rows, width = tokens.shape
    hq = HALF_QUERY
    part = weights.shape[2]
    return pl.pallas_call(
        ignoring(out_kernel, 7, after),
        grid=(1,),
        in_specs=[
            SCALARS,
            pl.BlockSpec((hq, rows), lambda i: (0, 0)),
            pl.BlockSpec((hq, rows), lambda i: (0, 0)),
            pl.BlockSpec((2, width, part), lambda i: (1, 0, 0)),
            pl.BlockSpec((2, width, part), lambda i: (0, 0, 0)),
            pl.BlockSpec((rows, width), lambda i: (0, 0)),
            pl.BlockSpec((1, width), lambda i: (0, 0)),
        ]
        + [ANY] * len(after),
        out_specs=[
            pl.BlockSpec((rows, width), lambda i: (0, 0)),
            pl.BlockSpec((rows, width), lambda i: (0, 0)),
            pl.BlockSpec((width, rows), lambda i: (0, 0)),
            pl.BlockSpec((hq, width), lambda i: (0, 0)),
        ],
        out_shape=[
            shape((rows, width), jnp.float32), shape((rows, width)), shape((width, rows)),
            shape((hq, width)),
        ],
        scratch_shapes=[pltpu.VMEM((width, width), low_type)],
        compiler_params=params(),
        cost_estimate=cost(2 * rows * width * width, 16 << 20),
    )(info, attended, came, weights, weights_other, tokens, gain, *after)


def ffn_kernel(chunk, pieces, held, after, info, *refs):
    x_refs, c_refs, xt_refs, ct_refs, w_ref = refs[0:2], refs[2:4], refs[4:6], refs[6:8], refs[8]
    others = refs[9 : 9 + pieces]
    refs = refs[9 + pieces :]
    sums = refs[: 2 * held]
    refs = refs[2 * held + after :]
    result_ref, grad_ref, outs = refs[0], refs[1], refs[2:-9]
    gate_s, up_s, down_s, hidden_s, dgate_s, dup_s, packed_s, sems, place_sems = refs[-9:]
    step = pl.program_id(0)
    size = result_ref.shape[0]
    half = 2
    block = gate_s.shape[1]
    part = packed_s.shape[2]
    width = gate_s.shape[0]
    lane = block // BLOCKS
    rows = width // BLOCKS

    @pl.when(step == 0)
    def _():
        if pieces:
            copies = place_pieces(
                info, BLOCKS, w_ref.at[chunk], others, chunk > 0, packed_s, place_sems
            )
        else:
            copies = [pltpu.make_async_copy(w_ref, packed_s, place_sems.at[0])]
            copies[0].start()
        for copy in copies:
            copy.wait()
        gate_s[:, :part] = packed_s[0]
        gate_s[:, part:] = packed_s[1, :, : block - part]
        up_s[:, : 2 * part - block] = packed_s[1, :, block - part :]
        up_s[:, 2 * part - block :] = packed_s[2, :, : 2 * block - 2 * part]
        for q in range(BLOCKS):
            for z in range(BLOCKS):
                column = 2 * block + q * lane
                b, at = column // part, column % part
                down_s[q * rows : (q + 1) * rows, z * lane : (z + 1) * lane] = packed_s[
                    b, z * rows : (z + 1) * rows, at : at + lane
                ]

    @pl.when(step < 2 * half)
    def _():
        mine = step < half
        x = jnp.where(mine, x_refs[0][...], x_refs[1][...])
        c = jnp.where(mine, c_refs[0][...], c_refs[1][...])
        gate = dot(x, gate_s[...])
        upward = dot(x, up_s[...])
        grad_hidden = dot(c, down_s[...])
        sigmoid = 1.0 / (1.0 + jnp.exp(-gate))
        silu = gate * sigmoid
        hidden = (silu * upward).astype(low_type)
        grad_gate = (grad_hidden * upward * sigmoid * (1.0 + gate * (1.0 - sigmoid))).astype(low_type)
        grad_up = (grad_hidden * silu).astype(low_type)
        at = pl.ds(pl.multiple_of(step * size, size), size)
        hidden_s[at, :] = hidden
        dgate_s[at, :] = grad_gate
        dup_s[at, :] = grad_up
        result = dot(hidden, down_s[...], (1, 1))
        grad = dot(grad_gate, gate_s[...], (1, 1)) + dot(grad_up, up_s[...], (1, 1))
        if held:
            result = result + sums[0][...]
            grad = grad + sums[1][...]
        result_ref[...] = result
        grad_ref[...] = grad

    @pl.when(step >= 2 * half)
    def _():
        q = step - 2 * half
        cut = half * size
        at = pl.ds(pl.multiple_of(q * rows, rows), rows)
        gate = dot(xt_refs[0][...], dgate_s[:cut]) + dot(xt_refs[1][...], dgate_s[cut:])
        up = dot(xt_refs[0][...], dup_s[:cut]) + dot(xt_refs[1][...], dup_s[cut:])
        down = dot(ct_refs[0][...], hidden_s[:cut]) + dot(ct_refs[1][...], hidden_s[cut:])
        gate, up, down = gate.astype(low_type), up.astype(low_type), down.astype(low_type)
        packed_s[0, at, :] = gate[:, :part]
        packed_s[1, at, : block - part] = gate[:, part:]
        packed_s[1, at, block - part :] = up[:, : 2 * part - block]
        packed_s[2, at, : 2 * block - 2 * part] = up[:, 2 * part - block :]
        column = 2 * block + q * lane
        b = lax.div(column, part)
        there = pl.ds(pl.multiple_of(lax.rem(column, part), lane), lane)
        for z in range(BLOCKS):
            packed_s[b, z * rows : (z + 1) * rows, there] = down[:, z * lane : (z + 1) * lane]

    @pl.when(step == pl.num_programs(0) - 1)
    def _():
        send_out(info, packed_s, outs, sems)


def ffn_chunk(chunk, info, xs, cs, xts, cts, weights, pieces, sums, after, tuned):
    rows, width = xs[0].shape
    size = rows // 2
    part = weights.shape[2] // (BLOCKS if tuned else 1)
    block = BLOCKS * part // 3
    turned = width // BLOCKS

    def first(i):
        return (jnp.minimum(i, 1), 0)

    def second(i):
        return (jnp.clip(i - 2, 0, 1), 0)

    def either(i):
        return (jnp.minimum(i, 3), 0)

    def later(i):
        return (jnp.maximum(i - 4, 0), 0)

    token = [pl.BlockSpec((size, width), first), pl.BlockSpec((size, width), second)]
    across = [pl.BlockSpec((turned, rows), later)] * 2
    total = [pl.BlockSpec((size, width), either)] * 2
    held = len(sums) > 0
    sent = sent_shapes(width, part, tuned)

    def kernel(info, *refs):
        ffn_kernel(chunk, len(pieces), held, len(after), info, *refs)

    return pl.pallas_call(
        kernel,
        grid=(8,),
        in_specs=[SCALARS] + token + token + across + across + [ANY] * (1 + len(pieces))
        + (total if held else []) + [ANY] * len(after),
        out_specs=total + [ANY] * len(sent),
        out_shape=[shape((2 * rows, width), jnp.float32)] * 2 + sent,
        scratch_shapes=[
            pltpu.VMEM((width, block), low_type),
            pltpu.VMEM((width, block), low_type),
            pltpu.VMEM((width, block), low_type),
            pltpu.VMEM((2 * rows, block), low_type),
            pltpu.VMEM((2 * rows, block), low_type),
            pltpu.VMEM((2 * rows, block), low_type),
            pltpu.VMEM((BLOCKS, width, part), low_type),
            pltpu.SemaphoreType.DMA((8,)),
            pltpu.SemaphoreType.DMA((BLOCKS * BLOCKS,)),
        ],
        compiler_params=params(),
        cost_estimate=cost(18 * 2 * rows * width * block, 40 << 20, 2 * rows * block),
    )(info, *xs, *cs, *xts, *cts, weights, *pieces, *sums, *after)


def branch_kernel(g_ref, g_other_ref, w_ref, attended_ref, grad_ref, delta_ref, rows_ref):
    rows = g_ref.shape[0]
    delta_ref[...] = jnp.zeros(delta_ref.shape, jnp.float32)
    for i, ref in enumerate((g_ref, g_other_ref)):
        at = slice(i * rows, (i + 1) * rows)
        grad = dot(w_ref[...], ref[...], (1, 1)).astype(low_type)
        grad_ref[:, at] = grad
        product = grad.astype(jnp.float32) * attended_ref[:, at]
        for h in range(GROUP * GROUPS):
            delta_ref[h // GROUP, h % GROUP : h % GROUP + 1, at] = jnp.sum(
                product[h * HEAD_WIDTH : (h + 1) * HEAD_WIDTH], axis=0, keepdims=True
            )
    attended = attended_ref[...].astype(low_type)
    rows_ref[...] = (
        dot(attended[:, :rows], g_ref[...]) + dot(attended[:, rows:], g_other_ref[...])
    ).astype(low_type)


def branch(grad, grad_other, out_rows, attended, after):
    rows, width = grad.shape
    return pl.pallas_call(
        ignoring(branch_kernel, 4, after),
        in_specs=[pl.BlockSpec()] * 4 + [ANY] * len(after),
        out_specs=[pl.BlockSpec()] * 3,
        out_shape=[
            shape(attended.shape), shape((GROUPS, 8, 2 * rows), jnp.float32),
            shape((HALF_QUERY, width)),
        ],
        compiler_params=params(),
        cost_estimate=cost(8 * rows * width * HALF_QUERY, 12 << 20),
    )(grad, grad_other, out_rows, attended, *after)


def attn_grad_kernel(
    info, dq_ref, dkv_ref, came_ref, cos_ref, sin_ref, normed_ref, mine_ref, other_ref, d_ref, *refs
):
    outs, packed_s, sems = refs[:-2], refs[-2], refs[-1]
    hq, hk = HALF_QUERY, HALF_KEY
    part = packed_s.shape[2]
    cosine, sine = cos_ref[...], -sin_ref[...]
    turn_heads(d_ref, dq_ref[...], cosine, sine, 0)
    whole = dkv_ref[...] + came_ref[...].astype(jnp.float32)
    turn_heads(d_ref, whole[0], cosine, sine, hq)
    d_ref[hq + hk :, :] = whole[1].astype(low_type)
    normed = normed_ref[...]
    packed_s[0] = dot(normed, d_ref[:part, :], (1, 1)).astype(low_type)
    packed_s[1] = dot(normed, d_ref[part : 2 * part, :], (1, 1)).astype(low_type)
    last = dot(normed, d_ref[2 * part :, :], (1, 1)).astype(low_type)
    mine, other = mine_ref[...], other_ref[...]
    low = info[0] == 0
    out = jnp.concatenate(
        [jnp.where(low, mine, other), jnp.where(low, other, mine)], axis=0
    )
    packed_s[2] = jnp.concatenate([last, out[:, : part - hk]], axis=1)
    packed_s[3] = out[:, part - hk :]
    send_out(info, packed_s, outs, sems)


def attn_grads(info, grad_query, grad_kv, came, cosine, sine, normed, mine, other, after, tuned):
    width, both = normed.shape
    part = (2 * HALF_QUERY + 2 * HALF_KEY) // BLOCKS
    sent = sent_shapes(width, part, tuned)
    return pl.pallas_call(
        ignoring(attn_grad_kernel, 9, after),
        in_specs=[SCALARS] + [pl.BlockSpec()] * 8 + [ANY] * len(after),
        out_specs=[pl.BlockSpec()] + [ANY] * len(sent),
        out_shape=[shape((HALF_QUERY + 2 * HALF_KEY, both))] + sent,
        scratch_shapes=[
            pltpu.VMEM((BLOCKS, width, part), low_type),
            pltpu.SemaphoreType.DMA((8,)),
        ],
        compiler_params=params(),
        cost_estimate=cost(2 * both * width * 960, 20 << 20),
    )(info, grad_query, grad_kv, came, cosine, sine, normed, mine, other, *after)


def normed_grad_kernel(d_ref, w_ref, mine_ref, other_ref):
    rows = mine_ref.shape[0]
    hk, part = HALF_KEY, w_ref.shape[2]
    for i, ref in enumerate((other_ref, mine_ref)):
        at = slice((1 - i) * rows, (2 - i) * rows)
        d = d_ref[:, at].T
        value = dot(d[:, :part], w_ref[0], (1, 1)) + dot(d[:, part : 2 * part], w_ref[1], (1, 1))
        value = value + dot(d[:, 2 * part :], w_ref[2][:, :hk], (1, 1))
        ref[...] = value.astype(ref.dtype)


def normed_grad(d, weights, after):
    width = weights.shape[1]
    rows = d.shape[1] // 2
    return pl.pallas_call(
        ignoring(normed_grad_kernel, 2, after),
        in_specs=[pl.BlockSpec()] * 2 + [ANY] * len(after),
        out_specs=[pl.BlockSpec()] * 2,
        out_shape=[shape((rows, width), jnp.float32), shape((rows, width))],
        compiler_params=params(),
        cost_estimate=cost(4 * rows * width * 960, 9 << 20),
    )(d, weights, *after)


def unpack_attn_kernel(all_ref, q_ref, k_ref, v_ref, o_ref):
    hq, hk = HALF_QUERY, HALF_KEY
    both = [
        jnp.concatenate([all_ref[h, b, 0] for b in range(BLOCKS)], axis=1).astype(jnp.float32)
        for h in range(2)
    ]
    start = 0
    for ref, size in ((q_ref, hq), (k_ref, hk), (v_ref, hk), (o_ref, hq)):
        ref[...] = jnp.concatenate([v[:, start : start + size] for v in both], axis=1)
        start += size


def unpack_attn(everyone):
    rows = everyone.shape[3]
    return pl.pallas_call(
        unpack_attn_kernel,
        in_specs=[pl.BlockSpec()],
        out_specs=[pl.BlockSpec()] * 4,
        out_shape=[
            shape((rows, 2 * n), jnp.float32) for n in (HALF_QUERY, HALF_KEY, HALF_KEY, HALF_QUERY)
        ],
        compiler_params=params(),
        cost_estimate=cost(0, 6 << 20),
    )(everyone)


def unpack_ffn_kernel(*refs):
    all_refs, (gate_ref, up_ref, down_ref) = refs[:CHUNKS], refs[CHUNKS:]
    rows, part = all_refs[0].shape[3], all_refs[0].shape[4]
    block = BLOCKS * part // 3
    lane = block // BLOCKS
    half = CHUNKS * lane
    for h in range(2):
        for c in range(CHUNKS):
            value = jnp.concatenate([all_refs[c][h, b, 0] for b in range(BLOCKS)], axis=1)
            value = value.astype(jnp.float32)
            for z in range(BLOCKS):
                at = z * 2 * half + h * half + c * lane
                gate_ref[:, at : at + lane] = value[:, z * lane : (z + 1) * lane]
                up_ref[:, at : at + lane] = value[:, block + z * lane : block + (z + 1) * lane]
            down = jnp.concatenate(
                [value[:, 2 * block + q * lane : 2 * block + (q + 1) * lane] for q in range(BLOCKS)],
                axis=0,
            )
            down_ref[h * half + c * lane : h * half + (c + 1) * lane, :] = down.T


def unpack_ffn(everyone):
    rows, part = everyone[0].shape[3:]
    lane = part // 3
    return pl.pallas_call(
        unpack_ffn_kernel,
        in_specs=[pl.BlockSpec()] * CHUNKS,
        out_specs=[pl.BlockSpec()] * 3,
        out_shape=[
            shape((rows, 2 * BLOCKS * CHUNKS * lane), jnp.float32),
            shape((rows, 2 * BLOCKS * CHUNKS * lane), jnp.float32),
            shape((2 * CHUNKS * lane, BLOCKS * rows), jnp.float32),
        ],
        compiler_params=params(),
        cost_estimate=cost(0, 16 << 20),
    )(*everyone)


def shards(sizes, *arrays):
    (
        tokens, segments, cotangent, attn_gain, w_query, key_matrix, value_matrix, w_out, ffn_gain,
        w_gate, w_up, w_down,
    ) = arrays
    ny, nx, nz = sizes
    tuned = (ny, nx) == (2, 2)
    core, xi = lax.axis_index("core"), lax.axis_index("x")
    place = lax.axis_index("y") * nx + xi
    info = jnp.stack([core, place, lax.axis_index("z"), xi]).astype(jnp.int32)
    tokens, cotangent, ids = tokens[0], cotangent[0], segments[0]
    rows, width = tokens.shape
    own_rows = w_query.shape[0]

    gains = jnp.stack([attn_gain, ffn_gain])
    attn_own, *attn_piece = pack_attn(
        info, (w_query, key_matrix, value_matrix, w_out), gains, tuned
    )
    ffn_own, *ffn_piece = pack_ffn(info, w_gate, w_up, w_down, tuned)
    if tuned:
        slots = travel_z(attn_piece[0], sizes)
        stack = jnp.stack([s[:own_rows] for s in slots])
        ffn_slots = travel_z(behind(ffn_piece[0], (stack,)), sizes)
        ffn_stacks = [jnp.stack(ffn_slots)]
        rest = lax.all_gather(behind(ffn_piece[1], ffn_slots), "z", axis=0)
        ffn_stacks += pick(info, rest)
        stacks = (
            stack,
            lax.ppermute(stack, "x", PAIR),
            lax.ppermute(stack, "y", PAIR),
            lax.ppermute(stack, ("y", "x"), [(i, 3 - i) for i in range(4)]),
        )
        weights = assemble(info, attn_own, stacks, nz)
        ffn_weights = [ffn_own] * CHUNKS
        gains = [gains.astype(low_type)] + [s[own_rows : own_rows + 2, :own_rows] for s in slots]
        gains = jnp.stack(gains[::-1] + gains[::-1])
        gains = lax.dynamic_slice_in_dim(gains, nz - 1 - lax.axis_index("z"), nz, 0)
        gains = gains.transpose(1, 0, 2).reshape(2, width)
    else:
        weights = gather_whole(attn_own)
        ffn_pieces = [()] * CHUNKS
        before_attend = before_out = ()
        ffn_weights = [gather_whole(ffn_own[c]) for c in range(CHUNKS)]
        gains = lax.all_gather(gains.astype(low_type), "z", axis=1, tiled=True)
    weights_other = swap_core(weights[2:])

    all_ids = lax.all_gather(ids, "x", axis=0, tiled=True)
    first = jnp.sum((all_ids[:, None] < ids[None, :]).astype(jnp.int32), axis=0)
    firsts = jnp.concatenate([first[None], swap_core(first[None])])
    token_place = xi * rows + jnp.arange(rows, dtype=jnp.int32)
    positions = (token_place[None] - firsts).reshape(-1)
    angles = inverse_freq()[:, None] * positions.astype(jnp.float32)[None, :]
    cosine, sine = jnp.cos(angles), jnp.sin(angles)
    size = rows // 2
    starts = firsts.reshape(2, rows // size, size)[:, :, 0] // size
    info = jnp.concatenate([info, starts.reshape(-1)])
    firsts = firsts[:, None, :]

    gain_one, gain_two = gains[:1].astype(jnp.float32), gains[1:].astype(jnp.float32)

    turned = cotangent.T
    cs, cts = (cotangent, swap_core(cotangent)), (turned, swap_core(turned))

    normed, query, keyvalue = project(
        tokens, swap_core(tokens), gain_one, weights, cosine, sine
    )
    if tuned:
        by_x = [lax.ppermute(s, "x", PAIR) for s in ffn_stacks]
        by_y = [lax.ppermute(s, "y", PAIR) for s in ffn_stacks]
        far = [
            lax.ppermute(by_x[0], "y", PAIR),
            lax.ppermute(by_x[1], "y", PAIR),
            lax.ppermute(by_y[2], "x", PAIR),
        ]
        ffn_pieces = list(zip(ffn_stacks, by_x, by_y, far))
        past = lax.ppermute(behind(keyvalue, (by_x[0],)), "x", [(0, 1)])[None]
        before_attend = (by_y[0], *ffn_stacks[1:])
        before_out = (by_x[1], by_y[1], far[0])
    else:
        past = lax.all_gather(keyvalue, "x", axis=0)
    attended, log_total = attend(info, query, keyvalue, past, firsts, size, before_attend)
    came = swap_core(attended[:, rows:].astype(low_type))
    middle, normed_two, normed_turned, out_rows = project_out(
        info, attended, came, weights, weights_other, tokens, gain_two, before_out
    )

    xs, xts = (normed_two, swap_core(normed_two)), (normed_turned, swap_core(normed_turned))
    sums, ready = (), ()
    sent, first, send, second, mine_ffn = ([None] * (CHUNKS + 1) for _ in range(5))
    for c in range(CHUNKS):
        *sums, = ffn_chunk(
            c, info, xs, cs, xts, cts, ffn_weights[c], ffn_pieces[c], sums, ready, tuned
        )
        sums, sent[c] = sums[:2], sums[2:]
        first[c] = scatter_first(sent[c])
        if c >= 1:
            ready = send[c - 1] = scatter_sums(sent[c - 1], first[c - 1], sums[:1])
            second[c - 1] = scatter_second(send[c - 1])
        if c >= 2:
            mine_ffn[c - 2] = scatter_mine(sent[c - 2], first[c - 2], second[c - 2], sums[:1], sizes)
    result, grad_normed_two = sums

    def pair_sum(value):
        return value[:rows] + swap_core(value[rows:].astype(low_type)).astype(jnp.float32)

    grad_normed_two = pair_sum(grad_normed_two)
    scale_two = norm_scale(middle)
    grad_gain_two = jnp.sum(grad_normed_two * middle * scale_two, axis=0)
    grad_middle = cotangent.astype(jnp.float32) + norm_back(
        grad_normed_two * gain_two, middle, scale_two
    )
    grad_branch = grad_middle.astype(low_type)
    output = (middle + pair_sum(result)).astype(low_type)

    grad_other = swap_core(grad_branch)
    grad_attended, delta, grad_rows = branch(
        grad_branch, grad_other, out_rows, attended, (mine_ffn[0], *send[1])
    )
    hq = HALF_QUERY
    mine = lax.dynamic_slice_in_dim(grad_rows, core * hq, hq, 1)
    other = swap_core(lax.dynamic_slice_in_dim(grad_rows, (1 - core) * hq, hq, 1))
    last = (grad_attended,)
    send[2] = scatter_sums(sent[2], first[2], last)
    second[2] = scatter_second(send[2])
    mine_ffn[1] = scatter_mine(sent[1], first[1], second[1], last, sizes)
    grad_query, grad_kv, grad_past = attend_back(
        info, query, keyvalue, past, grad_attended, firsts, log_total, delta, size,
        (*send[2], mine_ffn[1]),
    )
    mine_ffn[2] = scatter_mine(sent[2], first[2], second[2], (grad_past,), sizes)
    ffn_sums = [scatter_rows(mine) for mine in mine_ffn[:CHUNKS]]
    ffn_all = [spread(total[None], sizes) for total in ffn_sums]
    if tuned:
        came = lax.ppermute(grad_past[0], "x", [(1, 0)])
    else:
        came = lax.psum_scatter(grad_past, "x", scatter_dimension=0, tiled=True)[0]
    grad_projected, *attn_sent = attn_grads(
        info, grad_query, grad_kv, came, cosine, sine, normed, mine, other,
        (ffn_sums[0], mine_ffn[2]), tuned,
    )
    normed_mine, normed_other = normed_grad(grad_projected, weights, ())
    grad_normed = normed_mine + swap_core(normed_other).astype(jnp.float32)
    inputs = tokens.astype(jnp.float32)
    scale_one = norm_scale(inputs)
    grad_gain_one = jnp.sum(grad_normed * inputs * scale_one, axis=0)
    grad_inputs = (
        grad_middle + norm_back(grad_normed * gain_one, inputs, scale_one)
    ).astype(low_type)

    gain_grads = jnp.stack([grad_gain_one, grad_gain_two])
    for axis, count in (("core", 2), ("x", nx), ("y", ny), ("z", nz)):
        gain_grads = sum_over(gain_grads, axis, count)
    gain_grads = lax.dynamic_slice_in_dim(gain_grads, lax.axis_index("z") * own_rows, own_rows, 1)

    sent[3], first[3] = attn_sent, scatter_first(attn_sent)
    send[3] = scatter_sums(attn_sent, first[3], (normed_mine, ffn_all[0]))
    second[3] = scatter_second(send[3])
    mine_attn = scatter_mine(attn_sent, first[3], second[3], (ffn_all[1],), sizes)
    attn_sum = scatter_rows(mine_attn)
    grad_w_gate, grad_w_up, grad_w_down = unpack_ffn(ffn_all)
    attn_out = unpack_attn(spread(attn_sum[None], sizes))
    return (
        output[None], grad_inputs[None], gain_grads[0], *attn_out, gain_grads[1], grad_w_gate,
        grad_w_up, grad_w_down,
    )


def solution(mesh):
    dp, ctx, fsdp = (mesh.shape[name] for name in ("dp", "ctx", "fsdp"))
    fine = Mesh(mesh.devices.reshape(dp // 2, 2, ctx, fsdp), ("y", "core", "x", "z"))
    sizes = (dp // 2, ctx, fsdp)
    wide = P(("y", "core", "z"), "x", None)
    matrix, vector = P("z", None), P("z")
    in_specs = (
        wide, P(("y", "core", "z"), "x"), wide, vector, matrix, matrix, matrix, matrix, vector,
        matrix, matrix, matrix,
    )
    out_specs = (
        wide, wide, vector, matrix, matrix, matrix, matrix, vector, matrix, matrix, matrix
    )

    def layer(*arrays):
        return shards(sizes, *arrays)

    return jax.shard_map(
        layer, mesh=fine, in_specs=in_specs, out_specs=out_specs, check_vma=False
    )
```

```python
import math

import jax
import jax.numpy as jnp
from jax import lax
from jax.experimental import pallas as pl
from jax.experimental.pallas import tpu as pltpu
from jax.sharding import Mesh
from jax.sharding import PartitionSpec as P

QUERY_HEADS = 18
KEY_VALUE_HEADS = 6
HEAD_WIDTH = 64
TURN = HEAD_WIDTH // 2
GROUP = QUERY_HEADS // KEY_VALUE_HEADS
GROUPS = KEY_VALUE_HEADS // 2
HALF_QUERY = QUERY_HEADS // 2 * HEAD_WIDTH
HALF_KEY = GROUPS * HEAD_WIDTH
CHUNKS = 3
BLOCKS = 4
GAIN_ROWS = 16
FFN_ROWS = 512
COST = 0.1

low_type = jnp.bfloat16
eps_norm = 1e-05
masked_score = -1e30
lowest_peak = -1e20
LOG2E = math.log2(math.e)
SCORE_SCALE = HEAD_WIDTH ** (-0.5)
VMEM_LIMIT = 58 * 1024 * 1024

PAIR = [(0, 1), (1, 0)]
ANY = pl.BlockSpec(memory_space=pl.ANY)
SCALARS = pl.BlockSpec(memory_space=pltpu.SMEM)


def inverse_freq():
    return 10000.0 ** (-(jnp.arange(TURN, dtype=jnp.float32) * 2.0) / HEAD_WIDTH)


def norm_scale(value):
    return lax.rsqrt(jnp.mean(value * value, axis=-1, keepdims=True) + eps_norm)


def norm_back(scaled, value, scale):
    return scale * scaled - value * scale**3 * jnp.mean(scaled * value, axis=-1, keepdims=True)


def dot(left, right, over=(1, 0)):
    return lax.dot_general(
        left, right, (((over[0],), (over[1],)), ((), ())), preferred_element_type=jnp.float32
    )


def swap_core(value):
    return lax.ppermute(value, "core", PAIR)


def behind(value, others):
    return lax.optimization_barrier((value, *others))[0]


def ignoring(kernel, given, after):
    def wrapped(*refs):
        kernel(*refs[:given], *refs[given + len(after) :])

    return wrapped


def params():
    return pltpu.CompilerParams(vmem_limit_bytes=VMEM_LIMIT)


def cost(flops, moved, special=0):
    return pl.CostEstimate(
        flops=int(flops * COST), bytes_accessed=int(moved * COST), transcendentals=int(special * COST)
    )


def shape(dims, kind=low_type):
    return jax.ShapeDtypeStruct(tuple(dims), kind)


def pack_attn_kernel(info, q_ref, k_ref, v_ref, o_ref, gain_ref, own_ref, *piece_ref):
    def half(ref):
        size = ref.shape[1] // 2
        value = ref[...].astype(low_type)
        return jnp.where(info[0] == 0, value[:, :size], value[:, size:])

    own_ref[...] = jnp.concatenate([half(r) for r in (q_ref, k_ref, v_ref, o_ref)], axis=1)
    rows = own_ref.shape[0]
    for ref in piece_ref:
        part = ref.shape[1]
        ref[:rows, :] = own_ref[:, pl.ds(pl.multiple_of(info[1] * part, part), part)]
        gains = jnp.concatenate([gain_ref[...], jnp.zeros((GAIN_ROWS - 2, rows), jnp.float32)], axis=0)
        gains = jnp.concatenate([gains, jnp.zeros((GAIN_ROWS, part - rows), jnp.float32)], axis=1)
        ref[rows:, :] = gains.astype(low_type)


def pack_attn(info, arrays, gains, tuned):
    rows = arrays[0].shape[0]
    width = sum(a.shape[1] for a in arrays) // 2
    outs = [shape((rows, width))] + [shape((rows + GAIN_ROWS, width // BLOCKS))] * tuned
    return pl.pallas_call(
        pack_attn_kernel,
        in_specs=[SCALARS] + [pl.BlockSpec()] * 5,
        out_specs=[pl.BlockSpec()] * len(outs),
        out_shape=outs,
        compiler_params=params(),
        cost_estimate=cost(0, rows * width * 10),
    )(info, *arrays, gains)


def pack_ffn_kernel(info, gate_ref, up_ref, down_ref, own_ref, *piece_ref):
    step, steps = pl.program_id(0), pl.num_programs(0)
    part = gate_ref.shape[1] // CHUNKS
    rows = gate_ref.shape[0]
    blocks = own_ref.shape[2] // part // 3
    for c in range(CHUNKS):
        at = slice(c * part, (c + 1) * part)
        here = pl.ds(pl.multiple_of(step * part, part), part)
        own_ref[c, :, here] = gate_ref[:, at].astype(low_type)
        there = pl.ds(pl.multiple_of((blocks + step) * part, part), part)
        own_ref[c, :, there] = up_ref[:, at].astype(low_type)

    @pl.when(step == 0)
    def _():
        turned = down_ref[...].astype(low_type).T
        for c in range(CHUNKS):
            for q in range(blocks):
                own_ref[c, :, (2 * blocks + q) * part : (2 * blocks + q + 1) * part] = turned[
                    q * rows : (q + 1) * rows, c * part : (c + 1) * part
                ]

    @pl.when(step == steps - 1)
    def _():
        if piece_ref:
            one, two = piece_ref
            size, cut = one.shape[1], rows // 2
            at = pl.ds(pl.multiple_of(info[1] * size, size), size)
            one[:rows, :] = own_ref[0, :, at]
            one[rows:, :] = own_ref[1, :cut, at]
            two[:cut, :] = own_ref[1, cut:, at]
            two[cut:, :] = own_ref[2, :, at]


def pack_ffn(info, gate, up, down, tuned):
    rows, hidden = gate.shape
    hidden_rows, width = down.shape
    steps = hidden // hidden_rows
    half = hidden_rows // 2
    packed = 3 * steps * (half // CHUNKS)
    part = packed // BLOCKS
    outs = [shape((CHUNKS, rows, packed))]
    if tuned:
        outs += [shape((rows + rows // 2, part))] * 2
    columns = pl.BlockSpec((rows, half), lambda z, info: (0, 2 * z + info[0]))
    return pl.pallas_call(
        pack_ffn_kernel,
        grid_spec=pltpu.PrefetchScalarGridSpec(
            num_scalar_prefetch=1,
            grid=(steps,),
            in_specs=[columns, columns, pl.BlockSpec((half, width), lambda z, info: (info[0], 0))],
            out_specs=[
                pl.BlockSpec(o.shape, lambda z, info, n=len(o.shape): (0,) * n) for o in outs
            ],
        ),
        out_shape=outs,
        compiler_params=params(),
        cost_estimate=cost(0, rows * packed * CHUNKS * 6),
    )(info, gate, up, down)


def ring(count, step):
    return [(i, (i + step) % count) for i in range(count)]


def place_pieces(info, count, own, stacks, forward, out_ref, sems):
    rows, part = own.shape[0], out_ref.shape[2]
    copies = []

    def begin(source, block, row):
        target = out_ref.at[block, pl.ds(pl.multiple_of(row * rows, rows), rows), :]
        copies.append(pltpu.make_async_copy(source, target, sems.at[len(copies)]))
        copies[-1].start()

    for b in range(BLOCKS):
        begin(own.at[:, b * part : (b + 1) * part], b, info[2])
    for flip, stack in enumerate(stacks):
        for k in range(1, count):
            row = lax.rem(info[2] + (k if forward else count - k), count)
            begin(stack.at[k - 1], jnp.bitwise_xor(info[1], flip), row)
    return copies


def assemble(info, own, stacks, count, after):
    rows, width = own.shape
    out = shape((BLOCKS, rows * count, width // BLOCKS))

    def kernel(info, own_ref, *refs):
        for copy in place_pieces(info, count, own_ref, refs[:-2], False, refs[-2], refs[-1]):
            copy.wait()

    return pl.pallas_call(
        ignoring(kernel, 2 + len(stacks), after),
        in_specs=[SCALARS] + [ANY] * (1 + len(stacks) + len(after)),
        out_specs=pl.BlockSpec(),
        out_shape=out,
        scratch_shapes=[pltpu.SemaphoreType.DMA((BLOCKS * count,))],
        compiler_params=params(),
        cost_estimate=cost(0, rows * width * count * 4),
    )(info, own, *stacks, *after)


def pick_kernel(parts, info, *refs):
    ins = refs[: -1 - len({p[0] for p in parts})]
    outs, sems = refs[len(ins) : -1], refs[-1]
    copies = []
    for out, source, start, stop, at in parts:
        count = ins[source].shape[0]
        for k in range(1, count):
            rows = ins[source].at[lax.rem(info[2] + k, count), start:stop]
            target = outs[out].at[k - 1, at : at + stop - start]
            copies.append(pltpu.make_async_copy(rows, target, sems.at[len(copies)]))
            copies[-1].start()
    for copy in copies:
        copy.wait()


def pick(info, arrays, parts, rows):
    count, _, part = arrays[0].shape
    outs = [shape((count - 1, rows, part))] * len({p[0] for p in parts})

    def kernel(*refs):
        pick_kernel(parts, *refs)

    return pl.pallas_call(
        kernel,
        in_specs=[SCALARS] + [ANY] * len(arrays),
        out_specs=[pl.BlockSpec()] * len(outs),
        out_shape=outs,
        scratch_shapes=[pltpu.SemaphoreType.DMA((len(parts) * (count - 1),))],
        compiler_params=params(),
        cost_estimate=cost(0, len(outs) * count * rows * part * 4),
    )(info, *arrays)


def travel_z(piece, sizes):
    return [lax.ppermute(piece, "z", ring(sizes[2], k)) for k in range(1, sizes[2])]


def gather_whole(own):
    full = lax.all_gather(own, "z", axis=0, tiled=True)
    return full.reshape(full.shape[0], BLOCKS, -1).transpose(1, 0, 2)


def send_out(info, packed, outs, way, sems):
    copies = []

    def begin(source, target):
        copies.append(pltpu.make_async_copy(source, target, sems.at[len(copies)]))
        copies[-1].start()

    if way == "whole":
        begin(packed, outs[0])
    elif way == "z":
        count, _, rows, _ = outs[0].shape
        for z in range(count):
            for b in range(BLOCKS):
                begin(packed.at[b, z * rows : (z + 1) * rows], outs[0].at[z, b])
    else:
        keep_one, send_one, keep_two, send_two = outs
        cut = packed.shape[1] // 2
        y, x = lax.div(info[1], 2), lax.rem(info[1], 2)
        for i in range(2):
            at_y, at_x = jnp.bitwise_xor(y, i), jnp.bitwise_xor(x, i)
            begin(packed.at[at_y * 2 + x, :cut], keep_one.at[i])
            begin(packed.at[at_y * 2 + 1 - x, :cut], send_one.at[i])
            begin(packed.at[y * 2 + at_x, cut:], keep_two.at[i])
            begin(packed.at[(1 - y) * 2 + at_x, cut:], send_two.at[i])
    return copies


def sent_shapes(rows, part, way):
    if way == "xy":
        return [shape((2, rows // 2, part))] * 4
    if way == "z":
        return [shape((BLOCKS, BLOCKS, rows // BLOCKS, part))]
    return [shape((BLOCKS, rows, part))]


def split_kernel(info, packed_ref, *refs):
    for copy in send_out(info, packed_ref, refs[:-1], "xy", refs[-1]):
        copy.wait()


def split(info, packed):
    _, rows, part = packed.shape
    return pl.pallas_call(
        split_kernel,
        in_specs=[SCALARS, pl.BlockSpec()],
        out_specs=[ANY] * 4,
        out_shape=sent_shapes(rows, part, "xy"),
        scratch_shapes=[pltpu.SemaphoreType.DMA((8,))],
        compiler_params=params(),
        cost_estimate=cost(0, 4 * BLOCKS * rows * part),
    )(info, packed)


def sum_over(value, axis, count):
    if count & (count - 1):
        return lax.psum(value, axis)
    step = 1
    while step < count:
        value = value + lax.ppermute(value, axis, [(i, i ^ step) for i in range(count)])
        step *= 2
    return value


def add_low(kept, came):
    return (kept.astype(jnp.float32) + came.astype(jnp.float32)).astype(low_type)


def scatter_first(outs):
    if len(outs) == 1:
        return ()
    return lax.ppermute(outs[1], "x", PAIR), lax.ppermute(outs[3], "y", PAIR)


def scatter_sums(outs, came, last):
    if len(outs) == 1:
        return ()
    came = lax.optimization_barrier((*came, *last))
    return add_low(outs[0][1], came[0][1]), add_low(outs[2][1], came[1][1])


def scatter_second(sums):
    if len(sums) == 0:
        return ()
    return lax.ppermute(sums[0], "y", PAIR), lax.ppermute(sums[1], "x", PAIR)


def sum_over(value, axis, count):
    if count & (count - 1):
        return lax.psum(value, axis)
    step = 1
    while step < count:
        value = value + lax.ppermute(value, axis, [(i, i ^ step) for i in range(count)])
        step *= 2
    return value


def add_low(kept, came):
    return (kept.astype(jnp.float32) + came.astype(jnp.float32)).astype(low_type)


def scatter_first(outs):
    if len(outs) == 1:
        return ()
    return lax.ppermute(outs[1], "x", PAIR), lax.ppermute(outs[3], "y", PAIR)


def scatter_sums(outs, came, last):
    if len(outs) == 1:
        return ()
    came = lax.optimization_barrier((*came, *last))
    return add_low(outs[0][1], came[0][1]), add_low(outs[2][1], came[1][1])


def scatter_second(sums):
    if len(sums) == 0:
        return ()
    return lax.ppermute(sums[0], "y", PAIR), lax.ppermute(sums[1], "x", PAIR)


def scatter_mine(outs, first, second, last, sizes):
    ny, nx, nz = sizes
    if len(outs) == 1:
        packed = outs[0]
        total = packed.shape[1]
        split = packed.transpose(1, 0, 2).reshape(total, ny * nx, -1).transpose(1, 0, 2)
        return lax.psum_scatter(split, ("y", "x"), scatter_dimension=0, tiled=True)[0]
    second = lax.optimization_barrier((*second, *last))
    one = add_low(add_low(outs[0][0], first[0][0]), second[0])
    two = add_low(add_low(outs[2][0], first[1][0]), second[1])
    return jnp.concatenate([one, two])


def merge_kernel(*refs):
    parts, out = refs[:6], refs[6]
    cut = out.shape[0] // 2
    for i in range(2):
        kept, came, second = (ref[...].astype(jnp.float32) for ref in parts[3 * i : 3 * i + 3])
        out[i * cut : (i + 1) * cut, :] = (kept[0] + came[0] + second).astype(low_type)


def merge(outs, first, second):
    cut, part = second[0].shape
    half = pl.BlockSpec((1, cut, part), lambda i: (0, 0, 0))
    whole = pl.BlockSpec((cut, part), lambda i: (0, 0))
    return pl.pallas_call(
        merge_kernel,
        grid=(1,),
        in_specs=[half, half, whole] * 2,
        out_specs=pl.BlockSpec((2 * cut, part), lambda i: (0, 0)),
        out_shape=shape((2 * cut, part)),
        compiler_params=params(),
        cost_estimate=cost(0, 16 * cut * part),
    )(outs[0], first[0], second[0], outs[2], first[1], second[1])


def scatter_mine(outs, first, second, last, sizes):
    ny, nx, nz = sizes
    if len(outs) == 1:
        packed = outs[0]
        total = packed.shape[1]
        split = packed.transpose(1, 0, 2).reshape(total, ny * nx, -1).transpose(1, 0, 2)
        return lax.psum_scatter(split, ("y", "x"), scatter_dimension=0, tiled=True)[0]
    return merge(outs, first, lax.optimization_barrier((*second, *last))[: len(second)])


def scatter_rows(mine):
    return lax.psum_scatter(mine, "z", scatter_dimension=0, tiled=True)


def spread(total, sizes):
    if sizes[0] * sizes[1] == BLOCKS:
        mine = [
            total,
            lax.ppermute(total, "x", PAIR),
            lax.ppermute(total, "y", PAIR),
            lax.ppermute(total, ("y", "x"), [(i, 3 - i) for i in range(4)]),
        ]
        return mine, [swap_core(value) for value in mine]
    everyone = jnp.moveaxis(lax.all_gather(total, ("y", "x"), axis=0), 0, -2)
    everyone = jnp.moveaxis(everyone.reshape(total.shape[:2] + (BLOCKS, -1)), -2, 0)
    place = lax.axis_index("y") * sizes[1] + lax.axis_index("x")
    mine = [
        lax.dynamic_index_in_dim(everyone, (place % BLOCKS) ^ i, 0, False) for i in range(BLOCKS)
    ]
    return mine, [swap_core(value) for value in mine]


def gather_all(total, sizes):
    everyone = lax.all_gather(total, ("core", "y", "x"), axis=0)
    count = sizes[0] * sizes[1]
    if count == BLOCKS:
        return (everyone,)
    both = jnp.moveaxis(everyone.reshape((2, count) + total.shape), 1, -2)
    both = jnp.moveaxis(both.reshape((2,) + total.shape[:2] + (BLOCKS, -1)), -2, 1)
    return (both.reshape((2 * BLOCKS,) + both.shape[2:]),)


def turn_heads(ref, value, cosine, sine, start):
    for h in range(value.shape[0] // HEAD_WIDTH):
        former = value[h * HEAD_WIDTH : h * HEAD_WIDTH + TURN]
        latter = value[h * HEAD_WIDTH + TURN : (h + 1) * HEAD_WIDTH]
        at = start + h * HEAD_WIDTH
        ref[at : at + TURN, :] = (former * cosine - latter * sine).astype(ref.dtype)
        ref[at + TURN : at + HEAD_WIDTH, :] = (latter * cosine + former * sine).astype(ref.dtype)


def project_kernel(mine_ref, other_ref, gain_ref, w_ref, cos_ref, sin_ref, normed_ref, q_ref, kv_ref):
    rows = mine_ref.shape[0]
    hk, part = HALF_KEY, w_ref.shape[2]
    for i, ref in enumerate((mine_ref, other_ref)):
        value = ref[...].astype(jnp.float32)
        normed = (value * norm_scale(value) * gain_ref[...]).astype(low_type)
        at = slice(i * rows, (i + 1) * rows)
        normed_ref[:, at] = normed.T
    weights = [w_ref[0].T, w_ref[1].T, w_ref[2].T[:hk]]
    for i in range(2):
        at = slice(i * rows, (i + 1) * rows)
        normed = normed_ref[:, at]
        cosine, sine = cos_ref[:, at], sin_ref[:, at]
        first = dot(weights[0], normed)
        turn_heads(q_ref.at[:, at], first, cosine, sine, 0)
        second = dot(weights[1], normed)
        turn_heads(q_ref.at[:, at], second[: part - hk], cosine, sine, part)
        turn_heads(kv_ref.at[0, :, at], second[part - hk :], cosine, sine, 0)
        kv_ref[1, :, at] = dot(weights[2], normed).astype(low_type)


def project(mine, other, gain, weights, cosine, sine):
    rows, width = mine.shape
    return pl.pallas_call(
        project_kernel,
        in_specs=[pl.BlockSpec()] * 6,
        out_specs=[pl.BlockSpec()] * 3,
        out_shape=[
            shape((width, 2 * rows)), shape((HALF_QUERY, 2 * rows)), shape((2, HALF_KEY, 2 * rows))
        ],
        compiler_params=params(),
        cost_estimate=cost(4 * rows * width * 960, 14 << 20),
    )(mine, other, gain, weights, cosine, sine)


def tile_mask(first, place0, key0, size, causal):
    key_place = key0 + lax.broadcasted_iota(jnp.int32, (size, size), 0)
    allowed = key_place >= first
    if causal:
        place = place0 + lax.broadcasted_iota(jnp.int32, (size, size), 1)
        allowed = allowed & (key_place <= place)
    return jnp.concatenate([allowed] * GROUP, axis=1)


def heads_of(ref):
    return jnp.concatenate(
        [ref[r * HEAD_WIDTH : (r + 1) * HEAD_WIDTH, :] for r in range(GROUP)], axis=1
    )


def over_tiles(info, size, rows, turn):
    per = rows // size
    half = pl.program_id(2)
    own = info[3] * per
    hi = own + half
    lo = info[4 + pl.program_id(0) * per + half]

    def columns(b):
        return pl.ds(pl.multiple_of(lax.rem(b, per) * size, size), size)

    def earlier(b, _):
        turn(hi, b, lax.div(b, per), columns(b))
        return 0

    def here(b, _):
        turn(hi, b, None, columns(b))
        return 0

    lax.fori_loop(lo, own, earlier, 0)
    lax.fori_loop(jnp.maximum(lo, own), hi + 1, here, 0)


def attend_kernel(info, q_ref, kv_ref, past_ref, first_ref, o_ref, total_ref, peak_s, sum_s, acc_s):
    size, rows = q_ref.shape[1], kv_ref.shape[2]
    q = heads_of(q_ref)
    peak_s[...] = jnp.full(peak_s.shape, lowest_peak, jnp.float32)
    sum_s[...] = jnp.zeros(sum_s.shape, jnp.float32)
    acc_s[...] = jnp.zeros(acc_s.shape, jnp.float32)

    def turn(hi, b, past, at):
        k = kv_ref[0, :, at] if past is None else past_ref[past, 0, :, at]
        v = kv_ref[1, :, at] if past is None else past_ref[past, 1, :, at]
        allowed = tile_mask(first_ref[0], hi * size, b * size, size, past is None)
        scores = dot(k, q, (0, 0)) * (SCORE_SCALE * LOG2E)
        scores = jnp.where(allowed, scores, masked_score)
        peak = peak_s[...]
        fresh = jnp.maximum(peak, jnp.max(scores, axis=0, keepdims=True))
        shrink = jnp.exp2(peak - fresh)
        terms = jnp.exp2(scores - fresh)
        peak_s[...] = fresh
        sum_s[...] = sum_s[...] * shrink + jnp.sum(terms, axis=0, keepdims=True)
        acc_s[...] = acc_s[...] * shrink + dot(v, terms.astype(low_type))

    over_tiles(info, size, rows, turn)
    total = sum_s[...]
    mixed = acc_s[...] / total
    log_total = peak_s[...] + jnp.log2(total)
    for r in range(GROUP):
        o_ref[r * HEAD_WIDTH : (r + 1) * HEAD_WIDTH, :] = mixed[:, r * size : (r + 1) * size]
        total_ref[0, r : r + 1, :] = log_total[:, r * size : (r + 1) * size]


def attend_back_kernel(
    info, q_ref, kv_ref, past_ref, g_ref, first_ref, total_ref, delta_ref, dq_ref, dkv_ref, dpast_ref,
    acc_s, past_s,
):
    size, rows = q_ref.shape[1], kv_ref.shape[2]
    q = heads_of(q_ref)
    g = heads_of(g_ref)
    total = jnp.concatenate([total_ref[0, r : r + 1, :] for r in range(GROUP)], axis=1)
    delta = jnp.concatenate([delta_ref[0, r : r + 1, :] for r in range(GROUP)], axis=1)
    acc_s[...] = jnp.zeros(acc_s.shape, jnp.float32)

    @pl.when(pl.program_id(2) == 0)
    def _():
        dkv_ref[...] = jnp.zeros(dkv_ref.shape, jnp.float32)
        past_s[...] = jnp.zeros(past_s.shape, jnp.float32)

    def turn(hi, b, past, at):
        k = kv_ref[0, :, at] if past is None else past_ref[past, 0, :, at]
        v = kv_ref[1, :, at] if past is None else past_ref[past, 1, :, at]
        allowed = tile_mask(first_ref[0], hi * size, b * size, size, past is None)
        scores = dot(k, q, (0, 0)) * (SCORE_SCALE * LOG2E)
        weights = jnp.exp2(jnp.where(allowed, scores - total, masked_score))
        grad_weights = dot(v, g, (0, 0))
        grad_scores = (weights * (grad_weights - delta) * SCORE_SCALE).astype(low_type)
        dk = dot(q, grad_scores, (1, 1))
        dv = dot(g, weights.astype(low_type), (1, 1))
        if past is None:
            dkv_ref[0, :, at] += dk
            dkv_ref[1, :, at] += dv
        else:
            past_s[past, 0, :, at] += dk
            past_s[past, 1, :, at] += dv
        acc_s[...] += dot(k, grad_scores)

    over_tiles(info, size, rows, turn)
    acc = acc_s[...]
    for r in range(GROUP):
        dq_ref[r * HEAD_WIDTH : (r + 1) * HEAD_WIDTH, :] = acc[:, r * size : (r + 1) * size]

    @pl.when(pl.program_id(2) == pl.num_programs(2) - 1)
    def _():
        dpast_ref[...] = past_s[...].astype(low_type)


def attention_specs(parts, rows, size):
    per = rows // size
    wide = pl.BlockSpec((GROUP * HEAD_WIDTH, size), lambda s, g, h: (g, s * per + h))
    own = pl.BlockSpec((2, HEAD_WIDTH, rows), lambda s, g, h: (0, g, s))
    past = pl.BlockSpec((parts, 2, HEAD_WIDTH, rows), lambda s, g, h: (0, 0, g, s))
    first = pl.BlockSpec((1, 1, size), lambda s, g, h: (s, 0, h))
    stat = pl.BlockSpec((1, 8, size), lambda s, g, h: (g, 0, s * per + h))
    return (2, GROUPS, per), wide, own, past, first, stat


def attend(info, query, keyvalue, past, first, size, after):
    both = keyvalue.shape[2]
    rows = both // 2
    grid, wide, own, past_spec, first_spec, stat = attention_specs(past.shape[0], rows, size)
    pairs = 2 * rows * rows * 3 // 2
    return pl.pallas_call(
        ignoring(attend_kernel, 5, after),
        grid=grid,
        in_specs=[SCALARS, wide, own, past_spec, first_spec] + [ANY] * len(after),
        out_specs=[wide, stat],
        out_shape=[shape(query.shape, jnp.float32), shape((GROUPS, 8, both), jnp.float32)],
        scratch_shapes=[
            pltpu.VMEM((1, GROUP * size), jnp.float32),
            pltpu.VMEM((1, GROUP * size), jnp.float32),
            pltpu.VMEM((HEAD_WIDTH, GROUP * size), jnp.float32),
        ],
        compiler_params=params(),
        cost_estimate=cost(pairs * 9 * 64 * 4 * 5, 8 << 20, pairs * 9),
    )(info, query, keyvalue, past, first, *after)


def attend_back(info, query, keyvalue, past, grad, first, log_total, delta, size, after):
    both = keyvalue.shape[2]
    rows = both // 2
    grid, wide, own, past_spec, first_spec, stat = attention_specs(past.shape[0], rows, size)
    pairs = 2 * rows * rows * 3 // 2
    return pl.pallas_call(
        ignoring(attend_back_kernel, 8, after),
        grid=grid,
        in_specs=[SCALARS, wide, own, past_spec, wide, first_spec, stat, stat] + [ANY] * len(after),
        out_specs=[wide, own, past_spec],
        out_shape=[
            shape(query.shape, jnp.float32), shape(keyvalue.shape, jnp.float32), shape(past.shape)
        ],
        scratch_shapes=[
            pltpu.VMEM((HEAD_WIDTH, GROUP * size), jnp.float32),
            pltpu.VMEM((past.shape[0], 2, HEAD_WIDTH, rows), jnp.float32),
        ],
        compiler_params=params(),
        cost_estimate=cost(pairs * 9 * 64 * 10 * 3, 12 << 20, pairs * 9),
    )(info, query, keyvalue, past, grad, first, log_total, delta, *after)


def place_out(core, mine_ref, other_ref, out_ref):
    cut, part = HALF_KEY, mine_ref.shape[2]
    mine = jnp.concatenate([mine_ref[0][:, cut:], mine_ref[1]], axis=1)
    other = jnp.concatenate([other_ref[0][:, cut:], other_ref[1]], axis=1)
    out_ref[...] = jnp.where(
        core == 0,
        jnp.concatenate([mine, other], axis=1),
        jnp.concatenate([other, mine], axis=1),
    )


def out_kernel(
    info, mine_ref, came_ref, w_ref, w_other_ref, tokens_ref, gain_ref, middle_ref, normed_ref,
    turned_ref, rows_ref, w_s,
):
    place_out(info[0], w_ref, w_other_ref, w_s)
    hq = HALF_QUERY
    mine = w_s[pl.ds(pl.multiple_of(info[0] * hq, hq), hq), :]
    other = w_s[pl.ds(pl.multiple_of((1 - info[0]) * hq, hq), hq), :]
    rows_ref[...] = mine
    middle = (
        tokens_ref[...].astype(jnp.float32)
        + dot(mine_ref[...].astype(low_type).T, mine)
        + dot(came_ref[...].T, other)
    )
    middle_ref[...] = middle
    normed = (middle * norm_scale(middle) * gain_ref[...]).astype(low_type)
    normed_ref[...] = normed
    turned_ref[...] = normed.T


def project_out(info, attended, came, weights, weights_other, tokens, gain, after):
    rows, width = tokens.shape
    hq = HALF_QUERY
    part = weights.shape[2]
    return pl.pallas_call(
        ignoring(out_kernel, 7, after),
        grid=(1,),
        in_specs=[
            SCALARS,
            pl.BlockSpec((hq, rows), lambda i: (0, 0)),
            pl.BlockSpec((hq, rows), lambda i: (0, 0)),
            pl.BlockSpec((2, width, part), lambda i: (1, 0, 0)),
            pl.BlockSpec((2, width, part), lambda i: (0, 0, 0)),
            pl.BlockSpec((rows, width), lambda i: (0, 0)),
            pl.BlockSpec((1, width), lambda i: (0, 0)),
        ]
        + [ANY] * len(after),
        out_specs=[
            pl.BlockSpec((rows, width), lambda i: (0, 0)),
            pl.BlockSpec((rows, width), lambda i: (0, 0)),
            pl.BlockSpec((width, rows), lambda i: (0, 0)),
            pl.BlockSpec((hq, width), lambda i: (0, 0)),
        ],
        out_shape=[
            shape((rows, width), jnp.float32), shape((rows, width)), shape((width, rows)),
            shape((hq, width)),
        ],
        scratch_shapes=[pltpu.VMEM((width, width), low_type)],
        compiler_params=params(),
        cost_estimate=cost(2 * rows * width * width, 16 << 20),
    )(info, attended, came, weights, weights_other, tokens, gain, *after)


def ffn_kernel(tuned, ways, info, *refs):
    xs, cs, xts, cts, w_ref, refs = refs[0:2], refs[2:4], refs[4:6], refs[6:8], refs[8], refs[9:]
    stacks = [()] * CHUNKS
    if tuned:
        stacks, refs = [refs[4 * j : 4 * j + 4] for j in range(CHUNKS)], refs[4 * CHUNKS :]
    totals, outs, scratch = refs[:4], list(refs[4:-17]), refs[-17:]
    (
        x_s, c_s, xt_s, ct_s, result_s, grad_s, result_low, grad_low, land_s, gate_s, up_s, down_s,
        hidden_s, dgate_s, dup_s, packed_s, sems,
    ) = scratch
    rows = xs[0].shape[0]
    size = FFN_ROWS
    block, part = gate_s.shape[1], packed_s.shape[3]
    width = gate_s.shape[0]
    lane, turned = block // BLOCKS, width // BLOCKS

    def begin(source, target, sem):
        copy = pltpu.make_async_copy(source, target, sem)
        copy.start()
        return copy

    def weights_in(j):
        target = land_s.at[j % 2]
        if tuned:
            return place_pieces(info, BLOCKS, w_ref.at[j], stacks[j], True, target, sems.at[j])
        return [begin(w_ref.at[j], target, sems.at[j, 0])]

    coming = weights_in(0)
    there = [begin(ref, x_s.at[i * rows : (i + 1) * rows], sems.at[3, i]) for i, ref in enumerate(xs)]
    there += [begin(ref, c_s.at[i * rows : (i + 1) * rows], sems.at[3, 2 + i]) for i, ref in enumerate(cs)]
    across = [begin(ref, xt_s.at[:, i * rows : (i + 1) * rows], sems.at[3, 4 + i]) for i, ref in enumerate(xts)]
    across += [begin(ref, ct_s.at[:, i * rows : (i + 1) * rows], sems.at[3, 6 + i]) for i, ref in enumerate(cts)]
    going = [[] for _ in range(CHUNKS + 1)]
    for j in range(CHUNKS):
        for copy in coming:
            copy.wait()
        land = land_s.at[j % 2]
        gate_s[:, :part] = land[0]
        gate_s[:, part:] = land[1, :, : block - part]
        up_s[:, : 2 * part - block] = land[1, :, block - part :]
        up_s[:, 2 * part - block :] = land[2, :, : 2 * block - 2 * part]
        for q in range(BLOCKS):
            for z in range(BLOCKS):
                column = 2 * block + q * lane
                b, at = column // part, column % part
                down_s[q * turned : (q + 1) * turned, z * lane : (z + 1) * lane] = land[
                    b, z * turned : (z + 1) * turned, at : at + lane
                ]
        coming = weights_in(j + 1) if j + 1 < CHUNKS else []
        if j == 0:
            for copy in there:
                copy.wait()

        def forward(t, _, j=j):
            at = pl.ds(pl.multiple_of(t * size, size), size)
            x, c = x_s[at, :], c_s[at, :]
            gate = dot(x, gate_s[...])
            upward = dot(x, up_s[...])
            grad_hidden = dot(c, down_s[...])
            sigmoid = 1.0 / (1.0 + jnp.exp(-gate))
            silu = gate * sigmoid
            hidden = (silu * upward).astype(low_type)
            grad_gate = grad_hidden * upward * sigmoid * (1.0 + gate * (1.0 - sigmoid))
            grad_gate = grad_gate.astype(low_type)
            grad_up = (grad_hidden * silu).astype(low_type)
            hidden_s[at, :], dgate_s[at, :], dup_s[at, :] = hidden, grad_gate, grad_up
            result = dot(hidden, down_s[...], (1, 1))
            grad = dot(grad_gate, gate_s[...], (1, 1)) + dot(grad_up, up_s[...], (1, 1))
            if j > 0:
                result, grad = result + result_s[at, :], grad + grad_s[at, :]
            result_s[at, :], grad_s[at, :] = result, grad
            return 0

        lax.fori_loop(0, 2 * rows // size, forward, 0)
        if j == 0:
            for copy in across:
                copy.wait()
        if j == CHUNKS - 1:
            result_low[...] = result_s[rows:, :].astype(low_type)
            grad_low[...] = grad_s[rows:, :].astype(low_type)
            sources = (result_s.at[:rows], grad_s.at[:rows], result_low, grad_low)
            going[CHUNKS] = [begin(s, t, sems.at[3, 8 + i]) for i, (s, t) in enumerate(zip(sources, totals))]
        if j >= 2:
            for copy in going[j - 2]:
                copy.wait()
        packed = packed_s.at[j % 2]

        def backward(q, _, packed=packed):
            at = pl.ds(pl.multiple_of(q * turned, turned), turned)
            xt = xt_s[at, :]
            gate = dot(xt, dgate_s[...]).astype(low_type)
            up = dot(xt, dup_s[...]).astype(low_type)
            down = dot(ct_s[at, :], hidden_s[...]).astype(low_type)
            packed[0, at, :] = gate[:, :part]
            packed[1, at, : block - part] = gate[:, part:]
            packed[1, at, block - part :] = up[:, : 2 * part - block]
            packed[2, at, : 2 * block - 2 * part] = up[:, 2 * part - block :]
            column = 2 * block + q * lane
            b = lax.div(column, part)
            place = pl.ds(pl.multiple_of(lax.rem(column, part), lane), lane)
            for z in range(BLOCKS):
                packed[b, z * turned : (z + 1) * turned, place] = down[:, z * lane : (z + 1) * lane]
            return 0

        lax.fori_loop(0, BLOCKS, backward, 0)
        count = 4 if ways[j] == "xy" else 1
        going[j] = send_out(info, packed, outs[:count], ways[j], sems.at[4 + j])
        outs = outs[count:]
    for copy in going[CHUNKS - 2] + going[CHUNKS - 1] + going[CHUNKS]:
        copy.wait()


def feed_forward(info, xs, cs, xts, cts, weights, pieces, ways, tuned, after):
    rows, width = xs[0].shape
    part = weights.shape[2] // BLOCKS if tuned else weights.shape[3]
    block = BLOCKS * part // 3
    sent = [sent_shapes(width, part, way) for way in ways]
    given = sum((list(p) for p in pieces), [])
    totals = [shape((rows, width), jnp.float32)] * 2 + [shape((rows, width))] * 2

    def kernel(info, *refs):
        ffn_kernel(tuned, ways, info, *refs)

    whole = pltpu.VMEM((2 * rows, width), low_type)
    turned = pltpu.VMEM((width, 2 * rows), low_type)
    total = pltpu.VMEM((2 * rows, width), jnp.float32)
    low = pltpu.VMEM((rows, width), low_type)
    packed = pltpu.VMEM((2, BLOCKS, width, part), low_type)
    matrix = pltpu.VMEM((width, block), low_type)
    tokens = pltpu.VMEM((2 * rows, block), low_type)
    outs = pl.pallas_call(
        ignoring(kernel, 10 + len(given), after),
        in_specs=[SCALARS] + [ANY] * (9 + len(given) + len(after)),
        out_specs=[ANY] * (4 + sum(len(s) for s in sent)),
        out_shape=totals + sum(sent, []),
        scratch_shapes=[
            whole, whole, turned, turned, total, total, low, low, packed, matrix, matrix, matrix,
            tokens, tokens, tokens, packed, pltpu.SemaphoreType.DMA((4 + CHUNKS, 16)),
        ],
        compiler_params=params(),
        cost_estimate=cost(
            36 * rows * width * block * CHUNKS, 40 << 20, 2 * rows * block * CHUNKS
        ),
    )(info, *xs, *cs, *xts, *cts, weights, *given, *after)
    totals, outs = outs[:4], outs[4:]
    groups = []
    for shapes in sent:
        groups.append(outs[: len(shapes)])
        outs = outs[len(shapes) :]
    return totals, groups


def branch_kernel(g_ref, g_other_ref, w_ref, attended_ref, grad_ref, delta_ref, rows_ref):
    rows = g_ref.shape[0]
    delta_ref[...] = jnp.zeros(delta_ref.shape, jnp.float32)
    for i, ref in enumerate((g_ref, g_other_ref)):
        at = slice(i * rows, (i + 1) * rows)
        grad = dot(w_ref[...], ref[...], (1, 1)).astype(low_type)
        grad_ref[:, at] = grad
        product = grad.astype(jnp.float32) * attended_ref[:, at]
        for h in range(GROUP * GROUPS):
            delta_ref[h // GROUP, h % GROUP : h % GROUP + 1, at] = jnp.sum(
                product[h * HEAD_WIDTH : (h + 1) * HEAD_WIDTH], axis=0, keepdims=True
            )
    attended = attended_ref[...].astype(low_type)
    rows_ref[...] = (
        dot(attended[:, :rows], g_ref[...]) + dot(attended[:, rows:], g_other_ref[...])
    ).astype(low_type)


def branch(grad, grad_other, out_rows, attended, after):
    rows, width = grad.shape
    return pl.pallas_call(
        ignoring(branch_kernel, 4, after),
        in_specs=[pl.BlockSpec()] * 4 + [ANY] * len(after),
        out_specs=[pl.BlockSpec()] * 3,
        out_shape=[
            shape(attended.shape), shape((GROUPS, 8, 2 * rows), jnp.float32),
            shape((HALF_QUERY, width)),
        ],
        compiler_params=params(),
        cost_estimate=cost(8 * rows * width * HALF_QUERY, 12 << 20),
    )(grad, grad_other, out_rows, attended, *after)


def attn_grad_kernel(
    info, dq_ref, dkv_ref, came_ref, cos_ref, sin_ref, normed_ref, mine_ref, other_ref, d_ref, *refs
):
    outs, packed_s, sems = refs[:-2], refs[-2], refs[-1]
    hq, hk = HALF_QUERY, HALF_KEY
    part = packed_s.shape[2]
    cosine, sine = cos_ref[...], -sin_ref[...]
    turn_heads(d_ref, dq_ref[...], cosine, sine, 0)
    whole = dkv_ref[...] + came_ref[...].astype(jnp.float32)
    turn_heads(d_ref, whole[0], cosine, sine, hq)
    d_ref[hq + hk :, :] = whole[1].astype(low_type)
    normed = normed_ref[...]
    packed_s[0] = dot(normed, d_ref[:part, :], (1, 1)).astype(low_type)
    packed_s[1] = dot(normed, d_ref[part : 2 * part, :], (1, 1)).astype(low_type)
    last = dot(normed, d_ref[2 * part :, :], (1, 1)).astype(low_type)
    mine, other = mine_ref[...], other_ref[...]
    low = info[0] == 0
    out = jnp.concatenate(
        [jnp.where(low, mine, other), jnp.where(low, other, mine)], axis=0
    )
    packed_s[2] = jnp.concatenate([last, out[:, : part - hk]], axis=1)
    packed_s[3] = out[:, part - hk :]
    for copy in send_out(info, packed_s, outs, "xy" if len(outs) > 1 else "whole", sems):
        copy.wait()


def attn_grads(info, grad_query, grad_kv, came, cosine, sine, normed, mine, other, after, tuned):
    width, both = normed.shape
    part = (2 * HALF_QUERY + 2 * HALF_KEY) // BLOCKS
    sent = sent_shapes(width, part, "xy" if tuned else "whole")
    return pl.pallas_call(
        ignoring(attn_grad_kernel, 9, after),
        in_specs=[SCALARS] + [pl.BlockSpec()] * 8 + [ANY] * len(after),
        out_specs=[pl.BlockSpec()] + [ANY] * len(sent),
        out_shape=[shape((HALF_QUERY + 2 * HALF_KEY, both))] + sent,
        scratch_shapes=[
            pltpu.VMEM((BLOCKS, width, part), low_type),
            pltpu.SemaphoreType.DMA((8,)),
        ],
        compiler_params=params(),
        cost_estimate=cost(2 * both * width * 960, 20 << 20),
    )(info, grad_query, grad_kv, came, cosine, sine, normed, mine, other, *after)


def normed_grad_kernel(d_ref, w_ref, mine_ref, other_ref):
    rows = mine_ref.shape[0]
    hk, part = HALF_KEY, w_ref.shape[2]
    for i, ref in enumerate((other_ref, mine_ref)):
        at = slice((1 - i) * rows, (2 - i) * rows)
        d = d_ref[:, at].T
        value = dot(d[:, :part], w_ref[0], (1, 1)) + dot(d[:, part : 2 * part], w_ref[1], (1, 1))
        value = value + dot(d[:, 2 * part :], w_ref[2][:, :hk], (1, 1))
        ref[...] = value.astype(ref.dtype)


def normed_grad(d, weights, after):
    width = weights.shape[1]
    rows = d.shape[1] // 2
    return pl.pallas_call(
        ignoring(normed_grad_kernel, 2, after),
        in_specs=[pl.BlockSpec()] * 2 + [ANY] * len(after),
        out_specs=[pl.BlockSpec()] * 2,
        out_shape=[shape((rows, width), jnp.float32), shape((rows, width))],
        compiler_params=params(),
        cost_estimate=cost(4 * rows * width * 960, 9 << 20),
    )(d, weights, *after)


def halves(info, refs, chunk):
    mine, other = refs[:BLOCKS], refs[BLOCKS:]
    place = lax.rem(info[1], BLOCKS)

    def ordered(values):
        for bit in (1, 2):
            flip = lax.rem(lax.div(place, bit), 2) == 1
            values = [jnp.where(flip, values[b ^ bit], values[b]) for b in range(BLOCKS)]
        return jnp.concatenate(values, axis=1)

    mine = ordered([ref[chunk] for ref in mine])
    other = ordered([ref[chunk] for ref in other])
    low = info[0] == 0
    return jnp.where(low, mine, other), jnp.where(low, other, mine)


def unpack_attn_kernel(info, *refs):
    refs, outs = refs[: 2 * BLOCKS], refs[2 * BLOCKS :]
    both = [value.astype(jnp.float32) for value in halves(info, refs, 0)]
    start = 0
    for ref, size in zip(outs, (HALF_QUERY, HALF_KEY, HALF_KEY, HALF_QUERY)):
        ref[...] = jnp.concatenate([v[:, start : start + size] for v in both], axis=1)
        start += size


def unpack_attn(info, mine, other):
    rows = mine[0].shape[1]
    return pl.pallas_call(
        unpack_attn_kernel,
        in_specs=[SCALARS] + [pl.BlockSpec()] * (2 * BLOCKS),
        out_specs=[pl.BlockSpec()] * 4,
        out_shape=[
            shape((rows, 2 * n), jnp.float32) for n in (HALF_QUERY, HALF_KEY, HALF_KEY, HALF_QUERY)
        ],
        compiler_params=params(),
        cost_estimate=cost(0, 6 << 20),
    )(info, *mine, *other)


def unpack_ffn_kernel(all_ref, gate_ref, up_ref, down_ref):
    part = all_ref.shape[3]
    block = BLOCKS * part // 3
    lane = block // BLOCKS
    half = CHUNKS * lane
    for h in range(2):
        for c in range(CHUNKS):
            value = jnp.concatenate([all_ref[h * BLOCKS + b, c] for b in range(BLOCKS)], axis=1)
            value = value.astype(jnp.float32)
            for z in range(BLOCKS):
                at = z * 2 * half + h * half + c * lane
                gate_ref[:, at : at + lane] = value[:, z * lane : (z + 1) * lane]
                up_ref[:, at : at + lane] = value[:, block + z * lane : block + (z + 1) * lane]
            down = jnp.concatenate(
                [value[:, 2 * block + q * lane : 2 * block + (q + 1) * lane] for q in range(BLOCKS)],
                axis=0,
            )
            down_ref[h * half + c * lane : h * half + (c + 1) * lane, :] = down.T


def unpack_ffn(info, everyone):
    rows, part = everyone.shape[2:]
    lane = part // 3
    return pl.pallas_call(
        unpack_ffn_kernel,
        in_specs=[pl.BlockSpec()],
        out_specs=[pl.BlockSpec()] * 3,
        out_shape=[
            shape((rows, 2 * BLOCKS * CHUNKS * lane), jnp.float32),
            shape((rows, 2 * BLOCKS * CHUNKS * lane), jnp.float32),
            shape((2 * CHUNKS * lane, BLOCKS * rows), jnp.float32),
        ],
        compiler_params=params(),
        cost_estimate=cost(0, 16 << 20),
    )(everyone)


def shards(sizes, *arrays):
    (
        tokens, segments, cotangent, attn_gain, w_query, key_matrix, value_matrix, w_out, ffn_gain,
        w_gate, w_up, w_down,
    ) = arrays
    ny, nx, nz = sizes
    tuned = (ny, nx) == (2, 2)
    core, xi = lax.axis_index("core"), lax.axis_index("x")
    place = lax.axis_index("y") * nx + xi
    info = jnp.stack([core, place, lax.axis_index("z"), xi]).astype(jnp.int32)
    tokens, cotangent, ids = tokens[0], cotangent[0], segments[0]
    rows, width = tokens.shape
    own_rows = w_query.shape[0]

    gains = jnp.stack([attn_gain, ffn_gain])
    attn_own, *attn_piece = pack_attn(
        info, (w_query, key_matrix, value_matrix, w_out), gains, tuned
    )
    ffn_own, *ffn_piece = pack_ffn(info, w_gate, w_up, w_down, tuned)
    ids, tokens_sent, cotangent_sent, _ = lax.optimization_barrier((ids, tokens, cotangent, ffn_own))
    all_ids = lax.all_gather(ids, "x", axis=0, tiled=True)
    first = jnp.sum((all_ids[:, None] < ids[None, :]).astype(jnp.int32), axis=0)
    firsts = jnp.concatenate([first[None], swap_core(first[None])])
    token_place = xi * rows + jnp.arange(rows, dtype=jnp.int32)
    positions = (token_place[None] - firsts).reshape(-1)
    angles = inverse_freq()[:, None] * positions.astype(jnp.float32)[None, :]
    cosine, sine = jnp.cos(angles), jnp.sin(angles)
    size = rows // 2
    starts = firsts.reshape(2, rows // size, size)[:, :, 0] // size
    info = jnp.concatenate([info, starts.reshape(-1)])
    firsts = firsts[:, None, :]

    tokens_other, cotangent_other = swap_core(tokens_sent), swap_core(cotangent_sent)
    cotangent_turned = cotangent_sent.T

    if tuned:
        cut = own_rows // 2
        slots = travel_z(attn_piece[0], sizes)
        stack = jnp.stack([s[:own_rows] for s in slots])
        parts = [lax.all_gather(behind(piece, (stack,)), "z", axis=0) for piece in ffn_piece]
        ffn_stacks = list(pick(info, parts[:1], ((0, 0, 0, own_rows, 0),), own_rows))
        ffn_stacks += pick(
            info,
            parts,
            ((0, 0, own_rows, own_rows + cut, 0), (0, 1, 0, cut, cut), (1, 1, cut, cut + own_rows, 0)),
            own_rows,
        )
        stack = behind(stack, (cosine, firsts, tokens_other, cotangent_turned, cotangent_other))
        stacks = (
            stack,
            lax.ppermute(stack, "x", PAIR),
            lax.ppermute(stack, "y", PAIR),
            lax.ppermute(stack, ("y", "x"), [(i, 3 - i) for i in range(4)]),
        )
        weights = assemble(info, attn_own, stacks, nz, ffn_stacks[:1])
        ffn_weights = ffn_own
        gains = [gains.astype(low_type)] + [s[own_rows : own_rows + 2, :own_rows] for s in slots]
        gains = jnp.stack(gains[::-1] + gains[::-1])
        gains = lax.dynamic_slice_in_dim(gains, nz - 1 - lax.axis_index("z"), nz, 0)
        gains = gains.transpose(1, 0, 2).reshape(2, width)
    else:
        weights = gather_whole(attn_own)
        ffn_pieces = [()] * CHUNKS
        before_attend = before_out = ()
        ffn_weights = jnp.stack([gather_whole(ffn_own[c]) for c in range(CHUNKS)])
        gains = lax.all_gather(gains.astype(low_type), "z", axis=1, tiled=True)
    gain_one, gain_two = gains[:1].astype(jnp.float32), gains[1:].astype(jnp.float32)

    cs = (cotangent, cotangent_other)
    cts = (cotangent_turned, swap_core(cotangent_turned))

    normed, query, keyvalue = project(
        tokens, tokens_other, gain_one, weights, cosine, sine
    )
    weights_other = swap_core(behind(weights, (keyvalue,))[2:])
    if tuned:
        first_x, first_y = (lax.ppermute(ffn_stacks[0], axis, PAIR) for axis in ("x", "y"))
        past = lax.ppermute(behind(keyvalue, (first_x, first_y)), "x", [(0, 1)])[None]
        by_x = [first_x] + [lax.ppermute(s, "x", PAIR) for s in ffn_stacks[1:]]
        by_y = [first_y] + [lax.ppermute(s, "y", PAIR) for s in ffn_stacks[1:]]
        far = [
            lax.ppermute(by_x[0], "y", PAIR),
            lax.ppermute(by_x[1], "y", PAIR),
            lax.ppermute(by_y[2], "x", PAIR),
        ]
        ffn_pieces = list(zip(ffn_stacks, by_x, by_y, far))
        before_attend = ffn_stacks[1:]
        before_out = (by_x[1], by_y[1], far[0])
    else:
        past = lax.all_gather(keyvalue, "x", axis=0)
    attended, log_total = attend(info, query, keyvalue, past, firsts, size, before_attend)
    came = swap_core(attended[:, rows:].astype(low_type))
    middle, normed_two, normed_turned, out_rows = project_out(
        info, attended, came, weights, weights_other, tokens, gain_two, before_out
    )

    xs, xts = (normed_two, swap_core(normed_two)), (normed_turned, swap_core(normed_turned))
    sent, first, send, second, reduced = ([None] * (CHUNKS + 1) for _ in range(5))
    ways = ["xy", "xy", "z"] if tuned else ["whole"] * CHUNKS
    (result, grad_normed_two, result_other, grad_other), sent[:3] = feed_forward(
        info, xs, cs, xts, cts, ffn_weights, ffn_pieces, ways, tuned, ()
    )
    if tuned:
        rows_two = lax.psum_scatter(sent[2][0], "z", scatter_dimension=0, tiled=True)[0]
    first[0] = scatter_first(sent[0])

    grad_normed_two = grad_normed_two + swap_core(grad_other).astype(jnp.float32)
    result = result + swap_core(result_other).astype(jnp.float32)
    scale_two = norm_scale(middle)
    grad_gain_two = jnp.sum(grad_normed_two * middle * scale_two, axis=0)
    grad_middle = cotangent.astype(jnp.float32) + norm_back(
        grad_normed_two * gain_two, middle, scale_two
    )
    grad_branch = grad_middle.astype(low_type)
    output = (middle + result).astype(low_type)

    grad_other = swap_core(grad_branch)
    grad_attended, delta, grad_rows = branch(
        grad_branch, grad_other, out_rows, attended, ()
    )
    hq = HALF_QUERY
    mine = lax.dynamic_slice_in_dim(grad_rows, core * hq, hq, 1)
    other = swap_core(lax.dynamic_slice_in_dim(grad_rows, (1 - core) * hq, hq, 1))
    send[0] = scatter_sums(sent[0], first[0], (grad_attended,))
    second[0] = scatter_second(send[0])
    first[1] = scatter_first([behind(value, send[0]) for value in sent[1]])
    grad_query, grad_kv, grad_past = attend_back(
        info, query, keyvalue, past, grad_attended, firsts, log_total, delta, size,
        send[0],
    )
    if tuned:
        came = lax.ppermute(behind(grad_past[0], (*second[0], *first[1])), "x", [(1, 0)])
    else:
        came = lax.psum_scatter(grad_past, "x", scatter_dimension=0, tiled=True)[0]
    reduced[0] = scatter_mine(sent[0], first[0], second[0], (grad_past,), sizes)
    send[1] = scatter_sums(sent[1], first[1], (grad_past,))
    second[1] = scatter_second(send[1])
    grad_projected, *attn_sent = attn_grads(
        info, grad_query, grad_kv, came, cosine, sine, normed, mine, other,
        (*second[1], reduced[0]) if tuned else (), tuned,
    )
    normed_mine, normed_other = normed_grad(grad_projected, weights, ())
    grad_normed = normed_mine + swap_core(normed_other).astype(jnp.float32)
    inputs = tokens.astype(jnp.float32)
    scale_one = norm_scale(inputs)
    grad_gain_one = jnp.sum(grad_normed * inputs * scale_one, axis=0)
    grad_inputs = (
        grad_middle + norm_back(grad_normed * gain_one, inputs, scale_one)
    ).astype(low_type)

    gain_grads = jnp.stack([grad_gain_one, grad_gain_two])
    for axis, count in (("core", 2), ("x", nx), ("y", ny), ("z", nz)):
        gain_grads = sum_over(gain_grads, axis, count)
    gain_grads = lax.dynamic_slice_in_dim(gain_grads, lax.axis_index("z") * own_rows, own_rows, 1)

    sent[3], first[3] = attn_sent, scatter_first(attn_sent)
    last = (normed_mine,)
    send[3] = scatter_sums(sent[3], first[3], last)
    second[3] = scatter_second(send[3])
    reduced[1] = scatter_mine(sent[1], first[1], second[1], send[3][:1] or last, sizes)
    if tuned:
        sent[2] = split(info, behind(rows_two, (reduced[1],)))
        first[2] = scatter_first(sent[2])
        reduced[3] = scatter_mine(sent[3], first[3], second[3], sent[2][:1], sizes)
        last = (reduced[3],)
        send[2] = scatter_sums(sent[2], first[2], last)
        second[2] = scatter_second(send[2])
        reduced[2] = scatter_mine(sent[2], first[2], second[2], last, sizes)
    else:
        reduced[2] = scatter_rows(scatter_mine(sent[2], (), (), last, sizes))
        reduced[3] = scatter_mine(sent[3], (), (), last, sizes)
    attn_out = unpack_attn(info, *spread(scatter_rows(reduced[3])[None], sizes))
    ffn_total = jnp.stack([scatter_rows(reduced[0]), scatter_rows(reduced[1]), reduced[2]])
    grad_w_gate, grad_w_up, grad_w_down = unpack_ffn(info, *gather_all(ffn_total, sizes))
    return (
        output[None], grad_inputs[None], gain_grads[0], *attn_out, gain_grads[1], grad_w_gate,
        grad_w_up, grad_w_down,
    )


def solution(mesh):
    dp, ctx, fsdp = (mesh.shape[name] for name in ("dp", "ctx", "fsdp"))
    fine = Mesh(mesh.devices.reshape(dp // 2, 2, ctx, fsdp), ("y", "core", "x", "z"))
    sizes = (dp // 2, ctx, fsdp)
    wide = P(("y", "core", "z"), "x", None)
    matrix, vector = P("z", None), P("z")
    in_specs = (
        wide, P(("y", "core", "z"), "x"), wide, vector, matrix, matrix, matrix, matrix, vector,
        matrix, matrix, matrix,
    )
    out_specs = (
        wide, wide, vector, matrix, matrix, matrix, matrix, vector, matrix, matrix, matrix
    )

    def layer(*arrays):
        return shards(sizes, *arrays)

    return jax.shard_map(
        layer, mesh=fine, in_specs=in_specs, out_specs=out_specs, check_vma=False
    )
```

```python
import math

import jax
import jax.numpy as jnp
from jax import lax
from jax.experimental import pallas as pl
from jax.experimental.pallas import tpu as pltpu
from jax.sharding import Mesh
from jax.sharding import PartitionSpec as P

QUERY_HEADS = 18
KEY_VALUE_HEADS = 6
HEAD_WIDTH = 64
TURN = HEAD_WIDTH // 2
GROUP = QUERY_HEADS // KEY_VALUE_HEADS
GROUPS = KEY_VALUE_HEADS // 2
HALF_QUERY = QUERY_HEADS // 2 * HEAD_WIDTH
HALF_KEY = GROUPS * HEAD_WIDTH
CHUNKS = 3
BLOCKS = 4
GAIN_ROWS = 16
FFN_ROWS = 512
COST = 0.1

low_type = jnp.bfloat16
eps_norm = 1e-05
masked_score = -1e30
lowest_peak = -1e20
LOG2E = math.log2(math.e)
SCORE_SCALE = HEAD_WIDTH ** (-0.5)
VMEM_LIMIT = 58 * 1024 * 1024

PAIR = [(0, 1), (1, 0)]
ANY = pl.BlockSpec(memory_space=pl.ANY)
SCALARS = pl.BlockSpec(memory_space=pltpu.SMEM)


def inverse_freq():
    return 10000.0 ** (-(jnp.arange(TURN, dtype=jnp.float32) * 2.0) / HEAD_WIDTH)


def norm_scale(value):
    return lax.rsqrt(jnp.mean(value * value, axis=-1, keepdims=True) + eps_norm)


def norm_back(scaled, value, scale):
    return scale * scaled - value * scale**3 * jnp.mean(scaled * value, axis=-1, keepdims=True)


def dot(left, right, over=(1, 0)):
    return lax.dot_general(
        left, right, (((over[0],), (over[1],)), ((), ())), preferred_element_type=jnp.float32
    )


def swap_core(value):
    return lax.ppermute(value, "core", PAIR)


def behind(value, others):
    return lax.optimization_barrier((value, *others))[0]


def ignoring(kernel, given, after):
    def wrapped(*refs):
        kernel(*refs[:given], *refs[given + len(after) :])

    return wrapped


def params():
    return pltpu.CompilerParams(vmem_limit_bytes=VMEM_LIMIT)


def cost(flops, moved, special=0):
    return pl.CostEstimate(
        flops=int(flops * COST), bytes_accessed=int(moved * COST), transcendentals=int(special * COST)
    )


def shape(dims, kind=low_type):
    return jax.ShapeDtypeStruct(tuple(dims), kind)


def pack_attn_kernel(info, q_ref, k_ref, v_ref, o_ref, gain_ref, own_ref, *piece_ref):
    def half(ref):
        size = ref.shape[1] // 2
        value = ref[...].astype(low_type)
        return jnp.where(info[0] == 0, value[:, :size], value[:, size:])

    own_ref[...] = jnp.concatenate([half(r) for r in (q_ref, k_ref, v_ref, o_ref)], axis=1)
    rows = own_ref.shape[0]
    for ref in piece_ref:
        part = ref.shape[1]
        ref[:rows, :] = own_ref[:, pl.ds(pl.multiple_of(info[1] * part, part), part)]
        gains = jnp.concatenate([gain_ref[...], jnp.zeros((GAIN_ROWS - 2, rows), jnp.float32)], axis=0)
        gains = jnp.concatenate([gains, jnp.zeros((GAIN_ROWS, part - rows), jnp.float32)], axis=1)
        ref[rows:, :] = gains.astype(low_type)


def pack_attn(info, arrays, gains, tuned):
    rows = arrays[0].shape[0]
    width = sum(a.shape[1] for a in arrays) // 2
    outs = [shape((rows, width))] + [shape((rows + GAIN_ROWS, width // BLOCKS))] * tuned
    return pl.pallas_call(
        pack_attn_kernel,
        in_specs=[SCALARS] + [pl.BlockSpec()] * 5,
        out_specs=[pl.BlockSpec()] * len(outs),
        out_shape=outs,
        compiler_params=params(),
        cost_estimate=cost(0, rows * width * 10),
    )(info, *arrays, gains)


def pack_ffn_kernel(info, gate_ref, up_ref, down_ref, own_ref, *piece_ref):
    step, steps = pl.program_id(0), pl.num_programs(0)
    part = gate_ref.shape[1] // CHUNKS
    rows = gate_ref.shape[0]
    blocks = own_ref.shape[2] // part // 3
    for c in range(CHUNKS):
        at = slice(c * part, (c + 1) * part)
        here = pl.ds(pl.multiple_of(step * part, part), part)
        own_ref[c, :, here] = gate_ref[:, at].astype(low_type)
        there = pl.ds(pl.multiple_of((blocks + step) * part, part), part)
        own_ref[c, :, there] = up_ref[:, at].astype(low_type)

    @pl.when(step == 0)
    def _():
        turned = down_ref[...].astype(low_type).T
        for c in range(CHUNKS):
            for q in range(blocks):
                own_ref[c, :, (2 * blocks + q) * part : (2 * blocks + q + 1) * part] = turned[
                    q * rows : (q + 1) * rows, c * part : (c + 1) * part
                ]

    @pl.when(step == steps - 1)
    def _():
        if piece_ref:
            one, two = piece_ref
            size, cut = one.shape[1], rows // 2
            at = pl.ds(pl.multiple_of(info[1] * size, size), size)
            one[:rows, :] = own_ref[0, :, at]
            one[rows:, :] = own_ref[1, :cut, at]
            two[:cut, :] = own_ref[1, cut:, at]
            two[cut:, :] = own_ref[2, :, at]


def pack_ffn(info, gate, up, down, after, tuned):
    rows, hidden = gate.shape
    hidden_rows, width = down.shape
    steps = hidden // hidden_rows
    half = hidden_rows // 2
    packed = 3 * steps * (half // CHUNKS)
    part = packed // BLOCKS
    outs = [shape((CHUNKS, rows, packed))]
    if tuned:
        outs += [shape((rows + rows // 2, part))] * 2
    columns = pl.BlockSpec((rows, half), lambda z, info: (0, 2 * z + info[0]))
    return pl.pallas_call(
        ignoring(pack_ffn_kernel, 4, after),
        grid_spec=pltpu.PrefetchScalarGridSpec(
            num_scalar_prefetch=1,
            grid=(steps,),
            in_specs=[columns, columns, pl.BlockSpec((half, width), lambda z, info: (info[0], 0))]
            + [ANY] * len(after),
            out_specs=[
                pl.BlockSpec(o.shape, lambda z, info, n=len(o.shape): (0,) * n) for o in outs
            ],
        ),
        out_shape=outs,
        compiler_params=params(),
        cost_estimate=cost(0, rows * packed * CHUNKS * 6),
    )(info, gate, up, down, *after)


def ring(count, step):
    return [(i, (i + step) % count) for i in range(count)]


def place_pieces(info, count, own, stacks, forward, out_ref, sems):
    rows, part = own.shape[0], out_ref.shape[2]
    copies = []

    def begin(source, block, row):
        target = out_ref.at[block, pl.ds(pl.multiple_of(row * rows, rows), rows), :]
        copies.append(pltpu.make_async_copy(source, target, sems.at[len(copies)]))
        copies[-1].start()

    for b in range(BLOCKS):
        begin(own.at[:, b * part : (b + 1) * part], b, info[2])
    for flip, stack in enumerate(stacks):
        for k in range(1, count):
            row = lax.rem(info[2] + (k if forward else count - k), count)
            begin(stack.at[k - 1], jnp.bitwise_xor(info[1], flip), row)
    return copies


def assemble(info, own, stacks, count, after):
    rows, width = own.shape
    out = shape((BLOCKS, rows * count, width // BLOCKS))

    def kernel(info, own_ref, *refs):
        *stack_refs, out_ref, tail_ref, sems = refs
        for copy in place_pieces(info, count, own_ref, stack_refs, False, out_ref, sems):
            copy.wait()
        tail_ref[...] = out_ref[BLOCKS // 2 :]

    return pl.pallas_call(
        ignoring(kernel, 2 + len(stacks), after),
        in_specs=[SCALARS] + [ANY] * (1 + len(stacks) + len(after)),
        out_specs=[pl.BlockSpec()] * 2,
        out_shape=[out, shape((BLOCKS // 2, *out.shape[1:]))],
        scratch_shapes=[pltpu.SemaphoreType.DMA((BLOCKS * count,))],
        compiler_params=params(),
        cost_estimate=cost(0, rows * width * count * 4),
    )(info, own, *stacks, *after)


def pick_kernel(parts, info, *refs):
    ins = refs[: -1 - len({p[0] for p in parts})]
    outs, sems = refs[len(ins) : -1], refs[-1]
    copies = []
    for out, source, start, stop, at in parts:
        count = ins[source].shape[0]
        for k in range(1, count):
            rows = ins[source].at[lax.rem(info[2] + k, count), start:stop]
            target = outs[out].at[k - 1, at : at + stop - start]
            copies.append(pltpu.make_async_copy(rows, target, sems.at[len(copies)]))
            copies[-1].start()
    for copy in copies:
        copy.wait()


def pick(info, arrays, parts, rows, after):
    count, _, part = arrays[0].shape
    outs = [shape((count - 1, rows, part))] * len({p[0] for p in parts})

    def kernel(*refs):
        pick_kernel(parts, *refs)

    return pl.pallas_call(
        ignoring(kernel, 1 + len(arrays), after),
        in_specs=[SCALARS] + [ANY] * (len(arrays) + len(after)),
        out_specs=[pl.BlockSpec()] * len(outs),
        out_shape=outs,
        scratch_shapes=[pltpu.SemaphoreType.DMA((len(parts) * (count - 1),))],
        compiler_params=params(),
        cost_estimate=cost(0, len(outs) * count * rows * part * 4),
    )(info, *arrays, *after)


def travel_z(piece, sizes):
    return [lax.ppermute(piece, "z", ring(sizes[2], k)) for k in range(1, sizes[2])]


def gather_whole(own):
    full = lax.all_gather(own, "z", axis=0, tiled=True)
    return full.reshape(full.shape[0], BLOCKS, -1).transpose(1, 0, 2)


def send_out(info, packed, outs, way, sems):
    copies = []

    def begin(source, target):
        copies.append(pltpu.make_async_copy(source, target, sems.at[len(copies)]))
        copies[-1].start()

    if way == "whole":
        begin(packed, outs[0])
    elif way == "z":
        count, _, rows, _ = outs[0].shape
        for z in range(count):
            for b in range(BLOCKS):
                begin(packed.at[b, z * rows : (z + 1) * rows], outs[0].at[z, b])
    else:
        keep_one, send_one, keep_two, send_two = outs
        cut = packed.shape[1] // 2
        y, x = lax.div(info[1], 2), lax.rem(info[1], 2)
        for i in range(2):
            at_y, at_x = jnp.bitwise_xor(y, i), jnp.bitwise_xor(x, i)
            begin(packed.at[at_y * 2 + x, :cut], keep_one.at[i])
            begin(packed.at[at_y * 2 + 1 - x, :cut], send_one.at[i])
            begin(packed.at[y * 2 + at_x, cut:], keep_two.at[i])
            begin(packed.at[(1 - y) * 2 + at_x, cut:], send_two.at[i])
    return copies


def sent_shapes(rows, part, way):
    if way == "xy":
        return [shape((2, rows // 2, part))] * 4
    if way == "z":
        return [shape((BLOCKS, BLOCKS, rows // BLOCKS, part))]
    return [shape((BLOCKS, rows, part))]


def sum_over(value, axis, count):
    if count & (count - 1):
        return lax.psum(value, axis)
    step = 1
    while step < count:
        value = value + lax.ppermute(value, axis, [(i, i ^ step) for i in range(count)])
        step *= 2
    return value


def add_low(kept, came):
    return (kept.astype(jnp.float32) + came.astype(jnp.float32)).astype(low_type)


def scatter_first(outs):
    if len(outs) == 1:
        return ()
    return lax.ppermute(outs[1], "x", PAIR), lax.ppermute(outs[3], "y", PAIR)


def scatter_sums(outs, came, last):
    if len(outs) == 1:
        return ()
    came = lax.optimization_barrier((*came, *last))
    return add_low(outs[0][1], came[0][1]), add_low(outs[2][1], came[1][1])


def scatter_second(sums):
    if len(sums) == 0:
        return ()
    return lax.ppermute(sums[0], "y", PAIR), lax.ppermute(sums[1], "x", PAIR)


def merge_kernel(info, *refs):
    parts, outs, mine_s = refs[:6], refs[6:-1], refs[-1]
    cut = mine_s.shape[0] // 2
    rows = outs[0].shape[0]
    for i in range(2):
        kept, came, second = (ref[...].astype(jnp.float32) for ref in parts[3 * i : 3 * i + 3])
        mine_s[i * cut : (i + 1) * cut, :] = (kept[0] + came[0] + second).astype(low_type)
    for k, out in enumerate(outs):
        row = lax.rem(info[2] + k, len(outs)) * rows if len(outs) > 1 else 0
        out[...] = mine_s[pl.ds(row, rows), :]


def merge(info, outs, first, second, count):
    cut, part = second[0].shape
    half = pl.BlockSpec((1, cut, part), lambda i: (0, 0, 0))
    whole = pl.BlockSpec((cut, part), lambda i: (0, 0))
    rows = 2 * cut // count
    return pl.pallas_call(
        merge_kernel,
        grid=(1,),
        in_specs=[SCALARS] + [half, half, whole] * 2,
        out_specs=[pl.BlockSpec((rows, part), lambda i: (0, 0))] * count,
        out_shape=[shape((rows, part))] * count,
        scratch_shapes=[pltpu.VMEM((2 * cut, part), low_type)],
        compiler_params=params(),
        cost_estimate=cost(0, 16 * cut * part),
    )(info, outs[0], first[0], second[0], outs[2], first[1], second[1])


def scatter_mine(info, outs, first, second, last, sizes):
    ny, nx, nz = sizes
    if len(outs) == 1:
        packed = outs[0]
        total = packed.shape[1]
        split = packed.transpose(1, 0, 2).reshape(total, ny * nx, -1).transpose(1, 0, 2)
        return lax.psum_scatter(split, ("y", "x"), scatter_dimension=0, tiled=True)[0]
    return merge(info, outs, first, lax.optimization_barrier((*second, *last))[: len(second)], 1)[0]


def scatter_z(pieces, sizes):
    mine, *others = pieces
    came = [lax.ppermute(o, "z", ring(sizes[2], k + 1)) for k, o in enumerate(others)]
    return sum((c.astype(jnp.float32) for c in came), mine.astype(jnp.float32)).astype(low_type)


def scatter_rows(mine):
    return lax.psum_scatter(mine, "z", scatter_dimension=0, tiled=True)


def spread(total, sizes):
    if sizes[0] * sizes[1] == BLOCKS:
        mine = [
            total,
            lax.ppermute(total, "x", PAIR),
            lax.ppermute(total, "y", PAIR),
            lax.ppermute(total, ("y", "x"), [(i, 3 - i) for i in range(4)]),
        ]
        return mine, [swap_core(value) for value in mine]
    everyone = jnp.moveaxis(lax.all_gather(total, ("y", "x"), axis=0), 0, -2)
    everyone = jnp.moveaxis(everyone.reshape(total.shape[:2] + (BLOCKS, -1)), -2, 0)
    place = lax.axis_index("y") * sizes[1] + lax.axis_index("x")
    mine = [
        lax.dynamic_index_in_dim(everyone, (place % BLOCKS) ^ i, 0, False) for i in range(BLOCKS)
    ]
    return mine, [swap_core(value) for value in mine]


def gather_all(total, sizes):
    everyone = lax.all_gather(total, ("core", "y", "x"), axis=0)
    count = sizes[0] * sizes[1]
    if count == BLOCKS:
        return (everyone,)
    both = jnp.moveaxis(everyone.reshape((2, count) + total.shape), 1, -2)
    both = jnp.moveaxis(both.reshape((2,) + total.shape[:2] + (BLOCKS, -1)), -2, 1)
    return (both.reshape((2 * BLOCKS,) + both.shape[2:]),)


def turn_heads(ref, value, cosine, sine, start):
    for h in range(value.shape[0] // HEAD_WIDTH):
        former = value[h * HEAD_WIDTH : h * HEAD_WIDTH + TURN]
        latter = value[h * HEAD_WIDTH + TURN : (h + 1) * HEAD_WIDTH]
        at = start + h * HEAD_WIDTH
        ref[at : at + TURN, :] = (former * cosine - latter * sine).astype(ref.dtype)
        ref[at + TURN : at + HEAD_WIDTH, :] = (latter * cosine + former * sine).astype(ref.dtype)


def project_kernel(mine_ref, other_ref, gain_ref, w_ref, cos_ref, sin_ref, normed_ref, q_ref, kv_ref):
    rows = mine_ref.shape[0]
    hk, part = HALF_KEY, w_ref.shape[2]
    for i, ref in enumerate((mine_ref, other_ref)):
        value = ref[...].astype(jnp.float32)
        normed = (value * norm_scale(value) * gain_ref[...]).astype(low_type)
        at = slice(i * rows, (i + 1) * rows)
        normed_ref[:, at] = normed.T
    weights = [w_ref[0].T, w_ref[1].T, w_ref[2].T[:hk]]
    for i in range(2):
        at = slice(i * rows, (i + 1) * rows)
        normed = normed_ref[:, at]
        cosine, sine = cos_ref[:, at], sin_ref[:, at]
        first = dot(weights[0], normed)
        turn_heads(q_ref.at[:, at], first, cosine, sine, 0)
        second = dot(weights[1], normed)
        turn_heads(q_ref.at[:, at], second[: part - hk], cosine, sine, part)
        turn_heads(kv_ref.at[0, :, at], second[part - hk :], cosine, sine, 0)
        kv_ref[1, :, at] = dot(weights[2], normed).astype(low_type)


def project(mine, other, gain, weights, cosine, sine):
    rows, width = mine.shape
    return pl.pallas_call(
        project_kernel,
        in_specs=[pl.BlockSpec()] * 6,
        out_specs=[pl.BlockSpec()] * 3,
        out_shape=[
            shape((width, 2 * rows)), shape((HALF_QUERY, 2 * rows)), shape((2, HALF_KEY, 2 * rows))
        ],
        compiler_params=params(),
        cost_estimate=cost(4 * rows * width * 960, 14 << 20),
    )(mine, other, gain, weights, cosine, sine)


def tile_mask(first, place0, key0, size, causal):
    key_place = key0 + lax.broadcasted_iota(jnp.int32, (size, size), 0)
    allowed = key_place >= first
    if causal:
        place = place0 + lax.broadcasted_iota(jnp.int32, (size, size), 1)
        allowed = allowed & (key_place <= place)
    return jnp.concatenate([allowed] * GROUP, axis=1)


def heads_of(ref):
    return jnp.concatenate(
        [ref[r * HEAD_WIDTH : (r + 1) * HEAD_WIDTH, :] for r in range(GROUP)], axis=1
    )


def over_tiles(info, size, rows, turn):
    per = rows // size
    half = pl.program_id(2)
    own = info[3] * per
    hi = own + half
    lo = info[4 + pl.program_id(0) * per + half]

    def columns(b):
        return pl.ds(pl.multiple_of(lax.rem(b, per) * size, size), size)

    def earlier(b, _):
        turn(hi, b, lax.div(b, per), columns(b))
        return 0

    def here(b, _):
        turn(hi, b, None, columns(b))
        return 0

    lax.fori_loop(lo, own, earlier, 0)
    lax.fori_loop(jnp.maximum(lo, own), hi + 1, here, 0)


def attend_kernel(info, q_ref, kv_ref, past_ref, first_ref, o_ref, total_ref, peak_s, sum_s, acc_s):
    size, rows = q_ref.shape[1], kv_ref.shape[2]
    q = heads_of(q_ref)
    peak_s[...] = jnp.full(peak_s.shape, lowest_peak, jnp.float32)
    sum_s[...] = jnp.zeros(sum_s.shape, jnp.float32)
    acc_s[...] = jnp.zeros(acc_s.shape, jnp.float32)

    def turn(hi, b, past, at):
        k = kv_ref[0, :, at] if past is None else past_ref[past, 0, :, at]
        v = kv_ref[1, :, at] if past is None else past_ref[past, 1, :, at]
        allowed = tile_mask(first_ref[0], hi * size, b * size, size, past is None)
        scores = dot(k, q, (0, 0)) * (SCORE_SCALE * LOG2E)
        scores = jnp.where(allowed, scores, masked_score)
        peak = peak_s[...]
        fresh = jnp.maximum(peak, jnp.max(scores, axis=0, keepdims=True))
        shrink = jnp.exp2(peak - fresh)
        terms = jnp.exp2(scores - fresh)
        peak_s[...] = fresh
        sum_s[...] = sum_s[...] * shrink + jnp.sum(terms, axis=0, keepdims=True)
        acc_s[...] = acc_s[...] * shrink + dot(v, terms.astype(low_type))

    over_tiles(info, size, rows, turn)
    total = sum_s[...]
    mixed = acc_s[...] / total
    log_total = peak_s[...] + jnp.log2(total)
    for r in range(GROUP):
        o_ref[r * HEAD_WIDTH : (r + 1) * HEAD_WIDTH, :] = mixed[:, r * size : (r + 1) * size]
        total_ref[0, r : r + 1, :] = log_total[:, r * size : (r + 1) * size]


def attend_back_kernel(
    info, q_ref, kv_ref, past_ref, g_ref, first_ref, total_ref, delta_ref, dq_ref, dkv_ref, dpast_ref,
    acc_s, past_s,
):
    size, rows = q_ref.shape[1], kv_ref.shape[2]
    q = heads_of(q_ref)
    g = heads_of(g_ref)
    total = jnp.concatenate([total_ref[0, r : r + 1, :] for r in range(GROUP)], axis=1)
    delta = jnp.concatenate([delta_ref[0, r : r + 1, :] for r in range(GROUP)], axis=1)
    acc_s[...] = jnp.zeros(acc_s.shape, jnp.float32)

    @pl.when(pl.program_id(2) == 0)
    def _():
        dkv_ref[...] = jnp.zeros(dkv_ref.shape, jnp.float32)
        past_s[...] = jnp.zeros(past_s.shape, jnp.float32)

    def turn(hi, b, past, at):
        k = kv_ref[0, :, at] if past is None else past_ref[past, 0, :, at]
        v = kv_ref[1, :, at] if past is None else past_ref[past, 1, :, at]
        allowed = tile_mask(first_ref[0], hi * size, b * size, size, past is None)
        scores = dot(k, q, (0, 0)) * (SCORE_SCALE * LOG2E)
        weights = jnp.exp2(jnp.where(allowed, scores - total, masked_score))
        grad_weights = dot(v, g, (0, 0))
        grad_scores = (weights * (grad_weights - delta) * SCORE_SCALE).astype(low_type)
        dk = dot(q, grad_scores, (1, 1))
        dv = dot(g, weights.astype(low_type), (1, 1))
        if past is None:
            dkv_ref[0, :, at] += dk
            dkv_ref[1, :, at] += dv
        else:
            past_s[past, 0, :, at] += dk
            past_s[past, 1, :, at] += dv
        acc_s[...] += dot(k, grad_scores)

    over_tiles(info, size, rows, turn)
    acc = acc_s[...]
    for r in range(GROUP):
        dq_ref[r * HEAD_WIDTH : (r + 1) * HEAD_WIDTH, :] = acc[:, r * size : (r + 1) * size]

    @pl.when(pl.program_id(2) == pl.num_programs(2) - 1)
    def _():
        dpast_ref[...] = past_s[...].astype(low_type)


def attention_specs(parts, rows, size):
    per = rows // size
    wide = pl.BlockSpec((GROUP * HEAD_WIDTH, size), lambda s, g, h: (g, s * per + h))
    own = pl.BlockSpec((2, HEAD_WIDTH, rows), lambda s, g, h: (0, g, s))
    past = pl.BlockSpec((parts, 2, HEAD_WIDTH, rows), lambda s, g, h: (0, 0, g, s))
    first = pl.BlockSpec((1, 1, size), lambda s, g, h: (s, 0, h))
    stat = pl.BlockSpec((1, 8, size), lambda s, g, h: (g, 0, s * per + h))
    return (2, GROUPS, per), wide, own, past, first, stat


def attend(info, query, keyvalue, past, first, size, after):
    both = keyvalue.shape[2]
    rows = both // 2
    grid, wide, own, past_spec, first_spec, stat = attention_specs(past.shape[0], rows, size)
    pairs = 2 * rows * rows * 3 // 2
    return pl.pallas_call(
        ignoring(attend_kernel, 5, after),
        grid=grid,
        in_specs=[SCALARS, wide, own, past_spec, first_spec] + [ANY] * len(after),
        out_specs=[wide, stat],
        out_shape=[shape(query.shape, jnp.float32), shape((GROUPS, 8, both), jnp.float32)],
        scratch_shapes=[
            pltpu.VMEM((1, GROUP * size), jnp.float32),
            pltpu.VMEM((1, GROUP * size), jnp.float32),
            pltpu.VMEM((HEAD_WIDTH, GROUP * size), jnp.float32),
        ],
        compiler_params=params(),
        cost_estimate=cost(pairs * 9 * 64 * 4 * 5, 8 << 20, pairs * 9),
    )(info, query, keyvalue, past, first, *after)


def attend_back(info, query, keyvalue, past, grad, first, log_total, delta, size, after):
    both = keyvalue.shape[2]
    rows = both // 2
    grid, wide, own, past_spec, first_spec, stat = attention_specs(past.shape[0], rows, size)
    pairs = 2 * rows * rows * 3 // 2
    return pl.pallas_call(
        ignoring(attend_back_kernel, 8, after),
        grid=grid,
        in_specs=[SCALARS, wide, own, past_spec, wide, first_spec, stat, stat] + [ANY] * len(after),
        out_specs=[wide, own, past_spec],
        out_shape=[
            shape(query.shape, jnp.float32), shape(keyvalue.shape, jnp.float32), shape(past.shape)
        ],
        scratch_shapes=[
            pltpu.VMEM((HEAD_WIDTH, GROUP * size), jnp.float32),
            pltpu.VMEM((past.shape[0], 2, HEAD_WIDTH, rows), jnp.float32),
        ],
        compiler_params=params(),
        cost_estimate=cost(pairs * 9 * 64 * 10 * 3, 12 << 20, pairs * 9),
    )(info, query, keyvalue, past, grad, first, log_total, delta, *after)


def place_out(core, mine_ref, other_ref, out_ref):
    cut, part = HALF_KEY, mine_ref.shape[2]
    mine = jnp.concatenate([mine_ref[0][:, cut:], mine_ref[1]], axis=1)
    other = jnp.concatenate([other_ref[0][:, cut:], other_ref[1]], axis=1)
    out_ref[...] = jnp.where(
        core == 0,
        jnp.concatenate([mine, other], axis=1),
        jnp.concatenate([other, mine], axis=1),
    )


def out_kernel(
    info, mine_ref, came_ref, w_ref, w_other_ref, tokens_ref, gain_ref, middle_ref, *refs
):
    normed_refs, turned_refs, (rows_ref, w_s) = refs[:2], refs[2:4], refs[4:]
    place_out(info[0], w_ref, w_other_ref, w_s)
    hq = HALF_QUERY
    mine = w_s[pl.ds(pl.multiple_of(info[0] * hq, hq), hq), :]
    other = w_s[pl.ds(pl.multiple_of((1 - info[0]) * hq, hq), hq), :]
    rows_ref[...] = mine
    middle = (
        tokens_ref[...].astype(jnp.float32)
        + dot(mine_ref[...].astype(low_type).T, mine)
        + dot(came_ref[...].T, other)
    )
    middle_ref[...] = middle
    normed = (middle * norm_scale(middle) * gain_ref[...]).astype(low_type)
    cut = normed.shape[0] // 2
    for i in range(2):
        part = normed[i * cut : (i + 1) * cut]
        normed_refs[i][...] = part
        turned_refs[i][...] = part.T


def project_out(info, attended, came, weights, weights_other, tokens, gain, after):
    rows, width = tokens.shape
    hq = HALF_QUERY
    part = weights.shape[2]
    return pl.pallas_call(
        ignoring(out_kernel, 7, after),
        grid=(1,),
        in_specs=[
            SCALARS,
            pl.BlockSpec((hq, rows), lambda i: (0, 0)),
            pl.BlockSpec((hq, rows), lambda i: (0, 0)),
            pl.BlockSpec((2, width, part), lambda i: (1, 0, 0)),
            pl.BlockSpec((2, width, part), lambda i: (0, 0, 0)),
            pl.BlockSpec((rows, width), lambda i: (0, 0)),
            pl.BlockSpec((1, width), lambda i: (0, 0)),
        ]
        + [ANY] * len(after),
        out_specs=[
            pl.BlockSpec((rows, width), lambda i: (0, 0)),
            pl.BlockSpec((rows // 2, width), lambda i: (0, 0)),
            pl.BlockSpec((rows // 2, width), lambda i: (0, 0)),
            pl.BlockSpec((width, rows // 2), lambda i: (0, 0)),
            pl.BlockSpec((width, rows // 2), lambda i: (0, 0)),
            pl.BlockSpec((hq, width), lambda i: (0, 0)),
        ],
        out_shape=[
            shape((rows, width), jnp.float32), shape((rows // 2, width)), shape((rows // 2, width)),
            shape((width, rows // 2)), shape((width, rows // 2)), shape((hq, width)),
        ],
        scratch_shapes=[pltpu.VMEM((width, width), low_type)],
        compiler_params=params(),
        cost_estimate=cost(2 * rows * width * width, 16 << 20),
    )(info, attended, came, weights, weights_other, tokens, gain, *after)


def ffn_kernel(tuned, ways, info, *refs):
    xs, xts, cs, cts, w_ref, refs = refs[0:4], refs[4:8], refs[8:10], refs[10:12], refs[12], refs[13:]
    stacks = [()] * CHUNKS
    if tuned:
        stacks, refs = [refs[4 * j : 4 * j + 4] for j in range(CHUNKS)], refs[4 * CHUNKS :]
    totals, outs, scratch = refs[:4], list(refs[4:-17]), refs[-17:]
    (
        x_s, c_s, xt_s, ct_s, result_s, grad_s, result_low, grad_low, land_s, gate_s, up_s, down_s,
        hidden_s, dgate_s, dup_s, packed_s, sems,
    ) = scratch
    rows = cs[0].shape[0]
    size = FFN_ROWS
    block, part = gate_s.shape[1], packed_s.shape[3]
    width = gate_s.shape[0]
    lane, turned = block // BLOCKS, width // BLOCKS

    def begin(source, target, sem):
        copy = pltpu.make_async_copy(source, target, sem)
        copy.start()
        return copy

    def weights_in(j):
        target = land_s.at[j % 2]
        if tuned:
            return place_pieces(info, BLOCKS, w_ref.at[j], stacks[j], True, target, sems.at[j])
        return [begin(w_ref.at[j], target, sems.at[j, 0])]

    coming = weights_in(0)
    few = rows // 2
    there = [begin(ref, x_s.at[i * few : (i + 1) * few], sems.at[3, i]) for i, ref in enumerate(xs)]
    there += [begin(ref, c_s.at[i * rows : (i + 1) * rows], sems.at[3, 4 + i]) for i, ref in enumerate(cs)]
    across = [begin(ref, xt_s.at[:, i * few : (i + 1) * few], sems.at[3, 6 + i]) for i, ref in enumerate(xts)]
    across += [begin(ref, ct_s.at[:, i * rows : (i + 1) * rows], sems.at[3, 10 + i]) for i, ref in enumerate(cts)]
    going = [[] for _ in range(CHUNKS + 1)]
    for j in range(CHUNKS):
        for copy in coming:
            copy.wait()
        land = land_s.at[j % 2]
        gate_s[:, :part] = land[0]
        gate_s[:, part:] = land[1, :, : block - part]
        up_s[:, : 2 * part - block] = land[1, :, block - part :]
        up_s[:, 2 * part - block :] = land[2, :, : 2 * block - 2 * part]
        for q in range(BLOCKS):
            for z in range(BLOCKS):
                column = 2 * block + q * lane
                b, at = column // part, column % part
                down_s[q * turned : (q + 1) * turned, z * lane : (z + 1) * lane] = land[
                    b, z * turned : (z + 1) * turned, at : at + lane
                ]
        coming = weights_in(j + 1) if j + 1 < CHUNKS else []
        if j == 0:
            for copy in there:
                copy.wait()

        def forward(t, _, j=j):
            at = pl.ds(pl.multiple_of(t * size, size), size)
            x, c = x_s[at, :], c_s[at, :]
            gate = dot(x, gate_s[...])
            upward = dot(x, up_s[...])
            grad_hidden = dot(c, down_s[...])
            sigmoid = 1.0 / (1.0 + jnp.exp(-gate))
            silu = gate * sigmoid
            hidden = (silu * upward).astype(low_type)
            grad_gate = grad_hidden * upward * sigmoid * (1.0 + gate * (1.0 - sigmoid))
            grad_gate = grad_gate.astype(low_type)
            grad_up = (grad_hidden * silu).astype(low_type)
            hidden_s[at, :], dgate_s[at, :], dup_s[at, :] = hidden, grad_gate, grad_up
            result = dot(hidden, down_s[...], (1, 1))
            grad = dot(grad_gate, gate_s[...], (1, 1)) + dot(grad_up, up_s[...], (1, 1))
            if j > 0:
                result, grad = result + result_s[at, :], grad + grad_s[at, :]
            result_s[at, :], grad_s[at, :] = result, grad
            return 0

        lax.fori_loop(0, 2 * rows // size, forward, 0)
        if j == 0:
            for copy in across:
                copy.wait()
        if j == CHUNKS - 1:
            result_low[...] = result_s[rows:, :].astype(low_type)
            grad_low[...] = grad_s[rows:, :].astype(low_type)
            sources = (result_s.at[:rows], grad_s.at[:rows], result_low, grad_low)
            going[CHUNKS] = [begin(s, t, sems.at[3, 12 + i]) for i, (s, t) in enumerate(zip(sources, totals))]
        if j >= 2:
            for copy in going[j - 2]:
                copy.wait()
        packed = packed_s.at[j % 2]

        def backward(q, _, packed=packed):
            at = pl.ds(pl.multiple_of(q * turned, turned), turned)
            xt = xt_s[at, :]
            gate = dot(xt, dgate_s[...]).astype(low_type)
            up = dot(xt, dup_s[...]).astype(low_type)
            down = dot(ct_s[at, :], hidden_s[...]).astype(low_type)
            packed[0, at, :] = gate[:, :part]
            packed[1, at, : block - part] = gate[:, part:]
            packed[1, at, block - part :] = up[:, : 2 * part - block]
            packed[2, at, : 2 * block - 2 * part] = up[:, 2 * part - block :]
            column = 2 * block + q * lane
            b = lax.div(column, part)
            place = pl.ds(pl.multiple_of(lax.rem(column, part), lane), lane)
            for z in range(BLOCKS):
                packed[b, z * turned : (z + 1) * turned, place] = down[:, z * lane : (z + 1) * lane]
            return 0

        lax.fori_loop(0, BLOCKS, backward, 0)
        count = 4 if ways[j] == "xy" else 1
        going[j] = send_out(info, packed, outs[:count], ways[j], sems.at[4 + j])
        outs = outs[count:]
    for copy in going[CHUNKS - 2] + going[CHUNKS - 1] + going[CHUNKS]:
        copy.wait()


def feed_forward(info, xs, cs, xts, cts, weights, pieces, ways, tuned, after):
    rows, width = cs[0].shape
    part = weights.shape[2] // BLOCKS if tuned else weights.shape[3]
    block = BLOCKS * part // 3
    sent = [sent_shapes(width, part, way) for way in ways]
    given = sum((list(p) for p in pieces), [])
    totals = [shape((rows, width), jnp.float32)] * 2 + [shape((rows, width))] * 2

    def kernel(info, *refs):
        ffn_kernel(tuned, ways, info, *refs)

    whole = pltpu.VMEM((2 * rows, width), low_type)
    turned = pltpu.VMEM((width, 2 * rows), low_type)
    total = pltpu.VMEM((2 * rows, width), jnp.float32)
    low = pltpu.VMEM((rows, width), low_type)
    packed = pltpu.VMEM((2, BLOCKS, width, part), low_type)
    matrix = pltpu.VMEM((width, block), low_type)
    tokens = pltpu.VMEM((2 * rows, block), low_type)
    outs = pl.pallas_call(
        ignoring(kernel, 14 + len(given), after),
        in_specs=[SCALARS] + [ANY] * (13 + len(given) + len(after)),
        out_specs=[ANY] * (4 + sum(len(s) for s in sent)),
        out_shape=totals + sum(sent, []),
        scratch_shapes=[
            whole, whole, turned, turned, total, total, low, low, packed, matrix, matrix, matrix,
            tokens, tokens, tokens, packed, pltpu.SemaphoreType.DMA((4 + CHUNKS, 16)),
        ],
        compiler_params=params(),
        cost_estimate=cost(
            36 * rows * width * block * CHUNKS, 40 << 20, 2 * rows * block * CHUNKS
        ),
    )(info, *xs, *xts, *cs, *cts, weights, *given, *after)
    totals, outs = outs[:4], outs[4:]
    groups = []
    for shapes in sent:
        groups.append(outs[: len(shapes)])
        outs = outs[len(shapes) :]
    return totals, groups


def branch_kernel(g_ref, one_ref, two_ref, w_ref, attended_ref, grad_ref, delta_ref, rows_ref, other_s):
    rows = g_ref.shape[0]
    other_s[: rows // 2, :] = one_ref[...]
    other_s[rows // 2 :, :] = two_ref[...]
    g_other_ref = other_s
    delta_ref[...] = jnp.zeros(delta_ref.shape, jnp.float32)
    for i, ref in enumerate((g_ref, g_other_ref)):
        at = slice(i * rows, (i + 1) * rows)
        grad = dot(w_ref[...], ref[...], (1, 1)).astype(low_type)
        grad_ref[:, at] = grad
        product = grad.astype(jnp.float32) * attended_ref[:, at]
        for h in range(GROUP * GROUPS):
            delta_ref[h // GROUP, h % GROUP : h % GROUP + 1, at] = jnp.sum(
                product[h * HEAD_WIDTH : (h + 1) * HEAD_WIDTH], axis=0, keepdims=True
            )
    attended = attended_ref[...].astype(low_type)
    rows_ref[...] = (
        dot(attended[:, :rows], g_ref[...]) + dot(attended[:, rows:], g_other_ref[...])
    ).astype(low_type)


def branch(grad, grad_other, out_rows, attended, after):
    rows, width = grad.shape
    return pl.pallas_call(
        ignoring(branch_kernel, 5, after),
        in_specs=[pl.BlockSpec()] * 5 + [ANY] * len(after),
        out_specs=[pl.BlockSpec()] * 3,
        out_shape=[
            shape(attended.shape), shape((GROUPS, 8, 2 * rows), jnp.float32),
            shape((HALF_QUERY, width)),
        ],
        scratch_shapes=[pltpu.VMEM(grad.shape, low_type)],
        compiler_params=params(),
        cost_estimate=cost(8 * rows * width * HALF_QUERY, 12 << 20),
    )(grad, *grad_other, out_rows, attended, *after)


def attn_grad_kernel(
    info, dq_ref, dkv_ref, came_ref, cos_ref, sin_ref, normed_ref, mine_ref, other_ref, d_ref, *refs
):
    outs, packed_s, sems = refs[:-2], refs[-2], refs[-1]
    hq, hk = HALF_QUERY, HALF_KEY
    part = packed_s.shape[2]
    cosine, sine = cos_ref[...], -sin_ref[...]
    turn_heads(d_ref, dq_ref[...], cosine, sine, 0)
    whole = dkv_ref[...] + came_ref[...].astype(jnp.float32)
    turn_heads(d_ref, whole[0], cosine, sine, hq)
    d_ref[hq + hk :, :] = whole[1].astype(low_type)
    normed = normed_ref[...]
    packed_s[0] = dot(normed, d_ref[:part, :], (1, 1)).astype(low_type)
    packed_s[1] = dot(normed, d_ref[part : 2 * part, :], (1, 1)).astype(low_type)
    last = dot(normed, d_ref[2 * part :, :], (1, 1)).astype(low_type)
    mine, other = mine_ref[...], other_ref[...]
    low = info[0] == 0
    out = jnp.concatenate(
        [jnp.where(low, mine, other), jnp.where(low, other, mine)], axis=0
    )
    packed_s[2] = jnp.concatenate([last, out[:, : part - hk]], axis=1)
    packed_s[3] = out[:, part - hk :]
    for copy in send_out(info, packed_s, outs, "xy" if len(outs) > 1 else "whole", sems):
        copy.wait()


def attn_grads(info, grad_query, grad_kv, came, cosine, sine, normed, mine, other, after, tuned):
    width, both = normed.shape
    part = (2 * HALF_QUERY + 2 * HALF_KEY) // BLOCKS
    sent = sent_shapes(width, part, "xy" if tuned else "whole")
    return pl.pallas_call(
        ignoring(attn_grad_kernel, 9, after),
        in_specs=[SCALARS] + [pl.BlockSpec()] * 8 + [ANY] * len(after),
        out_specs=[pl.BlockSpec()] + [ANY] * len(sent),
        out_shape=[shape((HALF_QUERY + 2 * HALF_KEY, both))] + sent,
        scratch_shapes=[
            pltpu.VMEM((BLOCKS, width, part), low_type),
            pltpu.SemaphoreType.DMA((8,)),
        ],
        compiler_params=params(),
        cost_estimate=cost(2 * both * width * 960, 20 << 20),
    )(info, grad_query, grad_kv, came, cosine, sine, normed, mine, other, *after)


def normed_grad_kernel(d_ref, w_ref, mine_ref, other_ref):
    rows = mine_ref.shape[0]
    hk, part = HALF_KEY, w_ref.shape[2]
    for i, ref in enumerate((other_ref, mine_ref)):
        at = slice((1 - i) * rows, (2 - i) * rows)
        d = d_ref[:, at].T
        value = dot(d[:, :part], w_ref[0], (1, 1)) + dot(d[:, part : 2 * part], w_ref[1], (1, 1))
        value = value + dot(d[:, 2 * part :], w_ref[2][:, :hk], (1, 1))
        ref[...] = value.astype(ref.dtype)


def normed_grad(d, weights, after):
    width = weights.shape[1]
    rows = d.shape[1] // 2
    return pl.pallas_call(
        ignoring(normed_grad_kernel, 2, after),
        in_specs=[pl.BlockSpec()] * 2 + [ANY] * len(after),
        out_specs=[pl.BlockSpec()] * 2,
        out_shape=[shape((rows, width), jnp.float32), shape((rows, width))],
        compiler_params=params(),
        cost_estimate=cost(4 * rows * width * 960, 9 << 20),
    )(d, weights, *after)


def halves(info, refs, chunk):
    mine, other = refs[:BLOCKS], refs[BLOCKS:]
    place = lax.rem(info[1], BLOCKS)

    def ordered(values):
        for bit in (1, 2):
            flip = lax.rem(lax.div(place, bit), 2) == 1
            values = [jnp.where(flip, values[b ^ bit], values[b]) for b in range(BLOCKS)]
        return jnp.concatenate(values, axis=1)

    mine = ordered([ref[chunk] for ref in mine])
    other = ordered([ref[chunk] for ref in other])
    low = info[0] == 0
    return jnp.where(low, mine, other), jnp.where(low, other, mine)


def unpack_attn_kernel(info, *refs):
    refs, outs = refs[: 2 * BLOCKS], refs[2 * BLOCKS :]
    both = [value.astype(jnp.float32) for value in halves(info, refs, 0)]
    start = 0
    for ref, size in zip(outs, (HALF_QUERY, HALF_KEY, HALF_KEY, HALF_QUERY)):
        ref[...] = jnp.concatenate([v[:, start : start + size] for v in both], axis=1)
        start += size


def unpack_attn(info, mine, other):
    rows = mine[0].shape[1]
    return pl.pallas_call(
        unpack_attn_kernel,
        in_specs=[SCALARS] + [pl.BlockSpec()] * (2 * BLOCKS),
        out_specs=[pl.BlockSpec()] * 4,
        out_shape=[
            shape((rows, 2 * n), jnp.float32) for n in (HALF_QUERY, HALF_KEY, HALF_KEY, HALF_QUERY)
        ],
        compiler_params=params(),
        cost_estimate=cost(0, 6 << 20),
    )(info, *mine, *other)


def unpack_ffn_kernel(all_ref, gate_ref, up_ref, down_ref):
    part = all_ref.shape[3]
    block = BLOCKS * part // 3
    lane = block // BLOCKS
    half = CHUNKS * lane
    for h in range(2):
        for c in range(CHUNKS):
            value = jnp.concatenate([all_ref[h * BLOCKS + b, c] for b in range(BLOCKS)], axis=1)
            value = value.astype(jnp.float32)
            for z in range(BLOCKS):
                at = z * 2 * half + h * half + c * lane
                gate_ref[:, at : at + lane] = value[:, z * lane : (z + 1) * lane]
                up_ref[:, at : at + lane] = value[:, block + z * lane : block + (z + 1) * lane]
            down = jnp.concatenate(
                [value[:, 2 * block + q * lane : 2 * block + (q + 1) * lane] for q in range(BLOCKS)],
                axis=0,
            )
            down_ref[h * half + c * lane : h * half + (c + 1) * lane, :] = down.T


def unpack_ffn(info, everyone):
    rows, part = everyone.shape[2:]
    lane = part // 3
    return pl.pallas_call(
        unpack_ffn_kernel,
        in_specs=[pl.BlockSpec()],
        out_specs=[pl.BlockSpec()] * 3,
        out_shape=[
            shape((rows, 2 * BLOCKS * CHUNKS * lane), jnp.float32),
            shape((rows, 2 * BLOCKS * CHUNKS * lane), jnp.float32),
            shape((2 * CHUNKS * lane, BLOCKS * rows), jnp.float32),
        ],
        compiler_params=params(),
        cost_estimate=cost(0, 16 << 20),
    )(everyone)


def shards(sizes, *arrays):
    (
        tokens, segments, cotangent, attn_gain, w_query, key_matrix, value_matrix, w_out, ffn_gain,
        w_gate, w_up, w_down,
    ) = arrays
    ny, nx, nz = sizes
    tuned = (ny, nx) == (2, 2)
    core, xi = lax.axis_index("core"), lax.axis_index("x")
    place = lax.axis_index("y") * nx + xi
    info = jnp.stack([core, place, lax.axis_index("z"), xi]).astype(jnp.int32)
    tokens, cotangent, ids = tokens[0], cotangent[0], segments[0]
    rows, width = tokens.shape
    own_rows = w_query.shape[0]

    gains = jnp.stack([attn_gain, ffn_gain])
    attn_own, *attn_piece = pack_attn(
        info, (w_query, key_matrix, value_matrix, w_out), gains, tuned
    )
    ids = behind(ids, (attn_own,))
    if tuned:
        past_ids = lax.ppermute(ids, "x", [(0, 1)])
        past_ids = jnp.where(xi == 1, past_ids, jnp.iinfo(jnp.int32).max)
        all_ids = jnp.concatenate([ids, past_ids])
    else:
        all_ids = lax.all_gather(ids, "x", axis=0, tiled=True)
    first = jnp.sum((all_ids[:, None] < ids[None, :]).astype(jnp.int32), axis=0)
    firsts = jnp.concatenate([first[None], swap_core(first[None])])
    token_place = xi * rows + jnp.arange(rows, dtype=jnp.int32)
    positions = (token_place[None] - firsts).reshape(-1)
    angles = inverse_freq()[:, None] * positions.astype(jnp.float32)[None, :]
    cosine, sine = jnp.cos(angles), jnp.sin(angles)
    size = rows // 2
    starts = firsts.reshape(2, rows // size, size)[:, :, 0] // size
    info = jnp.concatenate([info, starts.reshape(-1)])
    firsts = firsts[:, None, :]

    ffn_own, *ffn_piece = pack_ffn(info, w_gate, w_up, w_down, (cosine, sine, firsts), tuned)
    tokens_sent, cotangent_sent, _ = lax.optimization_barrier((tokens, cotangent, ffn_own))
    tokens_other, cotangent_other = swap_core(jnp.stack([tokens_sent, cotangent_sent]))
    cotangent_turned, cotangent_turned_other = cotangent_sent.T, cotangent_other.T
    if tuned:
        cut = own_rows // 2
        slots = travel_z(attn_piece[0], sizes)
        stack = jnp.stack([s[:own_rows] for s in slots])
        tables = (tokens_other, cotangent_turned, cotangent_turned_other)
        parts = [lax.all_gather(behind(piece, (stack,)), "z", axis=0) for piece in ffn_piece]
        ffn_stacks = list(pick(info, parts[:1], ((0, 0, 0, own_rows, 0),), own_rows, tables))
        ffn_stacks += pick(
            info,
            parts,
            ((0, 0, own_rows, own_rows + cut, 0), (0, 1, 0, cut, cut), (1, 1, cut, cut + own_rows, 0)),
            own_rows,
            (),
        )
        stacks = (
            stack,
            lax.ppermute(stack, "x", PAIR),
            lax.ppermute(stack, "y", PAIR),
            lax.ppermute(stack, ("y", "x"), [(i, 3 - i) for i in range(4)]),
        )
        weights, weights_tail = assemble(info, attn_own, stacks, nz, ffn_stacks[:1])
        ffn_weights = ffn_own
        gains = [gains.astype(low_type)] + [s[own_rows : own_rows + 2, :own_rows] for s in slots]
        gains = jnp.stack(gains[::-1] + gains[::-1])
        gains = lax.dynamic_slice_in_dim(gains, nz - 1 - lax.axis_index("z"), nz, 0)
        gains = gains.transpose(1, 0, 2).reshape(2, width)
    else:
        weights = gather_whole(attn_own)
        weights_tail = weights[BLOCKS // 2 :]
        ffn_pieces = [()] * CHUNKS
        before_attend = before_out = ()
        ffn_weights = jnp.stack([gather_whole(ffn_own[c]) for c in range(CHUNKS)])
        gains = lax.all_gather(gains.astype(low_type), "z", axis=1, tiled=True)
    gain_one, gain_two = gains[:1].astype(jnp.float32), gains[1:].astype(jnp.float32)

    cs = (cotangent, cotangent_other)
    cts = (cotangent_turned, cotangent_turned_other)

    normed, query, keyvalue = project(
        tokens, tokens_other, gain_one, weights, cosine, sine
    )
    weights_other = swap_core(weights_tail)
    if tuned:
        first_x, first_y = (lax.ppermute(ffn_stacks[0], axis, PAIR) for axis in ("x", "y"))
        past = lax.ppermute(behind(keyvalue, (first_x, first_y)), "x", [(0, 1)])[None]
        by_x = [first_x] + [lax.ppermute(s, "x", PAIR) for s in ffn_stacks[1:]]
        by_y = [first_y] + [lax.ppermute(s, "y", PAIR) for s in ffn_stacks[1:]]
        far = [
            lax.ppermute(by_x[0], "y", PAIR),
            lax.ppermute(by_x[1], "y", PAIR),
            lax.ppermute(by_y[2], "x", PAIR),
        ]
        ffn_pieces = list(zip(ffn_stacks, by_x, by_y, far))
        before_attend = (*ffn_stacks[1:], far[0])
        before_out = (*by_x[1:], *by_y[1:])
    else:
        past = lax.all_gather(keyvalue, "x", axis=0)
    attended, log_total = attend(info, query, keyvalue, past, firsts, size, before_attend)
    came = swap_core(attended[:, rows:].astype(low_type))
    middle, *normed_parts, out_rows = project_out(
        info, attended, came, weights, weights_other, tokens, gain_two, before_out
    )

    normed_parts = [list(normed_parts[:2]), list(normed_parts[2:])]
    xs, xts = (parts + [swap_core(part) for part in parts] for parts in normed_parts)
    sent, first, send, second, reduced = ([None] * (CHUNKS + 1) for _ in range(5))
    ways = ["xy", "xy", "z"] if tuned else ["whole"] * CHUNKS
    (result, grad_normed_two, result_other, grad_other), sent[:3] = feed_forward(
        info, xs, cs, xts, cts, ffn_weights, ffn_pieces, ways, tuned, ()
    )
    if tuned:
        rows_two = lax.psum_scatter(sent[2][0], "z", scatter_dimension=0, tiled=True)[0]
        reduced[2] = lax.psum_scatter(rows_two, ("y", "x"), scatter_dimension=0, tiled=True)[0]
    first[0] = scatter_first(sent[0])

    grad_normed_two = grad_normed_two + swap_core(grad_other).astype(jnp.float32)
    result = result + swap_core(result_other).astype(jnp.float32)
    scale_two = norm_scale(middle)
    grad_gain_two = jnp.sum(grad_normed_two * middle * scale_two, axis=0)
    grad_middle = cotangent.astype(jnp.float32) + norm_back(
        grad_normed_two * gain_two, middle, scale_two
    )
    grad_branch = grad_middle.astype(low_type)
    output = (middle + result).astype(low_type)

    grad_other = [swap_core(grad_branch[i * rows // 2 : (i + 1) * rows // 2]) for i in range(2)]
    grad_attended, delta, grad_rows = branch(
        grad_branch, grad_other, out_rows, attended, ()
    )
    hq = HALF_QUERY
    mine = lax.dynamic_slice_in_dim(grad_rows, core * hq, hq, 1)
    other = swap_core(lax.dynamic_slice_in_dim(grad_rows, (1 - core) * hq, hq, 1))
    send[0] = scatter_sums(sent[0], first[0], (grad_attended,))
    second[0] = scatter_second(send[0])
    first[1] = scatter_first([behind(value, send[0]) for value in sent[1]])
    grad_query, grad_kv, grad_past = attend_back(
        info, query, keyvalue, past, grad_attended, firsts, log_total, delta, size,
        send[0],
    )
    if tuned:
        came = lax.ppermute(behind(grad_past[0], (*second[0], *first[1], other)), "x", [(1, 0)])
    else:
        came = lax.psum_scatter(grad_past, "x", scatter_dimension=0, tiled=True)[0]
    reduced[0] = scatter_mine(info, sent[0], first[0], second[0], (grad_past,), sizes)
    send[1] = scatter_sums(sent[1], first[1], (grad_past,))
    second[1] = scatter_second(send[1])
    last = (came, rows_two) if tuned else (came,)
    reduced[1] = scatter_mine(info, sent[1], first[1], second[1], last, sizes)
    grad_projected, *attn_sent = attn_grads(
        info, grad_query, grad_kv, came, cosine, sine, normed, mine, other,
        (reduced[0], reduced[1]) if tuned else (), tuned,
    )
    normed_mine, normed_other = normed_grad(grad_projected, weights, ())
    grad_normed = normed_mine + swap_core(normed_other).astype(jnp.float32)
    inputs = tokens.astype(jnp.float32)
    scale_one = norm_scale(inputs)
    grad_gain_one = jnp.sum(grad_normed * inputs * scale_one, axis=0)
    grad_inputs = (
        grad_middle + norm_back(grad_normed * gain_one, inputs, scale_one)
    ).astype(low_type)


    sent[3], first[3] = attn_sent, scatter_first(attn_sent)
    last = (normed_mine,)
    send[3] = scatter_sums(sent[3], first[3], last)
    second[3] = scatter_second(send[3])
    if tuned:
        pieces = merge(info, sent[3], first[3], second[3], nz)
        reduced[3] = scatter_z(pieces, sizes)
        last = pieces[:1]
    else:
        reduced[2] = scatter_rows(scatter_mine(info, sent[2], (), (), last, sizes))
        reduced[3] = scatter_rows(scatter_mine(info, sent[3], (), (), last, sizes))
    attn_out = unpack_attn(info, *spread(reduced[3][None], sizes))
    ffn_total = [scatter_rows(reduced[0]), scatter_rows(reduced[1]), reduced[2]]
    ffn_total = jnp.stack(lax.optimization_barrier((*ffn_total, *last))[:CHUNKS])
    grad_w_gate, grad_w_up, grad_w_down = unpack_ffn(info, *gather_all(ffn_total, sizes))
    gain_grads = jnp.stack([grad_gain_one, grad_gain_two])
    if tuned:
        gain_grads = behind(gain_grads, pieces[:1])
    for axis, count in (("core", 2), ("x", nx), ("y", ny), ("z", nz)):
        gain_grads = sum_over(gain_grads, axis, count)
    gain_grads = lax.dynamic_slice_in_dim(gain_grads, lax.axis_index("z") * own_rows, own_rows, 1)
    return (
        output[None], grad_inputs[None], gain_grads[0], *attn_out, gain_grads[1], grad_w_gate,
        grad_w_up, grad_w_down,
    )


def solution(mesh):
    dp, ctx, fsdp = (mesh.shape[name] for name in ("dp", "ctx", "fsdp"))
    fine = Mesh(mesh.devices.reshape(dp // 2, 2, ctx, fsdp), ("y", "core", "x", "z"))
    sizes = (dp // 2, ctx, fsdp)
    wide = P(("y", "core", "z"), "x", None)
    matrix, vector = P("z", None), P("z")
    in_specs = (
        wide, P(("y", "core", "z"), "x"), wide, vector, matrix, matrix, matrix, matrix, vector,
        matrix, matrix, matrix,
    )
    out_specs = (
        wide, wide, vector, matrix, matrix, matrix, matrix, vector, matrix, matrix, matrix
    )

    def layer(*arrays):
        return shards(sizes, *arrays)

    return jax.shard_map(
        layer, mesh=fine, in_specs=in_specs, out_specs=out_specs, check_vma=False
    )
```

```python
import math

import jax
import jax.numpy as jnp
from jax import lax
from jax.experimental import pallas as pl
from jax.experimental.pallas import tpu as pltpu
from jax.sharding import Mesh
from jax.sharding import PartitionSpec as P

QUERY_HEADS = 18
KEY_VALUE_HEADS = 6
HEAD_WIDTH = 64
TURN = HEAD_WIDTH // 2
GROUP = QUERY_HEADS // KEY_VALUE_HEADS
GROUPS = KEY_VALUE_HEADS // 2
HALF_QUERY = QUERY_HEADS // 2 * HEAD_WIDTH
HALF_KEY = GROUPS * HEAD_WIDTH
CHUNKS = 3
BLOCKS = 4
GAIN_ROWS = 16
FFN_ROWS = 512
COST = 0.1

low_type = jnp.bfloat16
eps_norm = 1e-05
masked_score = -1e30
lowest_peak = -1e20
LOG2E = math.log2(math.e)
SCORE_SCALE = HEAD_WIDTH ** (-0.5)
VMEM_LIMIT = 58 * 1024 * 1024

PAIR = [(0, 1), (1, 0)]
ANY = pl.BlockSpec(memory_space=pl.ANY)
SCALARS = pl.BlockSpec(memory_space=pltpu.SMEM)


def inverse_freq():
    return 10000.0 ** (-(jnp.arange(TURN, dtype=jnp.float32) * 2.0) / HEAD_WIDTH)


def norm_scale(value):
    return lax.rsqrt(jnp.mean(value * value, axis=-1, keepdims=True) + eps_norm)


def norm_back(scaled, value, scale):
    return scale * scaled - value * scale**3 * jnp.mean(scaled * value, axis=-1, keepdims=True)


def dot(left, right, over=(1, 0)):
    return lax.dot_general(
        left, right, (((over[0],), (over[1],)), ((), ())), preferred_element_type=jnp.float32
    )


def swap_core(value):
    return lax.ppermute(value, "core", PAIR)


def behind(value, others):
    return lax.optimization_barrier((value, *others))[0]


def ignoring(kernel, given, after):
    def wrapped(*refs):
        kernel(*refs[:given], *refs[given + len(after) :])

    return wrapped


def params():
    return pltpu.CompilerParams(vmem_limit_bytes=VMEM_LIMIT)


def cost(flops, moved, special=0):
    return pl.CostEstimate(
        flops=int(flops * COST), bytes_accessed=int(moved * COST), transcendentals=int(special * COST)
    )


def shape(dims, kind=low_type):
    return jax.ShapeDtypeStruct(tuple(dims), kind)


def pack_attn_kernel(info, q_ref, k_ref, v_ref, o_ref, gain_ref, own_ref, *piece_ref):
    def half(ref):
        size = ref.shape[1] // 2
        value = ref[...].astype(low_type)
        return jnp.where(info[0] == 0, value[:, :size], value[:, size:])

    own_ref[...] = jnp.concatenate([half(r) for r in (q_ref, k_ref, v_ref, o_ref)], axis=1)
    rows = own_ref.shape[0]
    for ref in piece_ref:
        part = ref.shape[1]
        ref[:rows, :] = own_ref[:, pl.ds(pl.multiple_of(info[1] * part, part), part)]
        gains = jnp.concatenate([gain_ref[...], jnp.zeros((GAIN_ROWS - 2, rows), jnp.float32)], axis=0)
        gains = jnp.concatenate([gains, jnp.zeros((GAIN_ROWS, part - rows), jnp.float32)], axis=1)
        ref[rows:, :] = gains.astype(low_type)


def pack_attn(info, arrays, gains, tuned):
    rows = arrays[0].shape[0]
    width = sum(a.shape[1] for a in arrays) // 2
    outs = [shape((rows, width))] + [shape((rows + GAIN_ROWS, width // BLOCKS))] * tuned
    return pl.pallas_call(
        pack_attn_kernel,
        in_specs=[SCALARS] + [pl.BlockSpec()] * 5,
        out_specs=[pl.BlockSpec()] * len(outs),
        out_shape=outs,
        compiler_params=params(),
        cost_estimate=cost(0, rows * width * 10),
    )(info, *arrays, gains)


def pack_ffn_kernel(info, gate_ref, up_ref, down_ref, own_ref, *piece_ref):
    step, steps = pl.program_id(0), pl.num_programs(0)
    part = gate_ref.shape[1] // CHUNKS
    rows = gate_ref.shape[0]
    blocks = own_ref.shape[2] // part // 3
    for c in range(CHUNKS):
        at = slice(c * part, (c + 1) * part)
        here = pl.ds(pl.multiple_of(step * part, part), part)
        own_ref[c, :, here] = gate_ref[:, at].astype(low_type)
        there = pl.ds(pl.multiple_of((blocks + step) * part, part), part)
        own_ref[c, :, there] = up_ref[:, at].astype(low_type)

    @pl.when(step == 0)
    def _():
        turned = down_ref[...].astype(low_type).T
        for c in range(CHUNKS):
            for q in range(blocks):
                own_ref[c, :, (2 * blocks + q) * part : (2 * blocks + q + 1) * part] = turned[
                    q * rows : (q + 1) * rows, c * part : (c + 1) * part
                ]

    @pl.when(step == steps - 1)
    def _():
        if piece_ref:
            one, two = piece_ref
            size, cut = one.shape[1], rows // 2
            at = pl.ds(pl.multiple_of(info[1] * size, size), size)
            one[:rows, :] = own_ref[0, :, at]
            one[rows:, :] = own_ref[1, :cut, at]
            two[:cut, :] = own_ref[1, cut:, at]
            two[cut:, :] = own_ref[2, :, at]


def pack_ffn(info, gate, up, down, after, tuned):
    rows, hidden = gate.shape
    hidden_rows, width = down.shape
    steps = hidden // hidden_rows
    half = hidden_rows // 2
    packed = 3 * steps * (half // CHUNKS)
    part = packed // BLOCKS
    outs = [shape((CHUNKS, rows, packed))]
    if tuned:
        outs += [shape((rows + rows // 2, part))] * 2
    columns = pl.BlockSpec((rows, half), lambda z, info: (0, 2 * z + info[0]))
    return pl.pallas_call(
        ignoring(pack_ffn_kernel, 4, after),
        grid_spec=pltpu.PrefetchScalarGridSpec(
            num_scalar_prefetch=1,
            grid=(steps,),
            in_specs=[columns, columns, pl.BlockSpec((half, width), lambda z, info: (info[0], 0))]
            + [ANY] * len(after),
            out_specs=[
                pl.BlockSpec(o.shape, lambda z, info, n=len(o.shape): (0,) * n) for o in outs
            ],
        ),
        out_shape=outs,
        compiler_params=params(),
        cost_estimate=cost(0, rows * packed * CHUNKS * 6),
    )(info, gate, up, down, *after)


def ring(count, step):
    return [(i, (i + step) % count) for i in range(count)]


def place_pieces(info, count, own, stacks, forward, out_ref, sems):
    rows, part = own.shape[0], out_ref.shape[2]
    copies = []

    def begin(source, block, row):
        target = out_ref.at[block, pl.ds(pl.multiple_of(row * rows, rows), rows), :]
        copies.append(pltpu.make_async_copy(source, target, sems.at[len(copies)]))
        copies[-1].start()

    for b in range(BLOCKS):
        begin(own.at[:, b * part : (b + 1) * part], b, info[2])
    for flip, stack in enumerate(stacks):
        for k in range(1, count):
            row = lax.rem(info[2] + (k if forward else count - k), count)
            begin(stack.at[k - 1], jnp.bitwise_xor(info[1], flip), row)
    return copies


def assemble(info, own, stacks, count, after):
    rows, width = own.shape
    out = shape((BLOCKS, rows * count, width // BLOCKS))

    def kernel(info, own_ref, *refs):
        *stack_refs, out_ref, tail_ref, sems = refs
        for copy in place_pieces(info, count, own_ref, stack_refs, False, out_ref, sems):
            copy.wait()
        tail_ref[...] = out_ref[BLOCKS // 2 :]

    return pl.pallas_call(
        ignoring(kernel, 2 + len(stacks), after),
        in_specs=[SCALARS] + [ANY] * (1 + len(stacks) + len(after)),
        out_specs=[pl.BlockSpec()] * 2,
        out_shape=[out, shape((BLOCKS // 2, *out.shape[1:]))],
        scratch_shapes=[pltpu.SemaphoreType.DMA((BLOCKS * count,))],
        compiler_params=params(),
        cost_estimate=cost(0, rows * width * count * 4),
    )(info, own, *stacks, *after)


def pick_kernel(parts, info, *refs):
    ins = refs[: -1 - len({p[0] for p in parts})]
    outs, sems = refs[len(ins) : -1], refs[-1]
    copies = []
    for out, source, start, stop, at in parts:
        count = ins[source].shape[0]
        for k in range(1, count):
            rows = ins[source].at[lax.rem(info[2] + k, count), start:stop]
            target = outs[out].at[k - 1, at : at + stop - start]
            copies.append(pltpu.make_async_copy(rows, target, sems.at[len(copies)]))
            copies[-1].start()
    for copy in copies:
        copy.wait()


def pick(info, arrays, parts, rows, after):
    count, _, part = arrays[0].shape
    outs = [shape((count - 1, rows, part))] * len({p[0] for p in parts})

    def kernel(*refs):
        pick_kernel(parts, *refs)

    return pl.pallas_call(
        ignoring(kernel, 1 + len(arrays), after),
        in_specs=[SCALARS] + [ANY] * (len(arrays) + len(after)),
        out_specs=[pl.BlockSpec()] * len(outs),
        out_shape=outs,
        scratch_shapes=[pltpu.SemaphoreType.DMA((len(parts) * (count - 1),))],
        compiler_params=params(),
        cost_estimate=cost(0, len(outs) * count * rows * part * 4),
    )(info, *arrays, *after)


def travel_z(piece, sizes):
    return [lax.ppermute(piece, "z", ring(sizes[2], k)) for k in range(1, sizes[2])]


def gather_whole(own):
    full = lax.all_gather(own, "z", axis=0, tiled=True)
    return full.reshape(full.shape[0], BLOCKS, -1).transpose(1, 0, 2)


def send_out(info, packed, outs, way, sems):
    copies = []

    def begin(source, target):
        copies.append(pltpu.make_async_copy(source, target, sems.at[len(copies)]))
        copies[-1].start()

    if way == "whole":
        begin(packed, outs[0])
    elif way == "z":
        count, _, rows, _ = outs[0].shape
        for z in range(count):
            for b in range(BLOCKS):
                begin(packed.at[b, z * rows : (z + 1) * rows], outs[0].at[z, b])
    else:
        keep_one, send_one, keep_two, send_two = outs
        cut = packed.shape[1] // 2
        y, x = lax.div(info[1], 2), lax.rem(info[1], 2)
        for i in range(2):
            at_y, at_x = jnp.bitwise_xor(y, i), jnp.bitwise_xor(x, i)
            begin(packed.at[at_y * 2 + x, :cut], keep_one.at[i])
            begin(packed.at[at_y * 2 + 1 - x, :cut], send_one.at[i])
            begin(packed.at[y * 2 + at_x, cut:], keep_two.at[i])
            begin(packed.at[(1 - y) * 2 + at_x, cut:], send_two.at[i])
    return copies


def sent_shapes(rows, part, way):
    if way == "xy":
        return [shape((2, rows // 2, part))] * 4
    if way == "z":
        return [shape((BLOCKS, BLOCKS, rows // BLOCKS, part))]
    return [shape((BLOCKS, rows, part))]


def add_low(kept, came):
    return (kept.astype(jnp.float32) + came.astype(jnp.float32)).astype(low_type)


def scatter_first(outs):
    if len(outs) == 1:
        return ()
    return lax.ppermute(outs[1], "x", PAIR), lax.ppermute(outs[3], "y", PAIR)


def scatter_sums(outs, came, last):
    if len(outs) == 1:
        return ()
    came = lax.optimization_barrier((*came, *last))
    return add_low(outs[0][1], came[0][1]), add_low(outs[2][1], came[1][1])


def scatter_second(sums):
    if len(sums) == 0:
        return ()
    return lax.ppermute(sums[0], "y", PAIR), lax.ppermute(sums[1], "x", PAIR)


def merge_kernel(more, info, *refs):
    parts, outs, mine_s = refs[:6], refs[6 + more : -1], refs[-1]
    cut = mine_s.shape[0] // 2
    rows = mine_s.shape[0] // len(outs)
    for i in range(2):
        kept, came, second = (ref[...].astype(jnp.float32) for ref in parts[3 * i : 3 * i + 3])
        mine_s[i * cut : (i + 1) * cut, :] = (kept[0] + came[0] + second).astype(low_type)
    for k, out in enumerate(outs):
        z = lax.rem(info[2] + k, len(outs)) if len(outs) > 1 else 0
        out[:rows, :] = mine_s[pl.ds(z * rows, rows), :]
        if more:
            out[rows:, :] = refs[6][z]


def merge(info, outs, first, second, count, more=()):
    cut, part = second[0].shape
    half = pl.BlockSpec((1, cut, part), lambda i: (0, 0, 0))
    whole = pl.BlockSpec((cut, part), lambda i: (0, 0))
    rows = 2 * cut // count + sum(m.shape[1] for m in more)

    def kernel(*refs):
        merge_kernel(len(more), *refs)

    return pl.pallas_call(
        kernel,
        grid=(1,),
        in_specs=[SCALARS] + [half, half, whole] * 2
        + [pl.BlockSpec(m.shape, lambda i: (0, 0, 0)) for m in more],
        out_specs=[pl.BlockSpec((rows, part), lambda i: (0, 0))] * count,
        out_shape=[shape((rows, part))] * count,
        scratch_shapes=[pltpu.VMEM((2 * cut, part), low_type)],
        compiler_params=params(),
        cost_estimate=cost(0, 16 * cut * part),
    )(info, outs[0], first[0], second[0], outs[2], first[1], second[1], *more)


def scatter_mine(info, outs, first, second, last, sizes):
    ny, nx, nz = sizes
    if len(outs) == 1:
        packed = outs[0]
        total = packed.shape[1]
        split = packed.transpose(1, 0, 2).reshape(total, ny * nx, -1).transpose(1, 0, 2)
        return lax.psum_scatter(split, ("y", "x"), scatter_dimension=0, tiled=True)[0]
    return merge(info, outs, first, lax.optimization_barrier((*second, *last))[: len(second)], 1)[0]


def send_z(pieces, sizes):
    return [lax.ppermute(o, "z", ring(sizes[2], k + 1)) for k, o in enumerate(pieces[1:])]


def sum_z(mine, came):
    return sum((c.astype(jnp.float32) for c in came), mine.astype(jnp.float32)).astype(low_type)


def scatter_rows(mine):
    return lax.psum_scatter(mine, "z", scatter_dimension=0, tiled=True)


def spread(total, sizes):
    if sizes[0] * sizes[1] == BLOCKS:
        mine = [
            total,
            lax.ppermute(total, "x", PAIR),
            lax.ppermute(total, "y", PAIR),
            lax.ppermute(total, ("y", "x"), [(i, 3 - i) for i in range(4)]),
        ]
        return mine, [swap_core(value) for value in mine]
    everyone = jnp.moveaxis(lax.all_gather(total, ("y", "x"), axis=0), 0, -2)
    everyone = jnp.moveaxis(everyone.reshape(total.shape[:2] + (BLOCKS, -1)), -2, 0)
    place = lax.axis_index("y") * sizes[1] + lax.axis_index("x")
    mine = [
        lax.dynamic_index_in_dim(everyone, (place % BLOCKS) ^ i, 0, False) for i in range(BLOCKS)
    ]
    return mine, [swap_core(value) for value in mine]


def gather_all(total, sizes):
    everyone = lax.all_gather(total, ("core", "y", "x"), axis=0)
    count = sizes[0] * sizes[1]
    if count == BLOCKS:
        return (everyone,)
    both = jnp.moveaxis(everyone.reshape((2, count) + total.shape), 1, -2)
    both = jnp.moveaxis(both.reshape((2,) + total.shape[:2] + (BLOCKS, -1)), -2, 1)
    return (both.reshape((2 * BLOCKS,) + both.shape[2:]),)


def turn_heads(ref, value, cosine, sine, start):
    for h in range(value.shape[0] // HEAD_WIDTH):
        former = value[h * HEAD_WIDTH : h * HEAD_WIDTH + TURN]
        latter = value[h * HEAD_WIDTH + TURN : (h + 1) * HEAD_WIDTH]
        at = start + h * HEAD_WIDTH
        ref[at : at + TURN, :] = (former * cosine - latter * sine).astype(ref.dtype)
        ref[at + TURN : at + HEAD_WIDTH, :] = (latter * cosine + former * sine).astype(ref.dtype)


def project_kernel(mine_ref, other_ref, gain_ref, w_ref, cos_ref, sin_ref, normed_ref, q_ref, kv_ref):
    rows = mine_ref.shape[0]
    hk, part = HALF_KEY, w_ref.shape[2]
    for i, ref in enumerate((mine_ref, other_ref)):
        value = ref[...].astype(jnp.float32)
        normed = (value * norm_scale(value) * gain_ref[...]).astype(low_type)
        at = slice(i * rows, (i + 1) * rows)
        normed_ref[:, at] = normed.T
    weights = [w_ref[0].T, w_ref[1].T, w_ref[2].T[:hk]]
    for i in range(2):
        at = slice(i * rows, (i + 1) * rows)
        normed = normed_ref[:, at]
        cosine, sine = cos_ref[:, at], sin_ref[:, at]
        first = dot(weights[0], normed)
        turn_heads(q_ref.at[:, at], first, cosine, sine, 0)
        second = dot(weights[1], normed)
        turn_heads(q_ref.at[:, at], second[: part - hk], cosine, sine, part)
        turn_heads(kv_ref.at[0, :, at], second[part - hk :], cosine, sine, 0)
        kv_ref[1, :, at] = dot(weights[2], normed).astype(low_type)


def project(mine, other, gain, weights, cosine, sine):
    rows, width = mine.shape
    return pl.pallas_call(
        project_kernel,
        in_specs=[pl.BlockSpec()] * 6,
        out_specs=[pl.BlockSpec()] * 3,
        out_shape=[
            shape((width, 2 * rows)), shape((HALF_QUERY, 2 * rows)), shape((2, HALF_KEY, 2 * rows))
        ],
        compiler_params=params(),
        cost_estimate=cost(4 * rows * width * 960, 14 << 20),
    )(mine, other, gain, weights, cosine, sine)


def tile_mask(first, place0, key0, size, causal):
    key_place = key0 + lax.broadcasted_iota(jnp.int32, (size, size), 0)
    allowed = key_place >= first
    if causal:
        place = place0 + lax.broadcasted_iota(jnp.int32, (size, size), 1)
        allowed = allowed & (key_place <= place)
    return jnp.concatenate([allowed] * GROUP, axis=1)


def heads_of(ref):
    return jnp.concatenate(
        [ref[r * HEAD_WIDTH : (r + 1) * HEAD_WIDTH, :] for r in range(GROUP)], axis=1
    )


def over_tiles(info, size, rows, turn):
    per = rows // size
    half = pl.program_id(2)
    own = info[3] * per
    hi = own + half
    lo = info[4 + pl.program_id(0) * per + half]

    def columns(b):
        return pl.ds(pl.multiple_of(lax.rem(b, per) * size, size), size)

    def earlier(b, _):
        turn(hi, b, lax.div(b, per), columns(b))
        return 0

    def here(b, _):
        turn(hi, b, None, columns(b))
        return 0

    lax.fori_loop(lo, own, earlier, 0)
    lax.fori_loop(jnp.maximum(lo, own), hi + 1, here, 0)


def attend_kernel(info, q_ref, kv_ref, past_ref, first_ref, o_ref, total_ref, peak_s, sum_s, acc_s):
    size, rows = q_ref.shape[1], kv_ref.shape[2]
    q = heads_of(q_ref)
    peak_s[...] = jnp.full(peak_s.shape, lowest_peak, jnp.float32)
    sum_s[...] = jnp.zeros(sum_s.shape, jnp.float32)
    acc_s[...] = jnp.zeros(acc_s.shape, jnp.float32)

    def turn(hi, b, past, at):
        k = kv_ref[0, :, at] if past is None else past_ref[past, 0, :, at]
        v = kv_ref[1, :, at] if past is None else past_ref[past, 1, :, at]
        allowed = tile_mask(first_ref[0], hi * size, b * size, size, past is None)
        scores = dot(k, q, (0, 0)) * (SCORE_SCALE * LOG2E)
        scores = jnp.where(allowed, scores, masked_score)
        peak = peak_s[...]
        fresh = jnp.maximum(peak, jnp.max(scores, axis=0, keepdims=True))
        shrink = jnp.exp2(peak - fresh)
        terms = jnp.exp2(scores - fresh)
        peak_s[...] = fresh
        sum_s[...] = sum_s[...] * shrink + jnp.sum(terms, axis=0, keepdims=True)
        acc_s[...] = acc_s[...] * shrink + dot(v, terms.astype(low_type))

    over_tiles(info, size, rows, turn)
    total = sum_s[...]
    mixed = acc_s[...] / total
    log_total = peak_s[...] + jnp.log2(total)
    for r in range(GROUP):
        o_ref[r * HEAD_WIDTH : (r + 1) * HEAD_WIDTH, :] = mixed[:, r * size : (r + 1) * size]
        total_ref[0, r : r + 1, :] = log_total[:, r * size : (r + 1) * size]


def attend_back_kernel(
    info, q_ref, kv_ref, past_ref, g_ref, first_ref, total_ref, delta_ref, dq_ref, dkv_ref, dpast_ref,
    acc_s, past_s,
):
    size, rows = q_ref.shape[1], kv_ref.shape[2]
    q = heads_of(q_ref)
    g = heads_of(g_ref)
    total = jnp.concatenate([total_ref[0, r : r + 1, :] for r in range(GROUP)], axis=1)
    delta = jnp.concatenate([delta_ref[0, r : r + 1, :] for r in range(GROUP)], axis=1)
    acc_s[...] = jnp.zeros(acc_s.shape, jnp.float32)

    @pl.when(pl.program_id(2) == 0)
    def _():
        dkv_ref[...] = jnp.zeros(dkv_ref.shape, jnp.float32)
        past_s[...] = jnp.zeros(past_s.shape, jnp.float32)

    def turn(hi, b, past, at):
        k = kv_ref[0, :, at] if past is None else past_ref[past, 0, :, at]
        v = kv_ref[1, :, at] if past is None else past_ref[past, 1, :, at]
        allowed = tile_mask(first_ref[0], hi * size, b * size, size, past is None)
        scores = dot(k, q, (0, 0)) * (SCORE_SCALE * LOG2E)
        weights = jnp.exp2(jnp.where(allowed, scores - total, masked_score))
        grad_weights = dot(v, g, (0, 0))
        grad_scores = (weights * (grad_weights - delta) * SCORE_SCALE).astype(low_type)
        dk = dot(q, grad_scores, (1, 1))
        dv = dot(g, weights.astype(low_type), (1, 1))
        if past is None:
            dkv_ref[0, :, at] += dk
            dkv_ref[1, :, at] += dv
        else:
            past_s[past, 0, :, at] += dk
            past_s[past, 1, :, at] += dv
        acc_s[...] += dot(k, grad_scores)

    over_tiles(info, size, rows, turn)
    acc = acc_s[...]
    for r in range(GROUP):
        dq_ref[r * HEAD_WIDTH : (r + 1) * HEAD_WIDTH, :] = acc[:, r * size : (r + 1) * size]

    @pl.when(pl.program_id(2) == pl.num_programs(2) - 1)
    def _():
        dpast_ref[...] = past_s[...].astype(low_type)


def attention_specs(parts, rows, size):
    per = rows // size
    wide = pl.BlockSpec((GROUP * HEAD_WIDTH, size), lambda s, g, h: (g, s * per + h))
    own = pl.BlockSpec((2, HEAD_WIDTH, rows), lambda s, g, h: (0, g, s))
    past = pl.BlockSpec((parts, 2, HEAD_WIDTH, rows), lambda s, g, h: (0, 0, g, s))
    first = pl.BlockSpec((1, 1, size), lambda s, g, h: (s, 0, h))
    stat = pl.BlockSpec((1, 8, size), lambda s, g, h: (g, 0, s * per + h))
    return (2, GROUPS, per), wide, own, past, first, stat


def attend(info, query, keyvalue, past, first, size, after):
    both = keyvalue.shape[2]
    rows = both // 2
    grid, wide, own, past_spec, first_spec, stat = attention_specs(past.shape[0], rows, size)
    pairs = 2 * rows * rows * 3 // 2
    return pl.pallas_call(
        ignoring(attend_kernel, 5, after),
        grid=grid,
        in_specs=[SCALARS, wide, own, past_spec, first_spec] + [ANY] * len(after),
        out_specs=[wide, stat],
        out_shape=[shape(query.shape, jnp.float32), shape((GROUPS, 8, both), jnp.float32)],
        scratch_shapes=[
            pltpu.VMEM((1, GROUP * size), jnp.float32),
            pltpu.VMEM((1, GROUP * size), jnp.float32),
            pltpu.VMEM((HEAD_WIDTH, GROUP * size), jnp.float32),
        ],
        compiler_params=params(),
        cost_estimate=cost(pairs * 9 * 64 * 4 * 5, 8 << 20, pairs * 9),
    )(info, query, keyvalue, past, first, *after)


def attend_back(info, query, keyvalue, past, grad, first, log_total, delta, size, after):
    both = keyvalue.shape[2]
    rows = both // 2
    grid, wide, own, past_spec, first_spec, stat = attention_specs(past.shape[0], rows, size)
    pairs = 2 * rows * rows * 3 // 2
    return pl.pallas_call(
        ignoring(attend_back_kernel, 8, after),
        grid=grid,
        in_specs=[SCALARS, wide, own, past_spec, wide, first_spec, stat, stat] + [ANY] * len(after),
        out_specs=[wide, own, past_spec],
        out_shape=[
            shape(query.shape, jnp.float32), shape(keyvalue.shape, jnp.float32), shape(past.shape)
        ],
        scratch_shapes=[
            pltpu.VMEM((HEAD_WIDTH, GROUP * size), jnp.float32),
            pltpu.VMEM((past.shape[0], 2, HEAD_WIDTH, rows), jnp.float32),
        ],
        compiler_params=params(),
        cost_estimate=cost(pairs * 9 * 64 * 10 * 3, 12 << 20, pairs * 9),
    )(info, query, keyvalue, past, grad, first, log_total, delta, *after)


def place_out(core, mine_ref, other_ref, out_ref):
    cut, part = HALF_KEY, mine_ref.shape[2]
    mine = jnp.concatenate([mine_ref[0][:, cut:], mine_ref[1]], axis=1)
    other = jnp.concatenate([other_ref[0][:, cut:], other_ref[1]], axis=1)
    out_ref[...] = jnp.where(
        core == 0,
        jnp.concatenate([mine, other], axis=1),
        jnp.concatenate([other, mine], axis=1),
    )


def out_kernel(
    info, mine_ref, came_ref, w_ref, w_other_ref, tokens_ref, gain_ref, middle_ref, *refs
):
    normed_refs, turned_refs, (rows_ref, w_s) = refs[:2], refs[2:4], refs[4:]
    place_out(info[0], w_ref, w_other_ref, w_s)
    hq = HALF_QUERY
    mine = w_s[pl.ds(pl.multiple_of(info[0] * hq, hq), hq), :]
    other = w_s[pl.ds(pl.multiple_of((1 - info[0]) * hq, hq), hq), :]
    rows_ref[...] = mine
    middle = (
        tokens_ref[...].astype(jnp.float32)
        + dot(mine_ref[...].astype(low_type).T, mine)
        + dot(came_ref[...].T, other)
    )
    middle_ref[...] = middle
    normed = (middle * norm_scale(middle) * gain_ref[...]).astype(low_type)
    cut = normed.shape[0] // 2
    for i in range(2):
        part = normed[i * cut : (i + 1) * cut]
        normed_refs[i][...] = part
        turned_refs[i][...] = part.T


def project_out(info, attended, came, weights, weights_other, tokens, gain, after):
    rows, width = tokens.shape
    hq = HALF_QUERY
    part = weights.shape[2]
    return pl.pallas_call(
        ignoring(out_kernel, 7, after),
        grid=(1,),
        in_specs=[
            SCALARS,
            pl.BlockSpec((hq, rows), lambda i: (0, 0)),
            pl.BlockSpec((hq, rows), lambda i: (0, 0)),
            pl.BlockSpec((2, width, part), lambda i: (1, 0, 0)),
            pl.BlockSpec((2, width, part), lambda i: (0, 0, 0)),
            pl.BlockSpec((rows, width), lambda i: (0, 0)),
            pl.BlockSpec((1, width), lambda i: (0, 0)),
        ]
        + [ANY] * len(after),
        out_specs=[
            pl.BlockSpec((rows, width), lambda i: (0, 0)),
            pl.BlockSpec((rows // 2, width), lambda i: (0, 0)),
            pl.BlockSpec((rows // 2, width), lambda i: (0, 0)),
            pl.BlockSpec((width, rows // 2), lambda i: (0, 0)),
            pl.BlockSpec((width, rows // 2), lambda i: (0, 0)),
            pl.BlockSpec((hq, width), lambda i: (0, 0)),
        ],
        out_shape=[
            shape((rows, width), jnp.float32), shape((rows // 2, width)), shape((rows // 2, width)),
            shape((width, rows // 2)), shape((width, rows // 2)), shape((hq, width)),
        ],
        scratch_shapes=[pltpu.VMEM((width, width), low_type)],
        compiler_params=params(),
        cost_estimate=cost(2 * rows * width * width, 16 << 20),
    )(info, attended, came, weights, weights_other, tokens, gain, *after)


def ffn_kernel(tuned, ways, info, *refs):
    xs, xts, cs, cts, w_ref, refs = refs[0:4], refs[4:8], refs[8:10], refs[10:12], refs[12], refs[13:]
    stacks = [()] * CHUNKS
    if tuned:
        stacks, refs = [refs[4 * j : 4 * j + 4] for j in range(CHUNKS)], refs[4 * CHUNKS :]
    totals, outs, scratch = refs[:4], list(refs[4:-17]), refs[-17:]
    (
        x_s, c_s, xt_s, ct_s, result_s, grad_s, result_low, grad_low, land_s, gate_s, up_s, down_s,
        hidden_s, dgate_s, dup_s, packed_s, sems,
    ) = scratch
    rows = cs[0].shape[0]
    size = FFN_ROWS
    block, part = gate_s.shape[1], packed_s.shape[3]
    width = gate_s.shape[0]
    lane, turned = block // BLOCKS, width // BLOCKS

    def begin(source, target, sem):
        copy = pltpu.make_async_copy(source, target, sem)
        copy.start()
        return copy

    def weights_in(j):
        target = land_s.at[j % 2]
        if tuned:
            return place_pieces(info, BLOCKS, w_ref.at[j], stacks[j], True, target, sems.at[j])
        return [begin(w_ref.at[j], target, sems.at[j, 0])]

    coming = weights_in(0)
    few = rows // 2
    there = [begin(ref, x_s.at[i * few : (i + 1) * few], sems.at[3, i]) for i, ref in enumerate(xs)]
    there += [begin(ref, c_s.at[i * rows : (i + 1) * rows], sems.at[3, 4 + i]) for i, ref in enumerate(cs)]
    across = [begin(ref, xt_s.at[:, i * few : (i + 1) * few], sems.at[3, 6 + i]) for i, ref in enumerate(xts)]
    across += [begin(ref, ct_s.at[:, i * rows : (i + 1) * rows], sems.at[3, 10 + i]) for i, ref in enumerate(cts)]
    going = [[] for _ in range(CHUNKS + 1)]
    for j in range(CHUNKS):
        for copy in coming:
            copy.wait()
        land = land_s.at[j % 2]
        gate_s[:, :part] = land[0]
        gate_s[:, part:] = land[1, :, : block - part]
        up_s[:, : 2 * part - block] = land[1, :, block - part :]
        up_s[:, 2 * part - block :] = land[2, :, : 2 * block - 2 * part]
        for q in range(BLOCKS):
            for z in range(BLOCKS):
                column = 2 * block + q * lane
                b, at = column // part, column % part
                down_s[q * turned : (q + 1) * turned, z * lane : (z + 1) * lane] = land[
                    b, z * turned : (z + 1) * turned, at : at + lane
                ]
        coming = weights_in(j + 1) if j + 1 < CHUNKS else []
        if j == 0:
            for copy in there:
                copy.wait()

        def forward(t, _, j=j):
            at = pl.ds(pl.multiple_of(t * size, size), size)
            x, c = x_s[at, :], c_s[at, :]
            gate = dot(x, gate_s[...])
            upward = dot(x, up_s[...])
            grad_hidden = dot(c, down_s[...])
            sigmoid = 1.0 / (1.0 + jnp.exp(-gate))
            silu = gate * sigmoid
            hidden = (silu * upward).astype(low_type)
            grad_gate = grad_hidden * upward * sigmoid * (1.0 + gate * (1.0 - sigmoid))
            grad_gate = grad_gate.astype(low_type)
            grad_up = (grad_hidden * silu).astype(low_type)
            hidden_s[at, :], dgate_s[at, :], dup_s[at, :] = hidden, grad_gate, grad_up
            result = dot(hidden, down_s[...], (1, 1))
            grad = dot(grad_gate, gate_s[...], (1, 1)) + dot(grad_up, up_s[...], (1, 1))
            if j > 0:
                result, grad = result + result_s[at, :], grad + grad_s[at, :]
            result_s[at, :], grad_s[at, :] = result, grad
            return 0

        lax.fori_loop(0, 2 * rows // size, forward, 0)
        if j == 0:
            for copy in across:
                copy.wait()
        if j == CHUNKS - 1:
            result_low[...] = result_s[rows:, :].astype(low_type)
            grad_low[...] = grad_s[rows:, :].astype(low_type)
            sources = (result_s.at[:rows], grad_s.at[:rows], result_low, grad_low)
            going[CHUNKS] = [begin(s, t, sems.at[3, 12 + i]) for i, (s, t) in enumerate(zip(sources, totals))]
        if j >= 2:
            for copy in going[j - 2]:
                copy.wait()
        packed = packed_s.at[j % 2]

        def backward(q, _, packed=packed):
            at = pl.ds(pl.multiple_of(q * turned, turned), turned)
            xt = xt_s[at, :]
            gate = dot(xt, dgate_s[...]).astype(low_type)
            up = dot(xt, dup_s[...]).astype(low_type)
            down = dot(ct_s[at, :], hidden_s[...]).astype(low_type)
            packed[0, at, :] = gate[:, :part]
            packed[1, at, : block - part] = gate[:, part:]
            packed[1, at, block - part :] = up[:, : 2 * part - block]
            packed[2, at, : 2 * block - 2 * part] = up[:, 2 * part - block :]
            column = 2 * block + q * lane
            b = lax.div(column, part)
            place = pl.ds(pl.multiple_of(lax.rem(column, part), lane), lane)
            for z in range(BLOCKS):
                packed[b, z * turned : (z + 1) * turned, place] = down[:, z * lane : (z + 1) * lane]
            return 0

        lax.fori_loop(0, BLOCKS, backward, 0)
        count = 4 if ways[j] == "xy" else 1
        going[j] = send_out(info, packed, outs[:count], ways[j], sems.at[4 + j])
        outs = outs[count:]
    for copy in going[CHUNKS - 2] + going[CHUNKS - 1] + going[CHUNKS]:
        copy.wait()


def feed_forward(info, xs, cs, xts, cts, weights, pieces, ways, tuned, after):
    rows, width = cs[0].shape
    part = weights.shape[2] // BLOCKS if tuned else weights.shape[3]
    block = BLOCKS * part // 3
    sent = [sent_shapes(width, part, way) for way in ways]
    given = sum((list(p) for p in pieces), [])
    totals = [shape((rows, width), jnp.float32)] * 2 + [shape((rows, width))] * 2

    def kernel(info, *refs):
        ffn_kernel(tuned, ways, info, *refs)

    whole = pltpu.VMEM((2 * rows, width), low_type)
    turned = pltpu.VMEM((width, 2 * rows), low_type)
    total = pltpu.VMEM((2 * rows, width), jnp.float32)
    low = pltpu.VMEM((rows, width), low_type)
    packed = pltpu.VMEM((2, BLOCKS, width, part), low_type)
    matrix = pltpu.VMEM((width, block), low_type)
    tokens = pltpu.VMEM((2 * rows, block), low_type)
    outs = pl.pallas_call(
        ignoring(kernel, 14 + len(given), after),
        in_specs=[SCALARS] + [ANY] * (13 + len(given) + len(after)),
        out_specs=[ANY] * (4 + sum(len(s) for s in sent)),
        out_shape=totals + sum(sent, []),
        scratch_shapes=[
            whole, whole, turned, turned, total, total, low, low, packed, matrix, matrix, matrix,
            tokens, tokens, tokens, packed, pltpu.SemaphoreType.DMA((4 + CHUNKS, 16)),
        ],
        compiler_params=params(),
        cost_estimate=cost(
            36 * rows * width * block * CHUNKS, 40 << 20, 2 * rows * block * CHUNKS
        ),
    )(info, *xs, *xts, *cs, *cts, weights, *given, *after)
    totals, outs = outs[:4], outs[4:]
    groups = []
    for shapes in sent:
        groups.append(outs[: len(shapes)])
        outs = outs[len(shapes) :]
    return totals, groups


def branch_kernel(g_ref, one_ref, two_ref, w_ref, attended_ref, grad_ref, delta_ref, rows_ref, other_s):
    rows = g_ref.shape[0]
    other_s[: rows // 2, :] = one_ref[...]
    other_s[rows // 2 :, :] = two_ref[...]
    g_other_ref = other_s
    delta_ref[...] = jnp.zeros(delta_ref.shape, jnp.float32)
    for i, ref in enumerate((g_ref, g_other_ref)):
        at = slice(i * rows, (i + 1) * rows)
        grad = dot(w_ref[...], ref[...], (1, 1)).astype(low_type)
        grad_ref[:, at] = grad
        product = grad.astype(jnp.float32) * attended_ref[:, at]
        for h in range(GROUP * GROUPS):
            delta_ref[h // GROUP, h % GROUP : h % GROUP + 1, at] = jnp.sum(
                product[h * HEAD_WIDTH : (h + 1) * HEAD_WIDTH], axis=0, keepdims=True
            )
    attended = attended_ref[...].astype(low_type)
    rows_ref[...] = (
        dot(attended[:, :rows], g_ref[...]) + dot(attended[:, rows:], g_other_ref[...])
    ).astype(low_type)


def branch(grad, grad_other, out_rows, attended, after):
    rows, width = grad.shape
    return pl.pallas_call(
        ignoring(branch_kernel, 5, after),
        in_specs=[pl.BlockSpec()] * 5 + [ANY] * len(after),
        out_specs=[pl.BlockSpec()] * 3,
        out_shape=[
            shape(attended.shape), shape((GROUPS, 8, 2 * rows), jnp.float32),
            shape((HALF_QUERY, width)),
        ],
        scratch_shapes=[pltpu.VMEM(grad.shape, low_type)],
        compiler_params=params(),
        cost_estimate=cost(8 * rows * width * HALF_QUERY, 12 << 20),
    )(grad, *grad_other, out_rows, attended, *after)


def attn_grad_kernel(
    info, dq_ref, dkv_ref, came_ref, cos_ref, sin_ref, normed_ref, mine_ref, other_ref, d_ref, *refs
):
    outs, packed_s, sems = refs[:-2], refs[-2], refs[-1]
    hq, hk = HALF_QUERY, HALF_KEY
    part = packed_s.shape[2]
    cosine, sine = cos_ref[...], -sin_ref[...]
    turn_heads(d_ref, dq_ref[...], cosine, sine, 0)
    whole = dkv_ref[...] + came_ref[...].astype(jnp.float32)
    turn_heads(d_ref, whole[0], cosine, sine, hq)
    d_ref[hq + hk :, :] = whole[1].astype(low_type)
    normed = normed_ref[...]
    packed_s[0] = dot(normed, d_ref[:part, :], (1, 1)).astype(low_type)
    packed_s[1] = dot(normed, d_ref[part : 2 * part, :], (1, 1)).astype(low_type)
    last = dot(normed, d_ref[2 * part :, :], (1, 1)).astype(low_type)
    mine, other = mine_ref[...], other_ref[...]
    low = info[0] == 0
    out = jnp.concatenate(
        [jnp.where(low, mine, other), jnp.where(low, other, mine)], axis=0
    )
    packed_s[2] = jnp.concatenate([last, out[:, : part - hk]], axis=1)
    packed_s[3] = out[:, part - hk :]
    for copy in send_out(info, packed_s, outs, "xy" if len(outs) > 1 else "whole", sems):
        copy.wait()


def attn_grads(info, grad_query, grad_kv, came, cosine, sine, normed, mine, other, after, tuned):
    width, both = normed.shape
    part = (2 * HALF_QUERY + 2 * HALF_KEY) // BLOCKS
    sent = sent_shapes(width, part, "xy" if tuned else "whole")
    return pl.pallas_call(
        ignoring(attn_grad_kernel, 9, after),
        in_specs=[SCALARS] + [pl.BlockSpec()] * 8 + [ANY] * len(after),
        out_specs=[pl.BlockSpec()] + [ANY] * len(sent),
        out_shape=[shape((HALF_QUERY + 2 * HALF_KEY, both))] + sent,
        scratch_shapes=[
            pltpu.VMEM((BLOCKS, width, part), low_type),
            pltpu.SemaphoreType.DMA((8,)),
        ],
        compiler_params=params(),
        cost_estimate=cost(2 * both * width * 960, 20 << 20),
    )(info, grad_query, grad_kv, came, cosine, sine, normed, mine, other, *after)


def normed_grad_kernel(d_ref, w_ref, mine_ref, *other_refs):
    rows = mine_ref.shape[0]
    hk, part = HALF_KEY, w_ref.shape[2]
    for i in range(2):
        d = d_ref[:, i * rows : (i + 1) * rows].T
        value = dot(d[:, :part], w_ref[0], (1, 1)) + dot(d[:, part : 2 * part], w_ref[1], (1, 1))
        value = value + dot(d[:, 2 * part :], w_ref[2][:, :hk], (1, 1))
        if i == 0:
            mine_ref[...] = value
        else:
            for j, ref in enumerate(other_refs):
                cut = ref.shape[0]
                ref[...] = value[j * cut : (j + 1) * cut].astype(low_type)


def normed_grad(d, weights, after):
    width = weights.shape[1]
    rows = d.shape[1] // 2
    return pl.pallas_call(
        ignoring(normed_grad_kernel, 2, after),
        in_specs=[pl.BlockSpec()] * 2 + [ANY] * len(after),
        out_specs=[pl.BlockSpec()] * 3,
        out_shape=[shape((rows, width), jnp.float32)] + [shape((rows // 2, width))] * 2,
        compiler_params=params(),
        cost_estimate=cost(4 * rows * width * 960, 9 << 20),
    )(d, weights, *after)


def halves(info, refs, chunk):
    mine, other = refs[:BLOCKS], refs[BLOCKS:]
    place = lax.rem(info[1], BLOCKS)

    def ordered(values):
        for bit in (1, 2):
            flip = lax.rem(lax.div(place, bit), 2) == 1
            values = [jnp.where(flip, values[b ^ bit], values[b]) for b in range(BLOCKS)]
        return jnp.concatenate(values, axis=1)

    mine = ordered([ref[chunk] for ref in mine])
    other = ordered([ref[chunk] for ref in other])
    low = info[0] == 0
    return jnp.where(low, mine, other), jnp.where(low, other, mine)


def unpack_attn_kernel(gains, info, *refs):
    refs, outs = refs[: 2 * BLOCKS], refs[2 * BLOCKS :]
    rows = outs[0].shape[0]
    both = [value[:rows].astype(jnp.float32) for value in halves(info, refs, 0)]
    start = 0
    for ref, size in zip(outs[:4], (HALF_QUERY, HALF_KEY, HALF_KEY, HALF_QUERY)):
        ref[...] = jnp.concatenate([v[:, start : start + size] for v in both], axis=1)
        start += size
    if gains:
        total = sum(ref[0, rows:, :].astype(jnp.float32) for ref in refs)
        outs[4][...] = total[:2, :rows]


def unpack_attn(info, mine, other, rows, after):
    gains = mine[0].shape[1] > rows
    outs = [shape((rows, 2 * n), jnp.float32) for n in (HALF_QUERY, HALF_KEY, HALF_KEY, HALF_QUERY)]
    if gains:
        outs.append(shape((2, rows), jnp.float32))

    def kernel(*refs):
        unpack_attn_kernel(gains, *refs)

    return pl.pallas_call(
        ignoring(kernel, 1 + 2 * BLOCKS, after),
        in_specs=[SCALARS] + [pl.BlockSpec()] * (2 * BLOCKS) + [ANY] * len(after),
        out_specs=[pl.BlockSpec()] * len(outs),
        out_shape=outs,
        compiler_params=params(),
        cost_estimate=cost(0, 6 << 20),
    )(info, *mine, *other, *after)


def unpack_ffn_kernel(all_ref, gate_ref, up_ref, down_ref):
    part = all_ref.shape[3]
    block = BLOCKS * part // 3
    lane = block // BLOCKS
    half = CHUNKS * lane
    for h in range(2):
        for c in range(CHUNKS):
            value = jnp.concatenate([all_ref[h * BLOCKS + b, c] for b in range(BLOCKS)], axis=1)
            value = value.astype(jnp.float32)
            for z in range(BLOCKS):
                at = z * 2 * half + h * half + c * lane
                gate_ref[:, at : at + lane] = value[:, z * lane : (z + 1) * lane]
                up_ref[:, at : at + lane] = value[:, block + z * lane : block + (z + 1) * lane]
            down = jnp.concatenate(
                [value[:, 2 * block + q * lane : 2 * block + (q + 1) * lane] for q in range(BLOCKS)],
                axis=0,
            )
            down_ref[h * half + c * lane : h * half + (c + 1) * lane, :] = down.T


def unpack_ffn(info, everyone):
    rows, part = everyone.shape[2:]
    lane = part // 3
    return pl.pallas_call(
        unpack_ffn_kernel,
        in_specs=[pl.BlockSpec()],
        out_specs=[pl.BlockSpec()] * 3,
        out_shape=[
            shape((rows, 2 * BLOCKS * CHUNKS * lane), jnp.float32),
            shape((rows, 2 * BLOCKS * CHUNKS * lane), jnp.float32),
            shape((2 * CHUNKS * lane, BLOCKS * rows), jnp.float32),
        ],
        compiler_params=params(),
        cost_estimate=cost(0, 16 << 20),
    )(everyone)


def shards(sizes, *arrays):
    (
        tokens, segments, cotangent, attn_gain, w_query, key_matrix, value_matrix, w_out, ffn_gain,
        w_gate, w_up, w_down,
    ) = arrays
    ny, nx, nz = sizes
    tuned = (ny, nx) == (2, 2)
    core, xi = lax.axis_index("core"), lax.axis_index("x")
    place = lax.axis_index("y") * nx + xi
    info = jnp.stack([core, place, lax.axis_index("z"), xi]).astype(jnp.int32)
    tokens, cotangent, ids = tokens[0], cotangent[0], segments[0]
    rows, width = tokens.shape
    own_rows = w_query.shape[0]

    gains = jnp.stack([attn_gain, ffn_gain])
    attn_own, *attn_piece = pack_attn(
        info, (w_query, key_matrix, value_matrix, w_out), gains, tuned
    )
    ids = behind(ids, (attn_own,))
    if tuned:
        past_ids = lax.ppermute(ids, "x", [(0, 1)])
        past_ids = jnp.where(xi == 1, past_ids, jnp.iinfo(jnp.int32).max)
        all_ids = jnp.concatenate([ids, past_ids])
    else:
        all_ids = lax.all_gather(ids, "x", axis=0, tiled=True)
    first = jnp.sum((all_ids[:, None] < ids[None, :]).astype(jnp.int32), axis=0)
    firsts = jnp.concatenate([first[None], swap_core(first[None])])
    token_place = xi * rows + jnp.arange(rows, dtype=jnp.int32)
    positions = (token_place[None] - firsts).reshape(-1)
    angles = inverse_freq()[:, None] * positions.astype(jnp.float32)[None, :]
    cosine, sine = jnp.cos(angles), jnp.sin(angles)
    size = rows // 2
    starts = firsts.reshape(2, rows // size, size)[:, :, 0] // size
    info = jnp.concatenate([info, starts.reshape(-1)])
    firsts = firsts[:, None, :]

    ffn_own, *ffn_piece = pack_ffn(info, w_gate, w_up, w_down, (cosine, sine, firsts), tuned)
    tokens_sent, cotangent_sent, _ = lax.optimization_barrier((tokens, cotangent, ffn_own))
    tokens_other, cotangent_other = swap_core(jnp.stack([tokens_sent, cotangent_sent]))
    cotangent_turned, cotangent_turned_other = cotangent_sent.T, cotangent_other.T
    if tuned:
        cut = own_rows // 2
        slots = travel_z(attn_piece[0], sizes)
        stack = jnp.stack([s[:own_rows] for s in slots])
        tables = (tokens_other, cotangent_turned, cotangent_turned_other)
        parts = [lax.all_gather(behind(piece, (stack,)), "z", axis=0) for piece in ffn_piece]
        ffn_stacks = list(pick(info, parts[:1], ((0, 0, 0, own_rows, 0),), own_rows, tables))
        ffn_stacks += pick(
            info,
            parts,
            ((0, 0, own_rows, own_rows + cut, 0), (0, 1, 0, cut, cut), (1, 1, cut, cut + own_rows, 0)),
            own_rows,
            (),
        )
        stacks = (
            stack,
            lax.ppermute(stack, "x", PAIR),
            lax.ppermute(stack, "y", PAIR),
            lax.ppermute(stack, ("y", "x"), [(i, 3 - i) for i in range(4)]),
        )
        weights, weights_tail = assemble(info, attn_own, stacks, nz, ffn_stacks[:1])
        ffn_weights = ffn_own
        gains = [gains.astype(low_type)] + [s[own_rows : own_rows + 2, :own_rows] for s in slots]
        gains = jnp.stack(gains[::-1] + gains[::-1])
        gains = lax.dynamic_slice_in_dim(gains, nz - 1 - lax.axis_index("z"), nz, 0)
        gains = gains.transpose(1, 0, 2).reshape(2, width)
    else:
        weights = gather_whole(attn_own)
        weights_tail = weights[BLOCKS // 2 :]
        ffn_pieces = [()] * CHUNKS
        before_attend = before_out = ()
        ffn_weights = jnp.stack([gather_whole(ffn_own[c]) for c in range(CHUNKS)])
        gains = lax.all_gather(gains.astype(low_type), "z", axis=1, tiled=True)
    gain_one, gain_two = gains[:1].astype(jnp.float32), gains[1:].astype(jnp.float32)

    cs = (cotangent, cotangent_other)
    cts = (cotangent_turned, cotangent_turned_other)

    normed, query, keyvalue = project(
        tokens, tokens_other, gain_one, weights, cosine, sine
    )
    weights_other = swap_core(weights_tail)
    if tuned:
        first_x, first_y = (lax.ppermute(ffn_stacks[0], axis, PAIR) for axis in ("x", "y"))
        far_first = lax.ppermute(first_x, "y", PAIR)
        past = lax.ppermute(behind(keyvalue, (first_x, first_y)), "x", [(0, 1)])[None]
        by_x = [first_x] + [lax.ppermute(s, "x", PAIR) for s in ffn_stacks[1:]]
        by_y = [first_y] + [lax.ppermute(s, "y", PAIR) for s in ffn_stacks[1:]]
        before_attend = (*ffn_stacks[1:], far_first)
        before_out = (*by_x[1:], *by_y[1:])
    else:
        past = lax.all_gather(keyvalue, "x", axis=0)
    attended, log_total = attend(info, query, keyvalue, past, firsts, size, before_attend)
    if tuned:
        far = [
            far_first,
            lax.ppermute(behind(by_x[1], (attended,)), "y", PAIR),
            lax.ppermute(behind(by_y[2], (attended,)), "x", PAIR),
        ]
        ffn_pieces = list(zip(ffn_stacks, by_x, by_y, far))
    came = swap_core(attended[:, rows:].astype(low_type))
    middle, *normed_parts, out_rows = project_out(
        info, attended, came, weights, weights_other, tokens, gain_two, before_out
    )

    normed_parts = [list(normed_parts[:2]), list(normed_parts[2:])]
    xs, xts = (parts + [swap_core(part) for part in parts] for parts in normed_parts)
    sent, first, send, second, reduced = ([None] * (CHUNKS + 1) for _ in range(5))
    ways = ["xy", "xy", "z"] if tuned else ["whole"] * CHUNKS
    (result, grad_normed_two, result_other, grad_other), sent[:3] = feed_forward(
        info, xs, cs, xts, cts, ffn_weights, ffn_pieces, ways, tuned, ()
    )
    if tuned:
        rows_two = lax.psum_scatter(sent[2][0], "z", scatter_dimension=0, tiled=True)[0]
    first[0] = scatter_first(sent[0])

    grad_normed_two = grad_normed_two + swap_core(grad_other).astype(jnp.float32)
    result = result + swap_core(result_other).astype(jnp.float32)
    scale_two = norm_scale(middle)
    grad_gain_two = jnp.sum(grad_normed_two * middle * scale_two, axis=0)
    grad_middle = cotangent.astype(jnp.float32) + norm_back(
        grad_normed_two * gain_two, middle, scale_two
    )
    grad_branch = grad_middle.astype(low_type)
    output = (middle + result).astype(low_type)

    grad_other = [swap_core(grad_branch[i * rows // 2 : (i + 1) * rows // 2]) for i in range(2)]
    grad_attended, delta, grad_rows = branch(
        grad_branch, grad_other, out_rows, attended, ()
    )
    hq = HALF_QUERY
    mine = lax.dynamic_slice_in_dim(grad_rows, core * hq, hq, 1)
    other = swap_core(lax.dynamic_slice_in_dim(grad_rows, (1 - core) * hq, hq, 1))
    send[0] = scatter_sums(sent[0], first[0], (grad_attended,))
    second[0] = scatter_second(send[0])
    first[1] = scatter_first([behind(value, send[0]) for value in sent[1]])
    grad_query, grad_kv, grad_past = attend_back(
        info, query, keyvalue, past, grad_attended, firsts, log_total, delta, size,
        send[0],
    )
    if tuned:
        pieces = merge(info, sent[0], first[0], lax.optimization_barrier((*second[0], grad_past))[:2], nz)
        first_pieces, first_z = pieces, send_z(pieces, sizes)
    else:
        reduced[0] = scatter_mine(info, sent[0], first[0], second[0], (grad_past,), sizes)
    if tuned:
        came = lax.ppermute(behind(grad_past[0], (first_pieces[0], *first[1], other)), "x", [(1, 0)])
    else:
        came = lax.psum_scatter(grad_past, "x", scatter_dimension=0, tiled=True)[0]
    send[1] = scatter_sums(sent[1], first[1], (grad_past,))
    second[1] = scatter_second(send[1])
    if tuned:
        rows_two, _ = lax.optimization_barrier((rows_two, came))
        reduced[2] = lax.psum_scatter(rows_two, ("y", "x"), scatter_dimension=0, tiled=True)[0]
    last = (came, rows_two) if tuned else (came,)
    reduced[1] = scatter_mine(info, sent[1], first[1], second[1], last, sizes)
    grad_projected, *attn_sent = attn_grads(
        info, grad_query, grad_kv, came, cosine, sine, normed, mine, other,
        (*first_z, reduced[1]) if tuned else (), tuned,
    )
    normed_mine, *normed_other = normed_grad(grad_projected, weights, ())
    normed_came = [swap_core(part) for part in normed_other]
    grad_normed = normed_mine + jnp.concatenate(normed_came).astype(jnp.float32)
    inputs = tokens.astype(jnp.float32)
    scale_one = norm_scale(inputs)
    grad_gain_one = jnp.sum(grad_normed * inputs * scale_one, axis=0)
    grad_inputs = (
        grad_middle + norm_back(grad_normed * gain_one, inputs, scale_one)
    ).astype(low_type)


    sent[3], first[3] = attn_sent, scatter_first(attn_sent)
    last = (normed_mine,)
    if tuned:
        first_z = lax.optimization_barrier((*first_z, normed_mine))[:-1]
        reduced[0] = sum_z(first_pieces[0], first_z)
    send[3] = scatter_sums(sent[3], first[3], (*normed_came, reduced[2]) if tuned else last)
    second[3] = scatter_second(send[3])
    if tuned:
        gain_grads = jnp.stack([grad_gain_one, grad_gain_two]).reshape(2, nz, own_rows)
        gain_grads = jnp.pad(
            gain_grads.transpose(1, 0, 2).astype(low_type),
            ((0, 0), (0, GAIN_ROWS - 2), (0, sent[3][0].shape[2] - own_rows)),
        )
        pieces = merge(info, sent[3], first[3], second[3], nz, (gain_grads,))
        came_z = send_z(pieces, sizes)
        reduced[3] = sum_z(pieces[0], came_z)
        last = send[3]
    else:
        reduced[2] = scatter_rows(scatter_mine(info, sent[2], (), (), last, sizes))
        reduced[3] = scatter_rows(scatter_mine(info, sent[3], (), (), last, sizes))
    ffn_total = [
        reduced[0] if tuned else scatter_rows(reduced[0]),
        scatter_rows(behind(reduced[1], (grad_projected,))),
        reduced[2],
    ]
    ffn_total = jnp.stack(lax.optimization_barrier((*ffn_total, *last))[:CHUNKS])
    grad_w_gate, grad_w_up, grad_w_down = unpack_ffn(info, *gather_all(ffn_total, sizes))
    attn_out = unpack_attn(info, *spread(reduced[3][None], sizes), own_rows, ())
    if tuned:
        attn_out, gain_grads = attn_out[:4], attn_out[4]
    else:
        gain_grads = lax.psum(jnp.stack([grad_gain_one, grad_gain_two]), ("y", "core", "x", "z"))
        gain_grads = lax.dynamic_slice_in_dim(gain_grads, lax.axis_index("z") * own_rows, own_rows, 1)
    return (
        output[None], grad_inputs[None], gain_grads[0], *attn_out, gain_grads[1], grad_w_gate,
        grad_w_up, grad_w_down,
    )


def solution(mesh):
    dp, ctx, fsdp = (mesh.shape[name] for name in ("dp", "ctx", "fsdp"))
    fine = Mesh(mesh.devices.reshape(dp // 2, 2, ctx, fsdp), ("y", "core", "x", "z"))
    sizes = (dp // 2, ctx, fsdp)
    wide = P(("y", "core", "z"), "x", None)
    matrix, vector = P("z", None), P("z")
    in_specs = (
        wide, P(("y", "core", "z"), "x"), wide, vector, matrix, matrix, matrix, matrix, vector,
        matrix, matrix, matrix,
    )
    out_specs = (
        wide, wide, vector, matrix, matrix, matrix, matrix, vector, matrix, matrix, matrix
    )

    def layer(*arrays):
        return shards(sizes, *arrays)

    return jax.shard_map(
        layer, mesh=fine, in_specs=in_specs, out_specs=out_specs, check_vma=False
    )
```

```python
import math

import jax
import jax.numpy as jnp
from jax import lax
from jax.experimental import pallas as pl
from jax.experimental.pallas import tpu as pltpu
from jax.sharding import Mesh
from jax.sharding import PartitionSpec as P

QUERY_HEADS = 18
KEY_VALUE_HEADS = 6
HEAD_WIDTH = 64
TURN = HEAD_WIDTH // 2
GROUP = QUERY_HEADS // KEY_VALUE_HEADS
GROUPS = KEY_VALUE_HEADS // 2
HALF_QUERY = QUERY_HEADS // 2 * HEAD_WIDTH
HALF_KEY = GROUPS * HEAD_WIDTH
CHUNKS = 3
BLOCKS = 4
GAIN_ROWS = 16
FFN_ROWS = 512
COST = 0.1

low_type = jnp.bfloat16
eps_norm = 1e-05
masked_score = -1e30
lowest_peak = -1e20
LOG2E = math.log2(math.e)
SCORE_SCALE = HEAD_WIDTH ** (-0.5)
VMEM_LIMIT = 58 * 1024 * 1024

PAIR = [(0, 1), (1, 0)]
ANY = pl.BlockSpec(memory_space=pl.ANY)
SCALARS = pl.BlockSpec(memory_space=pltpu.SMEM)


def inverse_freq():
    return 10000.0 ** (-(jnp.arange(TURN, dtype=jnp.float32) * 2.0) / HEAD_WIDTH)


def norm_scale(value):
    return lax.rsqrt(jnp.mean(value * value, axis=-1, keepdims=True) + eps_norm)


def norm_back(scaled, value, scale):
    return scale * scaled - value * scale**3 * jnp.mean(scaled * value, axis=-1, keepdims=True)


def dot(left, right, over=(1, 0)):
    return lax.dot_general(
        left, right, (((over[0],), (over[1],)), ((), ())), preferred_element_type=jnp.float32
    )


def swap_core(value):
    return lax.ppermute(value, "core", PAIR)


def behind(value, others):
    return lax.optimization_barrier((value, *others))[0]


def ignoring(kernel, given, after):
    def wrapped(*refs):
        kernel(*refs[:given], *refs[given + len(after) :])

    return wrapped


def params():
    return pltpu.CompilerParams(vmem_limit_bytes=VMEM_LIMIT)


def cost(flops, moved, special=0):
    return pl.CostEstimate(
        flops=int(flops * COST), bytes_accessed=int(moved * COST), transcendentals=int(special * COST)
    )


def shape(dims, kind=low_type):
    return jax.ShapeDtypeStruct(tuple(dims), kind)


def pack_attn_kernel(info, q_ref, k_ref, v_ref, o_ref, gain_ref, own_ref, *piece_ref):
    def half(ref):
        size = ref.shape[1] // 2
        value = ref[...].astype(low_type)
        return jnp.where(info[0] == 0, value[:, :size], value[:, size:])

    own_ref[...] = jnp.concatenate([half(r) for r in (q_ref, k_ref, v_ref, o_ref)], axis=1)
    rows = own_ref.shape[0]
    for ref in piece_ref:
        part = ref.shape[1]
        ref[:rows, :] = own_ref[:, pl.ds(pl.multiple_of(info[1] * part, part), part)]
        gains = jnp.concatenate([gain_ref[...], jnp.zeros((GAIN_ROWS - 2, rows), jnp.float32)], axis=0)
        gains = jnp.concatenate([gains, jnp.zeros((GAIN_ROWS, part - rows), jnp.float32)], axis=1)
        ref[rows:, :] = gains.astype(low_type)


def pack_attn(info, arrays, gains, tuned):
    rows = arrays[0].shape[0]
    width = sum(a.shape[1] for a in arrays) // 2
    outs = [shape((rows, width))] + [shape((rows + GAIN_ROWS, width // BLOCKS))] * tuned
    return pl.pallas_call(
        pack_attn_kernel,
        in_specs=[SCALARS] + [pl.BlockSpec()] * 5,
        out_specs=[pl.BlockSpec()] * len(outs),
        out_shape=outs,
        compiler_params=params(),
        cost_estimate=cost(0, rows * width * 10),
    )(info, *arrays, gains)


def pack_ffn_kernel(info, gate_ref, up_ref, down_ref, own_ref, *piece_ref):
    step, steps = pl.program_id(0), pl.num_programs(0)
    part = gate_ref.shape[1] // CHUNKS
    rows = gate_ref.shape[0]
    blocks = own_ref.shape[2] // part // 3
    for c in range(CHUNKS):
        at = slice(c * part, (c + 1) * part)
        here = pl.ds(pl.multiple_of(step * part, part), part)
        own_ref[c, :, here] = gate_ref[:, at].astype(low_type)
        there = pl.ds(pl.multiple_of((blocks + step) * part, part), part)
        own_ref[c, :, there] = up_ref[:, at].astype(low_type)

    @pl.when(step == 0)
    def _():
        turned = down_ref[...].astype(low_type).T
        for c in range(CHUNKS):
            for q in range(blocks):
                own_ref[c, :, (2 * blocks + q) * part : (2 * blocks + q + 1) * part] = turned[
                    q * rows : (q + 1) * rows, c * part : (c + 1) * part
                ]

    @pl.when(step == steps - 1)
    def _():
        if piece_ref:
            one, two = piece_ref
            size, cut = one.shape[1], rows // 2
            at = pl.ds(pl.multiple_of(info[1] * size, size), size)
            one[:rows, :] = own_ref[0, :, at]
            one[rows:, :] = own_ref[1, :cut, at]
            two[:cut, :] = own_ref[1, cut:, at]
            two[cut:, :] = own_ref[2, :, at]


def pack_ffn(info, gate, up, down, after, tuned):
    rows, hidden = gate.shape
    hidden_rows, width = down.shape
    steps = hidden // hidden_rows
    half = hidden_rows // 2
    packed = 3 * steps * (half // CHUNKS)
    part = packed // BLOCKS
    outs = [shape((CHUNKS, rows, packed))]
    if tuned:
        outs += [shape((rows + rows // 2, part))] * 2
    columns = pl.BlockSpec((rows, half), lambda z, info: (0, 2 * z + info[0]))
    return pl.pallas_call(
        ignoring(pack_ffn_kernel, 4, after),
        grid_spec=pltpu.PrefetchScalarGridSpec(
            num_scalar_prefetch=1,
            grid=(steps,),
            in_specs=[columns, columns, pl.BlockSpec((half, width), lambda z, info: (info[0], 0))]
            + [ANY] * len(after),
            out_specs=[
                pl.BlockSpec(o.shape, lambda z, info, n=len(o.shape): (0,) * n) for o in outs
            ],
        ),
        out_shape=outs,
        compiler_params=params(),
        cost_estimate=cost(0, rows * packed * CHUNKS * 6),
    )(info, gate, up, down, *after)


def ring(count, step):
    return [(i, (i + step) % count) for i in range(count)]


def place_pieces(info, count, own, stacks, forward, out_ref, sems):
    rows, part = own.shape[0], out_ref.shape[2]
    copies = []

    def begin(source, block, row):
        target = out_ref.at[block, pl.ds(pl.multiple_of(row * rows, rows), rows), :]
        copies.append(pltpu.make_async_copy(source, target, sems.at[len(copies)]))
        copies[-1].start()

    for b in range(BLOCKS):
        begin(own.at[:, b * part : (b + 1) * part], b, info[2])
    for flip, stack in enumerate(stacks):
        for k in range(1, count):
            row = lax.rem(info[2] + (k if forward else count - k), count)
            begin(stack.at[k - 1], jnp.bitwise_xor(info[1], flip), row)
    return copies


def assemble(info, own, stacks, count, after):
    rows, width = own.shape
    out = shape((BLOCKS, rows * count, width // BLOCKS))

    def kernel(info, own_ref, *refs):
        *stack_refs, out_ref, tail_ref, sems = refs
        for copy in place_pieces(info, count, own_ref, stack_refs, False, out_ref, sems):
            copy.wait()
        tail_ref[...] = out_ref[BLOCKS // 2 :]

    return pl.pallas_call(
        ignoring(kernel, 2 + len(stacks), after),
        in_specs=[SCALARS] + [ANY] * (1 + len(stacks) + len(after)),
        out_specs=[pl.BlockSpec()] * 2,
        out_shape=[out, shape((BLOCKS // 2, *out.shape[1:]))],
        scratch_shapes=[pltpu.SemaphoreType.DMA((BLOCKS * count,))],
        compiler_params=params(),
        cost_estimate=cost(0, rows * width * count * 4),
    )(info, own, *stacks, *after)


def pick_kernel(parts, info, *refs):
    ins = refs[: -1 - len({p[0] for p in parts})]
    outs, sems = refs[len(ins) : -1], refs[-1]
    copies = []
    for out, source, start, stop, at in parts:
        count = ins[source].shape[0]
        for k in range(1, count):
            rows = ins[source].at[lax.rem(info[2] + k, count), start:stop]
            target = outs[out].at[k - 1, at : at + stop - start]
            copies.append(pltpu.make_async_copy(rows, target, sems.at[len(copies)]))
            copies[-1].start()
    for copy in copies:
        copy.wait()


def pick(info, arrays, parts, rows, after):
    count, _, part = arrays[0].shape
    outs = [shape((count - 1, rows, part))] * len({p[0] for p in parts})

    def kernel(*refs):
        pick_kernel(parts, *refs)

    return pl.pallas_call(
        ignoring(kernel, 1 + len(arrays), after),
        in_specs=[SCALARS] + [ANY] * (len(arrays) + len(after)),
        out_specs=[pl.BlockSpec()] * len(outs),
        out_shape=outs,
        scratch_shapes=[pltpu.SemaphoreType.DMA((len(parts) * (count - 1),))],
        compiler_params=params(),
        cost_estimate=cost(0, len(outs) * count * rows * part * 4),
    )(info, *arrays, *after)


def travel_z(piece, sizes):
    return [lax.ppermute(piece, "z", ring(sizes[2], k)) for k in range(1, sizes[2])]


def gather_whole(own):
    full = lax.all_gather(own, "z", axis=0, tiled=True)
    return full.reshape(full.shape[0], BLOCKS, -1).transpose(1, 0, 2)


def send_out(info, packed, outs, way, sems):
    copies = []

    def begin(source, target):
        copies.append(pltpu.make_async_copy(source, target, sems.at[len(copies)]))
        copies[-1].start()

    if way == "whole":
        begin(packed, outs[0])
    elif way == "z":
        count, _, rows, _ = outs[0].shape
        for z in range(count):
            for b in range(BLOCKS):
                begin(packed.at[b, z * rows : (z + 1) * rows], outs[0].at[z, b])
    else:
        keep_one, send_one, keep_two, send_two = outs
        cut = packed.shape[1] // 2
        y, x = lax.div(info[1], 2), lax.rem(info[1], 2)
        for i in range(2):
            at_y, at_x = jnp.bitwise_xor(y, i), jnp.bitwise_xor(x, i)
            begin(packed.at[at_y * 2 + x, :cut], keep_one.at[i])
            begin(packed.at[at_y * 2 + 1 - x, :cut], send_one.at[i])
            begin(packed.at[y * 2 + at_x, cut:], keep_two.at[i])
            begin(packed.at[(1 - y) * 2 + at_x, cut:], send_two.at[i])
    return copies


def sent_shapes(rows, part, way):
    if way == "xy":
        return [shape((2, rows // 2, part))] * 4
    if way == "z":
        return [shape((BLOCKS, BLOCKS, rows // BLOCKS, part))]
    return [shape((BLOCKS, rows, part))]


def add_low(kept, came):
    return (kept.astype(jnp.float32) + came.astype(jnp.float32)).astype(low_type)


def scatter_first(outs):
    if len(outs) == 1:
        return ()
    return lax.ppermute(outs[1], "x", PAIR), lax.ppermute(outs[3], "y", PAIR)


def scatter_sums(outs, came, last):
    if len(outs) == 1:
        return ()
    came = lax.optimization_barrier((*came, *last))
    return add_low(outs[0][1], came[0][1]), add_low(outs[2][1], came[1][1])


def scatter_second(sums):
    if len(sums) == 0:
        return ()
    return lax.ppermute(sums[0], "y", PAIR), lax.ppermute(sums[1], "x", PAIR)


def merge_kernel(more, info, *refs):
    parts, outs, mine_s = refs[:6], refs[6 + more : -1], refs[-1]
    cut = mine_s.shape[0] // 2
    rows = mine_s.shape[0] // len(outs)
    for i in range(2):
        kept, came, second = (ref[...].astype(jnp.float32) for ref in parts[3 * i : 3 * i + 3])
        mine_s[i * cut : (i + 1) * cut, :] = (kept[0] + came[0] + second).astype(low_type)
    for k, out in enumerate(outs):
        z = lax.rem(info[2] + k, len(outs)) if len(outs) > 1 else 0
        out[:rows, :] = mine_s[pl.ds(z * rows, rows), :]
        if more:
            out[rows:, :] = refs[6][z]


def merge(info, outs, first, second, count, more=()):
    cut, part = second[0].shape
    half = pl.BlockSpec((1, cut, part), lambda i: (0, 0, 0))
    whole = pl.BlockSpec((cut, part), lambda i: (0, 0))
    rows = 2 * cut // count + sum(m.shape[1] for m in more)

    def kernel(*refs):
        merge_kernel(len(more), *refs)

    return pl.pallas_call(
        kernel,
        grid=(1,),
        in_specs=[SCALARS] + [half, half, whole] * 2
        + [pl.BlockSpec(m.shape, lambda i: (0, 0, 0)) for m in more],
        out_specs=[pl.BlockSpec((rows, part), lambda i: (0, 0))] * count,
        out_shape=[shape((rows, part))] * count,
        scratch_shapes=[pltpu.VMEM((2 * cut, part), low_type)],
        compiler_params=params(),
        cost_estimate=cost(0, 16 * cut * part),
    )(info, outs[0], first[0], second[0], outs[2], first[1], second[1], *more)


def scatter_mine(info, outs, first, second, last, sizes):
    ny, nx, nz = sizes
    if len(outs) == 1:
        packed = outs[0]
        total = packed.shape[1]
        split = packed.transpose(1, 0, 2).reshape(total, ny * nx, -1).transpose(1, 0, 2)
        return lax.psum_scatter(split, ("y", "x"), scatter_dimension=0, tiled=True)[0]
    return merge(info, outs, first, lax.optimization_barrier((*second, *last))[: len(second)], 1)[0]


def send_z(pieces, sizes):
    return [lax.ppermute(o, "z", ring(sizes[2], k + 1)) for k, o in enumerate(pieces[1:])]


def sum_z(mine, came):
    return sum((c.astype(jnp.float32) for c in came), mine.astype(jnp.float32)).astype(low_type)


def scatter_rows(mine):
    return lax.psum_scatter(mine, "z", scatter_dimension=0, tiled=True)


def spread(total, sizes, late):
    if sizes[0] * sizes[1] == BLOCKS:
        mine = [
            total,
            lax.ppermute(total, "x", PAIR),
            lax.ppermute(total, "y", PAIR),
            lax.ppermute(total, ("y", "x"), [(i, 3 - i) for i in range(4)]),
        ]
        return mine, [swap_core(behind(value, late)) for value in mine]
    everyone = jnp.moveaxis(lax.all_gather(total, ("y", "x"), axis=0), 0, -2)
    everyone = jnp.moveaxis(everyone.reshape(total.shape[:2] + (BLOCKS, -1)), -2, 0)
    place = lax.axis_index("y") * sizes[1] + lax.axis_index("x")
    mine = [
        lax.dynamic_index_in_dim(everyone, (place % BLOCKS) ^ i, 0, False) for i in range(BLOCKS)
    ]
    return mine, [swap_core(value) for value in mine]


def gather_all(total, sizes):
    everyone = lax.all_gather(total, ("core", "y", "x"), axis=0)
    count = sizes[0] * sizes[1]
    if count == BLOCKS:
        return (everyone,)
    both = jnp.moveaxis(everyone.reshape((2, count) + total.shape), 1, -2)
    both = jnp.moveaxis(both.reshape((2,) + total.shape[:2] + (BLOCKS, -1)), -2, 1)
    return (both.reshape((2 * BLOCKS,) + both.shape[2:]),)


def turn_heads(ref, value, cosine, sine, start):
    for h in range(value.shape[0] // HEAD_WIDTH):
        former = value[h * HEAD_WIDTH : h * HEAD_WIDTH + TURN]
        latter = value[h * HEAD_WIDTH + TURN : (h + 1) * HEAD_WIDTH]
        at = start + h * HEAD_WIDTH
        ref[at : at + TURN, :] = (former * cosine - latter * sine).astype(ref.dtype)
        ref[at + TURN : at + HEAD_WIDTH, :] = (latter * cosine + former * sine).astype(ref.dtype)


def project_kernel(mine_ref, other_ref, gain_ref, w_ref, cos_ref, sin_ref, normed_ref, q_ref, kv_ref):
    rows = mine_ref.shape[0]
    hk, part = HALF_KEY, w_ref.shape[2]
    for i, ref in enumerate((mine_ref, other_ref)):
        value = ref[...].astype(jnp.float32)
        normed = (value * norm_scale(value) * gain_ref[...]).astype(low_type)
        at = slice(i * rows, (i + 1) * rows)
        normed_ref[:, at] = normed.T
    weights = [w_ref[0].T, w_ref[1].T, w_ref[2].T[:hk]]
    for i in range(2):
        at = slice(i * rows, (i + 1) * rows)
        normed = normed_ref[:, at]
        cosine, sine = cos_ref[:, at], sin_ref[:, at]
        first = dot(weights[0], normed)
        turn_heads(q_ref.at[:, at], first, cosine, sine, 0)
        second = dot(weights[1], normed)
        turn_heads(q_ref.at[:, at], second[: part - hk], cosine, sine, part)
        turn_heads(kv_ref.at[0, :, at], second[part - hk :], cosine, sine, 0)
        kv_ref[1, :, at] = dot(weights[2], normed).astype(low_type)


def project(mine, other, gain, weights, cosine, sine):
    rows, width = mine.shape
    return pl.pallas_call(
        project_kernel,
        in_specs=[pl.BlockSpec()] * 6,
        out_specs=[pl.BlockSpec()] * 3,
        out_shape=[
            shape((width, 2 * rows)), shape((HALF_QUERY, 2 * rows)), shape((2, HALF_KEY, 2 * rows))
        ],
        compiler_params=params(),
        cost_estimate=cost(4 * rows * width * 960, 14 << 20),
    )(mine, other, gain, weights, cosine, sine)


def tile_mask(first, place0, key0, size, causal):
    key_place = key0 + lax.broadcasted_iota(jnp.int32, (size, size), 0)
    allowed = key_place >= first
    if causal:
        place = place0 + lax.broadcasted_iota(jnp.int32, (size, size), 1)
        allowed = allowed & (key_place <= place)
    return jnp.concatenate([allowed] * GROUP, axis=1)


def heads_of(ref):
    return jnp.concatenate(
        [ref[r * HEAD_WIDTH : (r + 1) * HEAD_WIDTH, :] for r in range(GROUP)], axis=1
    )


def over_tiles(info, size, rows, turn):
    per = rows // size
    half = pl.program_id(2)
    own = info[3] * per
    hi = own + half
    lo = info[4 + pl.program_id(0) * per + half]

    def columns(b):
        return pl.ds(pl.multiple_of(lax.rem(b, per) * size, size), size)

    def earlier(b, _):
        turn(hi, b, lax.div(b, per), columns(b))
        return 0

    def here(b, _):
        turn(hi, b, None, columns(b))
        return 0

    lax.fori_loop(lo, own, earlier, 0)
    lax.fori_loop(jnp.maximum(lo, own), hi + 1, here, 0)


def attend_kernel(info, q_ref, kv_ref, past_ref, first_ref, o_ref, total_ref, peak_s, sum_s, acc_s):
    size, rows = q_ref.shape[1], kv_ref.shape[2]
    q = heads_of(q_ref)
    peak_s[...] = jnp.full(peak_s.shape, lowest_peak, jnp.float32)
    sum_s[...] = jnp.zeros(sum_s.shape, jnp.float32)
    acc_s[...] = jnp.zeros(acc_s.shape, jnp.float32)

    def turn(hi, b, past, at):
        k = kv_ref[0, :, at] if past is None else past_ref[past, 0, :, at]
        v = kv_ref[1, :, at] if past is None else past_ref[past, 1, :, at]
        allowed = tile_mask(first_ref[0], hi * size, b * size, size, past is None)
        scores = dot(k, q, (0, 0)) * (SCORE_SCALE * LOG2E)
        scores = jnp.where(allowed, scores, masked_score)
        peak = peak_s[...]
        fresh = jnp.maximum(peak, jnp.max(scores, axis=0, keepdims=True))
        shrink = jnp.exp2(peak - fresh)
        terms = jnp.exp2(scores - fresh)
        peak_s[...] = fresh
        sum_s[...] = sum_s[...] * shrink + jnp.sum(terms, axis=0, keepdims=True)
        acc_s[...] = acc_s[...] * shrink + dot(v, terms.astype(low_type))

    over_tiles(info, size, rows, turn)
    total = sum_s[...]
    mixed = acc_s[...] / total
    log_total = peak_s[...] + jnp.log2(total)
    for r in range(GROUP):
        o_ref[r * HEAD_WIDTH : (r + 1) * HEAD_WIDTH, :] = mixed[:, r * size : (r + 1) * size]
        total_ref[0, r : r + 1, :] = log_total[:, r * size : (r + 1) * size]


def attend_back_kernel(
    info, q_ref, kv_ref, past_ref, g_ref, first_ref, total_ref, delta_ref, dq_ref, dkv_ref, dpast_ref,
    acc_s, past_s,
):
    size, rows = q_ref.shape[1], kv_ref.shape[2]
    q = heads_of(q_ref)
    g = heads_of(g_ref)
    total = jnp.concatenate([total_ref[0, r : r + 1, :] for r in range(GROUP)], axis=1)
    delta = jnp.concatenate([delta_ref[0, r : r + 1, :] for r in range(GROUP)], axis=1)
    acc_s[...] = jnp.zeros(acc_s.shape, jnp.float32)

    @pl.when(pl.program_id(2) == 0)
    def _():
        dkv_ref[...] = jnp.zeros(dkv_ref.shape, jnp.float32)
        past_s[...] = jnp.zeros(past_s.shape, jnp.float32)

    def turn(hi, b, past, at):
        k = kv_ref[0, :, at] if past is None else past_ref[past, 0, :, at]
        v = kv_ref[1, :, at] if past is None else past_ref[past, 1, :, at]
        allowed = tile_mask(first_ref[0], hi * size, b * size, size, past is None)
        scores = dot(k, q, (0, 0)) * (SCORE_SCALE * LOG2E)
        weights = jnp.exp2(jnp.where(allowed, scores - total, masked_score))
        grad_weights = dot(v, g, (0, 0))
        grad_scores = (weights * (grad_weights - delta) * SCORE_SCALE).astype(low_type)
        dk = dot(q, grad_scores, (1, 1))
        dv = dot(g, weights.astype(low_type), (1, 1))
        if past is None:
            dkv_ref[0, :, at] += dk
            dkv_ref[1, :, at] += dv
        else:
            past_s[past, 0, :, at] += dk
            past_s[past, 1, :, at] += dv
        acc_s[...] += dot(k, grad_scores)

    over_tiles(info, size, rows, turn)
    acc = acc_s[...]
    for r in range(GROUP):
        dq_ref[r * HEAD_WIDTH : (r + 1) * HEAD_WIDTH, :] = acc[:, r * size : (r + 1) * size]

    @pl.when(pl.program_id(2) == pl.num_programs(2) - 1)
    def _():
        dpast_ref[...] = past_s[...].astype(low_type)


def attention_specs(parts, rows, size):
    per = rows // size
    wide = pl.BlockSpec((GROUP * HEAD_WIDTH, size), lambda s, g, h: (g, s * per + h))
    own = pl.BlockSpec((2, HEAD_WIDTH, rows), lambda s, g, h: (0, g, s))
    past = pl.BlockSpec((parts, 2, HEAD_WIDTH, rows), lambda s, g, h: (0, 0, g, s))
    first = pl.BlockSpec((1, 1, size), lambda s, g, h: (s, 0, h))
    stat = pl.BlockSpec((1, 8, size), lambda s, g, h: (g, 0, s * per + h))
    return (2, GROUPS, per), wide, own, past, first, stat


def attend(info, query, keyvalue, past, first, size, after):
    both = keyvalue.shape[2]
    rows = both // 2
    grid, wide, own, past_spec, first_spec, stat = attention_specs(past.shape[0], rows, size)
    pairs = 2 * rows * rows * 3 // 2
    return pl.pallas_call(
        ignoring(attend_kernel, 5, after),
        grid=grid,
        in_specs=[SCALARS, wide, own, past_spec, first_spec] + [ANY] * len(after),
        out_specs=[wide, stat],
        out_shape=[shape(query.shape, jnp.float32), shape((GROUPS, 8, both), jnp.float32)],
        scratch_shapes=[
            pltpu.VMEM((1, GROUP * size), jnp.float32),
            pltpu.VMEM((1, GROUP * size), jnp.float32),
            pltpu.VMEM((HEAD_WIDTH, GROUP * size), jnp.float32),
        ],
        compiler_params=params(),
        cost_estimate=cost(pairs * 9 * 64 * 4 * 5, 8 << 20, pairs * 9),
    )(info, query, keyvalue, past, first, *after)


def attend_back(info, query, keyvalue, past, grad, first, log_total, delta, size, after):
    both = keyvalue.shape[2]
    rows = both // 2
    grid, wide, own, past_spec, first_spec, stat = attention_specs(past.shape[0], rows, size)
    pairs = 2 * rows * rows * 3 // 2
    return pl.pallas_call(
        ignoring(attend_back_kernel, 8, after),
        grid=grid,
        in_specs=[SCALARS, wide, own, past_spec, wide, first_spec, stat, stat] + [ANY] * len(after),
        out_specs=[wide, own, past_spec],
        out_shape=[
            shape(query.shape, jnp.float32), shape(keyvalue.shape, jnp.float32), shape(past.shape)
        ],
        scratch_shapes=[
            pltpu.VMEM((HEAD_WIDTH, GROUP * size), jnp.float32),
            pltpu.VMEM((past.shape[0], 2, HEAD_WIDTH, rows), jnp.float32),
        ],
        compiler_params=params(),
        cost_estimate=cost(pairs * 9 * 64 * 10 * 3, 12 << 20, pairs * 9),
    )(info, query, keyvalue, past, grad, first, log_total, delta, *after)


def place_out(core, mine_ref, other_ref, out_ref):
    cut, part = HALF_KEY, mine_ref.shape[2]
    mine = jnp.concatenate([mine_ref[0][:, cut:], mine_ref[1]], axis=1)
    other = jnp.concatenate([other_ref[0][:, cut:], other_ref[1]], axis=1)
    out_ref[...] = jnp.where(
        core == 0,
        jnp.concatenate([mine, other], axis=1),
        jnp.concatenate([other, mine], axis=1),
    )


def out_kernel(
    info, mine_ref, came_ref, w_ref, w_other_ref, tokens_ref, gain_ref, middle_ref, *refs
):
    normed_refs, turned_refs, (rows_ref, w_s) = refs[:2], refs[2:4], refs[4:]
    place_out(info[0], w_ref, w_other_ref, w_s)
    hq = HALF_QUERY
    mine = w_s[pl.ds(pl.multiple_of(info[0] * hq, hq), hq), :]
    other = w_s[pl.ds(pl.multiple_of((1 - info[0]) * hq, hq), hq), :]
    rows_ref[...] = mine
    middle = (
        tokens_ref[...].astype(jnp.float32)
        + dot(mine_ref[...].astype(low_type).T, mine)
        + dot(came_ref[...].T, other)
    )
    middle_ref[...] = middle
    normed = (middle * norm_scale(middle) * gain_ref[...]).astype(low_type)
    cut = normed.shape[0] // 2
    for i in range(2):
        part = normed[i * cut : (i + 1) * cut]
        normed_refs[i][...] = part
        turned_refs[i][...] = part.T


def project_out(info, attended, came, weights, weights_other, tokens, gain, after):
    rows, width = tokens.shape
    hq = HALF_QUERY
    part = weights.shape[2]
    return pl.pallas_call(
        ignoring(out_kernel, 7, after),
        grid=(1,),
        in_specs=[
            SCALARS,
            pl.BlockSpec((hq, rows), lambda i: (0, 0)),
            pl.BlockSpec((hq, rows), lambda i: (0, 0)),
            pl.BlockSpec((2, width, part), lambda i: (1, 0, 0)),
            pl.BlockSpec((2, width, part), lambda i: (0, 0, 0)),
            pl.BlockSpec((rows, width), lambda i: (0, 0)),
            pl.BlockSpec((1, width), lambda i: (0, 0)),
        ]
        + [ANY] * len(after),
        out_specs=[
            pl.BlockSpec((rows, width), lambda i: (0, 0)),
            pl.BlockSpec((rows // 2, width), lambda i: (0, 0)),
            pl.BlockSpec((rows // 2, width), lambda i: (0, 0)),
            pl.BlockSpec((width, rows // 2), lambda i: (0, 0)),
            pl.BlockSpec((width, rows // 2), lambda i: (0, 0)),
            pl.BlockSpec((hq, width), lambda i: (0, 0)),
        ],
        out_shape=[
            shape((rows, width), jnp.float32), shape((rows // 2, width)), shape((rows // 2, width)),
            shape((width, rows // 2)), shape((width, rows // 2)), shape((hq, width)),
        ],
        scratch_shapes=[pltpu.VMEM((width, width), low_type)],
        compiler_params=params(),
        cost_estimate=cost(2 * rows * width * width, 16 << 20),
    )(info, attended, came, weights, weights_other, tokens, gain, *after)


def ffn_kernel(tuned, ways, info, *refs):
    xs, xts, cs, cts, w_ref, refs = refs[0:4], refs[4:8], refs[8:10], refs[10:12], refs[12], refs[13:]
    stacks = [()] * CHUNKS
    if tuned:
        stacks, refs = [refs[4 * j : 4 * j + 4] for j in range(CHUNKS)], refs[4 * CHUNKS :]
    totals, outs, scratch = refs[:4], list(refs[4:-17]), refs[-17:]
    (
        x_s, c_s, xt_s, ct_s, result_s, grad_s, result_low, grad_low, land_s, gate_s, up_s, down_s,
        hidden_s, dgate_s, dup_s, packed_s, sems,
    ) = scratch
    rows = cs[0].shape[0]
    size = FFN_ROWS
    block, part = gate_s.shape[1], packed_s.shape[3]
    width = gate_s.shape[0]
    lane, turned = block // BLOCKS, width // BLOCKS

    def begin(source, target, sem):
        copy = pltpu.make_async_copy(source, target, sem)
        copy.start()
        return copy

    def weights_in(j):
        target = land_s.at[j % 2]
        if tuned:
            return place_pieces(info, BLOCKS, w_ref.at[j], stacks[j], True, target, sems.at[j])
        return [begin(w_ref.at[j], target, sems.at[j, 0])]

    coming = weights_in(0)
    few = rows // 2
    there = [begin(ref, x_s.at[i * few : (i + 1) * few], sems.at[3, i]) for i, ref in enumerate(xs)]
    there += [begin(ref, c_s.at[i * rows : (i + 1) * rows], sems.at[3, 4 + i]) for i, ref in enumerate(cs)]
    across = [begin(ref, xt_s.at[:, i * few : (i + 1) * few], sems.at[3, 6 + i]) for i, ref in enumerate(xts)]
    across += [begin(ref, ct_s.at[:, i * rows : (i + 1) * rows], sems.at[3, 10 + i]) for i, ref in enumerate(cts)]
    going = [[] for _ in range(CHUNKS + 1)]
    for j in range(CHUNKS):
        for copy in coming:
            copy.wait()
        land = land_s.at[j % 2]
        gate_s[:, :part] = land[0]
        gate_s[:, part:] = land[1, :, : block - part]
        up_s[:, : 2 * part - block] = land[1, :, block - part :]
        up_s[:, 2 * part - block :] = land[2, :, : 2 * block - 2 * part]
        for q in range(BLOCKS):
            for z in range(BLOCKS):
                column = 2 * block + q * lane
                b, at = column // part, column % part
                down_s[q * turned : (q + 1) * turned, z * lane : (z + 1) * lane] = land[
                    b, z * turned : (z + 1) * turned, at : at + lane
                ]
        coming = weights_in(j + 1) if j + 1 < CHUNKS else []
        if j == 0:
            for copy in there:
                copy.wait()

        def forward(t, _, j=j):
            at = pl.ds(pl.multiple_of(t * size, size), size)
            x, c = x_s[at, :], c_s[at, :]
            gate = dot(x, gate_s[...])
            upward = dot(x, up_s[...])
            grad_hidden = dot(c, down_s[...])
            sigmoid = 1.0 / (1.0 + jnp.exp(-gate))
            silu = gate * sigmoid
            hidden = (silu * upward).astype(low_type)
            grad_gate = grad_hidden * upward * sigmoid * (1.0 + gate * (1.0 - sigmoid))
            grad_gate = grad_gate.astype(low_type)
            grad_up = (grad_hidden * silu).astype(low_type)
            hidden_s[at, :], dgate_s[at, :], dup_s[at, :] = hidden, grad_gate, grad_up
            result = dot(hidden, down_s[...], (1, 1))
            grad = dot(grad_gate, gate_s[...], (1, 1)) + dot(grad_up, up_s[...], (1, 1))
            if j > 0:
                result, grad = result + result_s[at, :], grad + grad_s[at, :]
            result_s[at, :], grad_s[at, :] = result, grad
            return 0

        lax.fori_loop(0, 2 * rows // size, forward, 0)
        if j == 0:
            for copy in across:
                copy.wait()
        if j == CHUNKS - 1:
            result_low[...] = result_s[rows:, :].astype(low_type)
            grad_low[...] = grad_s[rows:, :].astype(low_type)
            sources = (result_s.at[:rows], grad_s.at[:rows], result_low, grad_low)
            going[CHUNKS] = [begin(s, t, sems.at[3, 12 + i]) for i, (s, t) in enumerate(zip(sources, totals))]
        if j >= 2:
            for copy in going[j - 2]:
                copy.wait()
        packed = packed_s.at[j % 2]

        def backward(q, _, packed=packed):
            at = pl.ds(pl.multiple_of(q * turned, turned), turned)
            xt = xt_s[at, :]
            gate = dot(xt, dgate_s[...]).astype(low_type)
            up = dot(xt, dup_s[...]).astype(low_type)
            down = dot(ct_s[at, :], hidden_s[...]).astype(low_type)
            packed[0, at, :] = gate[:, :part]
            packed[1, at, : block - part] = gate[:, part:]
            packed[1, at, block - part :] = up[:, : 2 * part - block]
            packed[2, at, : 2 * block - 2 * part] = up[:, 2 * part - block :]
            column = 2 * block + q * lane
            b = lax.div(column, part)
            place = pl.ds(pl.multiple_of(lax.rem(column, part), lane), lane)
            for z in range(BLOCKS):
                packed[b, z * turned : (z + 1) * turned, place] = down[:, z * lane : (z + 1) * lane]
            return 0

        lax.fori_loop(0, BLOCKS, backward, 0)
        count = 4 if ways[j] == "xy" else 1
        going[j] = send_out(info, packed, outs[:count], ways[j], sems.at[4 + j])
        outs = outs[count:]
    for copy in going[CHUNKS - 2] + going[CHUNKS - 1] + going[CHUNKS]:
        copy.wait()


def feed_forward(info, xs, cs, xts, cts, weights, pieces, ways, tuned, after):
    rows, width = cs[0].shape
    part = weights.shape[2] // BLOCKS if tuned else weights.shape[3]
    block = BLOCKS * part // 3
    sent = [sent_shapes(width, part, way) for way in ways]
    given = sum((list(p) for p in pieces), [])
    totals = [shape((rows, width), jnp.float32)] * 2 + [shape((rows, width))] * 2

    def kernel(info, *refs):
        ffn_kernel(tuned, ways, info, *refs)

    whole = pltpu.VMEM((2 * rows, width), low_type)
    turned = pltpu.VMEM((width, 2 * rows), low_type)
    total = pltpu.VMEM((2 * rows, width), jnp.float32)
    low = pltpu.VMEM((rows, width), low_type)
    packed = pltpu.VMEM((2, BLOCKS, width, part), low_type)
    matrix = pltpu.VMEM((width, block), low_type)
    tokens = pltpu.VMEM((2 * rows, block), low_type)
    outs = pl.pallas_call(
        ignoring(kernel, 14 + len(given), after),
        in_specs=[SCALARS] + [ANY] * (13 + len(given) + len(after)),
        out_specs=[ANY] * (4 + sum(len(s) for s in sent)),
        out_shape=totals + sum(sent, []),
        scratch_shapes=[
            whole, whole, turned, turned, total, total, low, low, packed, matrix, matrix, matrix,
            tokens, tokens, tokens, packed, pltpu.SemaphoreType.DMA((4 + CHUNKS, 16)),
        ],
        compiler_params=params(),
        cost_estimate=cost(
            36 * rows * width * block * CHUNKS, 40 << 20, 2 * rows * block * CHUNKS
        ),
    )(info, *xs, *xts, *cs, *cts, weights, *given, *after)
    totals, outs = outs[:4], outs[4:]
    groups = []
    for shapes in sent:
        groups.append(outs[: len(shapes)])
        outs = outs[len(shapes) :]
    return totals, groups


def branch_kernel(g_ref, one_ref, two_ref, w_ref, attended_ref, grad_ref, delta_ref, rows_ref, other_s):
    rows = g_ref.shape[0]
    other_s[: rows // 2, :] = one_ref[...]
    other_s[rows // 2 :, :] = two_ref[...]
    g_other_ref = other_s
    delta_ref[...] = jnp.zeros(delta_ref.shape, jnp.float32)
    for i, ref in enumerate((g_ref, g_other_ref)):
        at = slice(i * rows, (i + 1) * rows)
        grad = dot(w_ref[...], ref[...], (1, 1)).astype(low_type)
        grad_ref[:, at] = grad
        product = grad.astype(jnp.float32) * attended_ref[:, at]
        for h in range(GROUP * GROUPS):
            delta_ref[h // GROUP, h % GROUP : h % GROUP + 1, at] = jnp.sum(
                product[h * HEAD_WIDTH : (h + 1) * HEAD_WIDTH], axis=0, keepdims=True
            )
    attended = attended_ref[...].astype(low_type)
    rows_ref[...] = (
        dot(attended[:, :rows], g_ref[...]) + dot(attended[:, rows:], g_other_ref[...])
    ).astype(low_type)


def branch(grad, grad_other, out_rows, attended, after):
    rows, width = grad.shape
    return pl.pallas_call(
        ignoring(branch_kernel, 5, after),
        in_specs=[pl.BlockSpec()] * 5 + [ANY] * len(after),
        out_specs=[pl.BlockSpec()] * 3,
        out_shape=[
            shape(attended.shape), shape((GROUPS, 8, 2 * rows), jnp.float32),
            shape((HALF_QUERY, width)),
        ],
        scratch_shapes=[pltpu.VMEM(grad.shape, low_type)],
        compiler_params=params(),
        cost_estimate=cost(8 * rows * width * HALF_QUERY, 12 << 20),
    )(grad, *grad_other, out_rows, attended, *after)


def attn_grad_kernel(
    info, dq_ref, dkv_ref, came_ref, cos_ref, sin_ref, normed_ref, mine_ref, other_ref, d_ref, *refs
):
    outs, packed_s, sems = refs[:-2], refs[-2], refs[-1]
    hq, hk = HALF_QUERY, HALF_KEY
    part = packed_s.shape[2]
    cosine, sine = cos_ref[...], -sin_ref[...]
    turn_heads(d_ref, dq_ref[...], cosine, sine, 0)
    whole = dkv_ref[...] + came_ref[...].astype(jnp.float32)
    turn_heads(d_ref, whole[0], cosine, sine, hq)
    d_ref[hq + hk :, :] = whole[1].astype(low_type)
    normed = normed_ref[...]
    packed_s[0] = dot(normed, d_ref[:part, :], (1, 1)).astype(low_type)
    packed_s[1] = dot(normed, d_ref[part : 2 * part, :], (1, 1)).astype(low_type)
    last = dot(normed, d_ref[2 * part :, :], (1, 1)).astype(low_type)
    mine, other = mine_ref[...], other_ref[...]
    low = info[0] == 0
    out = jnp.concatenate(
        [jnp.where(low, mine, other), jnp.where(low, other, mine)], axis=0
    )
    packed_s[2] = jnp.concatenate([last, out[:, : part - hk]], axis=1)
    packed_s[3] = out[:, part - hk :]
    for copy in send_out(info, packed_s, outs, "xy" if len(outs) > 1 else "whole", sems):
        copy.wait()


def attn_grads(info, grad_query, grad_kv, came, cosine, sine, normed, mine, other, after, tuned):
    width, both = normed.shape
    part = (2 * HALF_QUERY + 2 * HALF_KEY) // BLOCKS
    sent = sent_shapes(width, part, "xy" if tuned else "whole")
    return pl.pallas_call(
        ignoring(attn_grad_kernel, 9, after),
        in_specs=[SCALARS] + [pl.BlockSpec()] * 8 + [ANY] * len(after),
        out_specs=[pl.BlockSpec()] + [ANY] * len(sent),
        out_shape=[shape((HALF_QUERY + 2 * HALF_KEY, both))] + sent,
        scratch_shapes=[
            pltpu.VMEM((BLOCKS, width, part), low_type),
            pltpu.SemaphoreType.DMA((8,)),
        ],
        compiler_params=params(),
        cost_estimate=cost(2 * both * width * 960, 20 << 20),
    )(info, grad_query, grad_kv, came, cosine, sine, normed, mine, other, *after)


def normed_grad_kernel(d_ref, w_ref, mine_ref, *other_refs):
    rows = mine_ref.shape[0]
    hk, part = HALF_KEY, w_ref.shape[2]
    for i in range(2):
        d = d_ref[:, i * rows : (i + 1) * rows].T
        value = dot(d[:, :part], w_ref[0], (1, 1)) + dot(d[:, part : 2 * part], w_ref[1], (1, 1))
        value = value + dot(d[:, 2 * part :], w_ref[2][:, :hk], (1, 1))
        if i == 0:
            mine_ref[...] = value
        else:
            for j, ref in enumerate(other_refs):
                cut = ref.shape[0]
                ref[...] = value[j * cut : (j + 1) * cut].astype(low_type)


def normed_grad(d, weights, after):
    width = weights.shape[1]
    rows = d.shape[1] // 2
    return pl.pallas_call(
        ignoring(normed_grad_kernel, 2, after),
        in_specs=[pl.BlockSpec()] * 2 + [ANY] * len(after),
        out_specs=[pl.BlockSpec()] * 3,
        out_shape=[shape((rows, width), jnp.float32)] + [shape((rows // 2, width))] * 2,
        compiler_params=params(),
        cost_estimate=cost(4 * rows * width * 960, 9 << 20),
    )(d, weights, *after)


def halves(info, refs, chunk):
    mine, other = refs[:BLOCKS], refs[BLOCKS:]
    place = lax.rem(info[1], BLOCKS)

    def ordered(values):
        for bit in (1, 2):
            flip = lax.rem(lax.div(place, bit), 2) == 1
            values = [jnp.where(flip, values[b ^ bit], values[b]) for b in range(BLOCKS)]
        return jnp.concatenate(values, axis=1)

    mine = ordered([ref[chunk] for ref in mine])
    other = ordered([ref[chunk] for ref in other])
    low = info[0] == 0
    return jnp.where(low, mine, other), jnp.where(low, other, mine)


def unpack_attn_kernel(gains, info, *refs):
    refs, outs = refs[: 2 * BLOCKS], refs[2 * BLOCKS :]
    rows = outs[0].shape[0]
    both = [value[:rows].astype(jnp.float32) for value in halves(info, refs, 0)]
    start = 0
    for ref, size in zip(outs[:4], (HALF_QUERY, HALF_KEY, HALF_KEY, HALF_QUERY)):
        ref[...] = jnp.concatenate([v[:, start : start + size] for v in both], axis=1)
        start += size
    if gains:
        total = sum(ref[0, rows:, :].astype(jnp.float32) for ref in refs)
        outs[4][...] = total[:2, :rows]


def unpack_attn(info, mine, other, rows, after):
    gains = mine[0].shape[1] > rows
    outs = [shape((rows, 2 * n), jnp.float32) for n in (HALF_QUERY, HALF_KEY, HALF_KEY, HALF_QUERY)]
    if gains:
        outs.append(shape((2, rows), jnp.float32))

    def kernel(*refs):
        unpack_attn_kernel(gains, *refs)

    return pl.pallas_call(
        ignoring(kernel, 1 + 2 * BLOCKS, after),
        in_specs=[SCALARS] + [pl.BlockSpec()] * (2 * BLOCKS) + [ANY] * len(after),
        out_specs=[pl.BlockSpec()] * len(outs),
        out_shape=outs,
        compiler_params=params(),
        cost_estimate=cost(0, 6 << 20),
    )(info, *mine, *other, *after)


def unpack_ffn_kernel(all_ref, gate_ref, up_ref, down_ref):
    part = all_ref.shape[3]
    block = BLOCKS * part // 3
    lane = block // BLOCKS
    half = CHUNKS * lane
    for h in range(2):
        for c in range(CHUNKS):
            value = jnp.concatenate([all_ref[h * BLOCKS + b, c] for b in range(BLOCKS)], axis=1)
            value = value.astype(jnp.float32)
            for z in range(BLOCKS):
                at = z * 2 * half + h * half + c * lane
                gate_ref[:, at : at + lane] = value[:, z * lane : (z + 1) * lane]
                up_ref[:, at : at + lane] = value[:, block + z * lane : block + (z + 1) * lane]
            down = jnp.concatenate(
                [value[:, 2 * block + q * lane : 2 * block + (q + 1) * lane] for q in range(BLOCKS)],
                axis=0,
            )
            down_ref[h * half + c * lane : h * half + (c + 1) * lane, :] = down.T


def unpack_ffn(info, everyone):
    rows, part = everyone.shape[2:]
    lane = part // 3
    return pl.pallas_call(
        unpack_ffn_kernel,
        in_specs=[pl.BlockSpec()],
        out_specs=[pl.BlockSpec()] * 3,
        out_shape=[
            shape((rows, 2 * BLOCKS * CHUNKS * lane), jnp.float32),
            shape((rows, 2 * BLOCKS * CHUNKS * lane), jnp.float32),
            shape((2 * CHUNKS * lane, BLOCKS * rows), jnp.float32),
        ],
        compiler_params=params(),
        cost_estimate=cost(0, 16 << 20),
    )(everyone)


def shards(sizes, *arrays):
    (
        tokens, segments, cotangent, attn_gain, w_query, key_matrix, value_matrix, w_out, ffn_gain,
        w_gate, w_up, w_down,
    ) = arrays
    ny, nx, nz = sizes
    tuned = (ny, nx) == (2, 2)
    core, xi = lax.axis_index("core"), lax.axis_index("x")
    place = lax.axis_index("y") * nx + xi
    info = jnp.stack([core, place, lax.axis_index("z"), xi]).astype(jnp.int32)
    tokens, cotangent, ids = tokens[0], cotangent[0], segments[0]
    rows, width = tokens.shape
    own_rows = w_query.shape[0]

    gains = jnp.stack([attn_gain, ffn_gain])
    attn_own, *attn_piece = pack_attn(
        info, (w_query, key_matrix, value_matrix, w_out), gains, tuned
    )
    ids = behind(ids, (attn_own,))
    if tuned:
        past_ids = lax.ppermute(ids, "x", [(0, 1)])
        past_ids = jnp.where(xi == 1, past_ids, jnp.iinfo(jnp.int32).max)
        all_ids = jnp.concatenate([ids, past_ids])
    else:
        all_ids = lax.all_gather(ids, "x", axis=0, tiled=True)
    first = jnp.sum((all_ids[:, None] < ids[None, :]).astype(jnp.int32), axis=0)
    firsts = jnp.concatenate([first[None], swap_core(first[None])])
    token_place = xi * rows + jnp.arange(rows, dtype=jnp.int32)
    positions = (token_place[None] - firsts).reshape(-1)
    angles = inverse_freq()[:, None] * positions.astype(jnp.float32)[None, :]
    cosine, sine = jnp.cos(angles), jnp.sin(angles)
    size = rows // 2
    starts = firsts.reshape(2, rows // size, size)[:, :, 0] // size
    info = jnp.concatenate([info, starts.reshape(-1)])
    firsts = firsts[:, None, :]

    ffn_own, *ffn_piece = pack_ffn(info, w_gate, w_up, w_down, (cosine, sine, firsts), tuned)
    tokens_sent, cotangent_sent, _ = lax.optimization_barrier((tokens, cotangent, ffn_own))
    tokens_other, cotangent_other = swap_core(jnp.stack([tokens_sent, cotangent_sent]))
    cotangent_turned, cotangent_turned_other = cotangent_sent.T, cotangent_other.T
    if tuned:
        cut = own_rows // 2
        slots = travel_z(attn_piece[0], sizes)
        stack = jnp.stack([s[:own_rows] for s in slots])
        tables = (tokens_other, cotangent_turned, cotangent_turned_other)
        parts = [lax.all_gather(behind(piece, (stack,)), "z", axis=0) for piece in ffn_piece]
        ffn_stacks = list(pick(info, parts[:1], ((0, 0, 0, own_rows, 0),), own_rows, tables))
        ffn_stacks += pick(
            info,
            parts,
            ((0, 0, own_rows, own_rows + cut, 0), (0, 1, 0, cut, cut), (1, 1, cut, cut + own_rows, 0)),
            own_rows,
            (),
        )
        stacks = (
            stack,
            lax.ppermute(stack, "x", PAIR),
            lax.ppermute(stack, "y", PAIR),
            lax.ppermute(stack, ("y", "x"), [(i, 3 - i) for i in range(4)]),
        )
        weights, weights_tail = assemble(info, attn_own, stacks, nz, ffn_stacks[:1])
        ffn_weights = ffn_own
        gains = [gains.astype(low_type)] + [s[own_rows : own_rows + 2, :own_rows] for s in slots]
        gains = jnp.stack(gains[::-1] + gains[::-1])
        gains = lax.dynamic_slice_in_dim(gains, nz - 1 - lax.axis_index("z"), nz, 0)
        gains = gains.transpose(1, 0, 2).reshape(2, width)
    else:
        weights = gather_whole(attn_own)
        weights_tail = weights[BLOCKS // 2 :]
        ffn_pieces = [()] * CHUNKS
        before_attend = before_out = ()
        ffn_weights = jnp.stack([gather_whole(ffn_own[c]) for c in range(CHUNKS)])
        gains = lax.all_gather(gains.astype(low_type), "z", axis=1, tiled=True)
    gain_one, gain_two = gains[:1].astype(jnp.float32), gains[1:].astype(jnp.float32)

    cs = (cotangent, cotangent_other)
    cts = (cotangent_turned, cotangent_turned_other)

    normed, query, keyvalue = project(
        tokens, tokens_other, gain_one, weights, cosine, sine
    )
    weights_other = swap_core(weights_tail)
    if tuned:
        first_x, first_y = (lax.ppermute(ffn_stacks[0], axis, PAIR) for axis in ("x", "y"))
        far_first = lax.ppermute(first_x, "y", PAIR)
        past = lax.ppermute(behind(keyvalue, (first_x, first_y)), "x", [(0, 1)])[None]
        by_x = [first_x] + [lax.ppermute(s, "x", PAIR) for s in ffn_stacks[1:]]
        by_y = [first_y] + [lax.ppermute(s, "y", PAIR) for s in ffn_stacks[1:]]
        before_attend = (*ffn_stacks[1:], far_first)
        before_out = (*by_x[1:], *by_y[1:])
    else:
        past = lax.all_gather(keyvalue, "x", axis=0)
    attended, log_total = attend(info, query, keyvalue, past, firsts, size, before_attend)
    if tuned:
        far = [
            far_first,
            lax.ppermute(behind(by_x[1], (attended,)), "y", PAIR),
            lax.ppermute(behind(by_y[2], (attended,)), "x", PAIR),
        ]
        ffn_pieces = list(zip(ffn_stacks, by_x, by_y, far))
    came = swap_core(attended[:, rows:].astype(low_type))
    middle, *normed_parts, out_rows = project_out(
        info, attended, came, weights, weights_other, tokens, gain_two, before_out
    )

    normed_parts = [list(normed_parts[:2]), list(normed_parts[2:])]
    xs, xts = (parts + [swap_core(part) for part in parts] for parts in normed_parts)
    sent, first, send, second, reduced = ([None] * (CHUNKS + 1) for _ in range(5))
    ways = ["xy", "xy", "z"] if tuned else ["whole"] * CHUNKS
    (result, grad_normed_two, result_other, grad_other), sent[:3] = feed_forward(
        info, xs, cs, xts, cts, ffn_weights, ffn_pieces, ways, tuned, ()
    )
    if tuned:
        rows_two = lax.psum_scatter(sent[2][0], "z", scatter_dimension=0, tiled=True)[0]
    first[0] = scatter_first(sent[0])

    grad_normed_two = grad_normed_two + swap_core(grad_other).astype(jnp.float32)
    result = result + swap_core(result_other).astype(jnp.float32)
    scale_two = norm_scale(middle)
    grad_gain_two = jnp.sum(grad_normed_two * middle * scale_two, axis=0)
    grad_middle = cotangent.astype(jnp.float32) + norm_back(
        grad_normed_two * gain_two, middle, scale_two
    )
    grad_branch = grad_middle.astype(low_type)
    output = (middle + result).astype(low_type)

    grad_other = [swap_core(grad_branch[i * rows // 2 : (i + 1) * rows // 2]) for i in range(2)]
    grad_attended, delta, grad_rows = branch(
        grad_branch, grad_other, out_rows, attended, ()
    )
    hq = HALF_QUERY
    mine = lax.dynamic_slice_in_dim(grad_rows, core * hq, hq, 1)
    other = swap_core(lax.dynamic_slice_in_dim(grad_rows, (1 - core) * hq, hq, 1))
    send[0] = scatter_sums(sent[0], first[0], (grad_attended,))
    second[0] = scatter_second(send[0])
    first[1] = scatter_first([behind(value, send[0]) for value in sent[1]])
    grad_query, grad_kv, grad_past = attend_back(
        info, query, keyvalue, past, grad_attended, firsts, log_total, delta, size,
        send[0],
    )
    if tuned:
        pieces = merge(info, sent[0], first[0], lax.optimization_barrier((*second[0], grad_past))[:2], nz)
        first_pieces, first_z = pieces, send_z(pieces, sizes)
    else:
        reduced[0] = scatter_mine(info, sent[0], first[0], second[0], (grad_past,), sizes)
    if tuned:
        came = lax.ppermute(behind(grad_past[0], (first_pieces[0], *first[1], other)), "x", [(1, 0)])
    else:
        came = lax.psum_scatter(grad_past, "x", scatter_dimension=0, tiled=True)[0]
    send[1] = scatter_sums(sent[1], first[1], (grad_past,))
    second[1] = scatter_second(send[1])
    if tuned:
        rows_two, _ = lax.optimization_barrier((rows_two, came))
        reduced[2] = lax.psum_scatter(rows_two, ("y", "x"), scatter_dimension=0, tiled=True)[0]
    last = (came, rows_two) if tuned else (came,)
    reduced[1] = scatter_mine(info, sent[1], first[1], second[1], last, sizes)
    grad_projected, *attn_sent = attn_grads(
        info, grad_query, grad_kv, came, cosine, sine, normed, mine, other,
        (*first_z, reduced[1]) if tuned else (), tuned,
    )
    normed_mine, *normed_other = normed_grad(grad_projected, weights, ())
    normed_came = [swap_core(part) for part in normed_other]
    grad_normed = normed_mine + jnp.concatenate(normed_came).astype(jnp.float32)
    inputs = tokens.astype(jnp.float32)
    scale_one = norm_scale(inputs)
    grad_gain_one = jnp.sum(grad_normed * inputs * scale_one, axis=0)
    grad_inputs = (
        grad_middle + norm_back(grad_normed * gain_one, inputs, scale_one)
    ).astype(low_type)


    sent[3], first[3] = attn_sent, scatter_first(attn_sent)
    last = (normed_mine,)
    if tuned:
        first_z = lax.optimization_barrier((*first_z, normed_mine))[:-1]
        reduced[0] = sum_z(first_pieces[0], first_z)
    send[3] = scatter_sums(sent[3], first[3], (*normed_came, reduced[2]) if tuned else last)
    second[3] = scatter_second(send[3])
    if tuned:
        gain_grads = jnp.stack([grad_gain_one, grad_gain_two]).reshape(2, nz, own_rows)
        gain_grads = jnp.pad(
            gain_grads.transpose(1, 0, 2).astype(low_type),
            ((0, 0), (0, GAIN_ROWS - 2), (0, sent[3][0].shape[2] - own_rows)),
        )
        pieces = merge(info, sent[3], first[3], second[3], nz, (gain_grads,))
        came_z = send_z(pieces, sizes)
        reduced[3] = sum_z(pieces[0], came_z)
        last = send[3]
    else:
        reduced[2] = scatter_rows(scatter_mine(info, sent[2], (), (), last, sizes))
        reduced[3] = scatter_rows(scatter_mine(info, sent[3], (), (), last, sizes))
    ffn_total = [
        reduced[0] if tuned else scatter_rows(reduced[0]),
        scatter_rows(behind(reduced[1], (grad_projected,))),
        reduced[2],
    ]
    ffn_total = jnp.stack(lax.optimization_barrier((*ffn_total, *last))[:CHUNKS])
    grad_w_gate, grad_w_up, grad_w_down = unpack_ffn(info, *gather_all(ffn_total, sizes))
    attn_out = unpack_attn(info, *spread(reduced[3][None], sizes, (grad_w_gate,)), own_rows, ())
    if tuned:
        attn_out, gain_grads = attn_out[:4], attn_out[4]
    else:
        gain_grads = lax.psum(jnp.stack([grad_gain_one, grad_gain_two]), ("y", "core", "x", "z"))
        gain_grads = lax.dynamic_slice_in_dim(gain_grads, lax.axis_index("z") * own_rows, own_rows, 1)
    return (
        output[None], grad_inputs[None], gain_grads[0], *attn_out, gain_grads[1], grad_w_gate,
        grad_w_up, grad_w_down,
    )


def solution(mesh):
    dp, ctx, fsdp = (mesh.shape[name] for name in ("dp", "ctx", "fsdp"))
    fine = Mesh(mesh.devices.reshape(dp // 2, 2, ctx, fsdp), ("y", "core", "x", "z"))
    sizes = (dp // 2, ctx, fsdp)
    wide = P(("y", "core", "z"), "x", None)
    matrix, vector = P("z", None), P("z")
    in_specs = (
        wide, P(("y", "core", "z"), "x"), wide, vector, matrix, matrix, matrix, matrix, vector,
        matrix, matrix, matrix,
    )
    out_specs = (
        wide, wide, vector, matrix, matrix, matrix, matrix, vector, matrix, matrix, matrix
    )

    def layer(*arrays):
        return shards(sizes, *arrays)

    return jax.shard_map(
        layer, mesh=fine, in_specs=in_specs, out_specs=out_specs, check_vma=False
    )
```
